32 devices in a mesh: dp: 8 (over z, core), tensor: 4 (over y, x).
Axes of the slice: x: 2, y: 2, z: 4, core: 2. Of those that a mesh axis runs over, the one named last changes fastest.
Arguments:
- tokens: bfloat16 [16384, 1024], P(('dp', 'tensor')), may hold values from -6 to 6
- cotangent: bfloat16 [16384, 1024], P(('dp', 'tensor')), may hold values from -6 to 6
- routes: int32 [1, 16384, 8], P(None, 'dp'), may hold values from 0 to 31, all different within a row; in each aligned block of 2048 rows (0 to 2047, 2048 to 4095, ..., all dimensions but the last counted through in order) at most 1024 rows name the same one
- gate_weights: float32 [1, 16384, 8], P(None, 'dp'), may hold values from 0.05 to 0.25
- norm_gains: float32 [1, 2, 1024], P(None, None, ('dp', 'tensor')), may hold values from 0.5 to 1.5
- norm_gains_first: float32 [1, 2, 1024], P(None, None, ('dp', 'tensor')), may hold values from -128 to 128
- norm_gains_second: float32 [1, 2, 1024], P(None, None, ('dp', 'tensor')), may hold values from 1619.0862 to 6476.3447
- query_weight: float32 [1, 1024, 1024], P(None, 'dp', 'tensor'), may hold values from -0.1875 to 0.1875
- query_first: float32 [1, 1024, 1024], P(None, 'dp', 'tensor'), may hold values from -96 to 96
- query_second: float32 [1, 1024, 1024], P(None, 'dp', 'tensor'), may hold values from 1152 to 4608
- keyval_weight: float32 [1, 1024, 1024], P(None, 'dp', 'tensor'), may hold values from -0.1875 to 0.1875
- keyval_first: float32 [1, 1024, 1024], P(None, 'dp', 'tensor'), may hold values from -96 to 96
- keyval_second: float32 [1, 1024, 1024], P(None, 'dp', 'tensor'), may hold values from 1152 to 4608
- output_weight: float32 [1, 1024, 1024], P(None, 'tensor', 'dp'), may hold values from -1.5 to 1.5
- output_first: float32 [1, 1024, 1024], P(None, 'tensor', 'dp'), may hold values from -12 to 12
- output_second: float32 [1, 1024, 1024], P(None, 'tensor', 'dp'), may hold values from 17.92 to 72
- expert_in: float32 [1, 32, 1024, 1024], P(None, 'tensor', 'dp'), may hold values from -0.1875 to 0.1875
- expert_in_first: float32 [1, 32, 1024, 1024], P(None, 'tensor', 'dp'), may hold values from -20 to 20
- expert_in_second: float32 [1, 32, 1024, 1024], P(None, 'tensor', 'dp'), may hold values from 49.152 to 204.8
- expert_down: float32 [1, 32, 512, 1024], P(None, 'tensor', 'dp'), may hold values from -1 to 1
- expert_down_first: float32 [1, 32, 512, 1024], P(None, 'tensor', 'dp'), may hold values from -4 to 4
- expert_down_second: float32 [1, 32, 512, 1024], P(None, 'tensor', 'dp'), may hold values from 1.6384 to 6.5536
Outputs:
- block_out: float32 [16384, 1024], P(('dp', 'tensor'))
- input_grad: float32 [16384, 1024], P(('dp', 'tensor'))
- gains_step: float32 [1, 2, 1024], P(None, None, ('dp', 'tensor'))
- new_gains_first: float32 [1, 2, 1024], P(None, None, ('dp', 'tensor'))
- new_gains_second: float32 [1, 2, 1024], P(None, None, ('dp', 'tensor'))
- new_query: float32 [1, 1024, 1024], P(None, 'dp', 'tensor')
- new_query_first: float32 [1, 1024, 1024], P(None, 'dp', 'tensor')
- new_query_second: float32 [1, 1024, 1024], P(None, 'dp', 'tensor')
- new_keyval: float32 [1, 1024, 1024], P(None, 'dp', 'tensor')
- new_keyval_first: float32 [1, 1024, 1024], P(None, 'dp', 'tensor')
- new_keyval_second: float32 [1, 1024, 1024], P(None, 'dp', 'tensor')
- new_output: float32 [1, 1024, 1024], P(None, 'tensor', 'dp')
- new_output_first: float32 [1, 1024, 1024], P(None, 'tensor', 'dp')
- new_output_second: float32 [1, 1024, 1024], P(None, 'tensor', 'dp')
- new_expert_in: float32 [1, 32, 1024, 1024], P(None, 'tensor', 'dp')
- new_expert_in_first: float32 [1, 32, 1024, 1024], P(None, 'tensor', 'dp')
- new_expert_in_second: float32 [1, 32, 1024, 1024], P(None, 'tensor', 'dp')
- new_expert_down: float32 [1, 32, 512, 1024], P(None, 'tensor', 'dp')
- new_expert_down_first: float32 [1, 32, 512, 1024], P(None, 'tensor', 'dp')
- new_expert_down_second: float32 [1, 32, 512, 1024], P(None, 'tensor', 'dp')
The draws below stay inside these ranges and needn't reach their ends.
Inputs may be any that keep to these rules, and one draw needn't show every extreme that they name: `routes`: in every block of 2048 consecutive tokens of a layer, each row names 8 different experts and no expert is named by more than 1024 rows; some expert is named by exactly 1024 rows.
All inputs are finite; a program needn't handle non-finite values.
Results may differ from the reference program's by a relative error of at most 0.012.
Values may be sent and summed in bfloat16 or wider, within the bound.
No kernel may reach another device: no remote copies, remote signals or barrier semaphores. Data moves between devices by JAX's collectives and lax.ppermute only.
A program may use at most 320 MiB of HBM per device.

```python
import math
import jax
import jax.numpy as jnp
import numpy as np
from jax import lax

D = 1024
HEADS = 16
KV = 8
HD = 64
EXPERTS = 32
FFE = 512
TOPK = 8
SEQ_LEN = 512
LAYERS = 1
STEP = 10
GROUP_TOK = 2048
CAP = 1024
TOKENS = 16384


def steps_of(rng, extent, split, least, largest):
    def one(axis_at, blocks):
        steps = jax.random.uniform(jax.random.fold_in(jax.random.fold_in(rng, 6), axis_at), (blocks,), jnp.float32, least / len(split), largest / len(split))
        return jnp.repeat(jnp.exp(steps), extent[axis_at] // blocks).reshape((-1,) + (1,) * (len(extent) - axis_at - 1))

    level = one(*split[0])
    for cut in split[1:]:
        level = level * one(*cut)
    return level


def shared_out(rng, own, number, rows, number_of, top, most, skew):
    ranking = jax.random.permutation(rng, number_of)
    heavy_load, usual = shares(number_of, rows * top, most, skew, True), shares(number_of, rows * top, most, skew, False)
    places = jnp.arange(number_of)

    def named(lengths, turn):
        used = int((lengths > 0).sum())
        fixed = max(1, used // 4)
        shifted = fixed + (places - fixed + turn * (used - fixed)) % max(1, number_of - fixed)
        return jnp.zeros((number_of,), jnp.int32).at[ranking[jnp.where(places < fixed, places, shifted)]].set(jnp.asarray(lengths, jnp.int32))

    lengths = jnp.where(number % 4 == 0, named(heavy_load, number // 4), named(usual, number - number // 4 - 1))
    mixed = jax.random.permutation(jax.random.fold_in(own, 3), number_of)
    source_of, receiver = mixed[0:number_of // 2 * 2:2], mixed[1:number_of // 2 * 2:2]
    slack = jnp.minimum(lengths[source_of] - 1, most - lengths[receiver]) // 2
    slack = jnp.where((source_of == ranking[0]) | (receiver == ranking[0]) | (lengths[receiver] == 0), 0, jnp.maximum(slack, 0))
    shifted = jax.random.randint(jax.random.fold_in(own, 4), (number_of // 2,), 0, 1 << 20) % (slack + 1)
    lengths = lengths.at[source_of].add(-shifted).at[receiver].add(shifted)
    members = jnp.searchsorted(jnp.cumsum(lengths), jnp.arange(rows * top), side="right").astype(jnp.int32)
    listing = members.reshape(top, rows).T
    listing = listing[jax.random.permutation(jax.random.fold_in(own, 1), rows)]
    turn = jax.random.randint(jax.random.fold_in(own, 2), (rows, 1), 0, top)
    return jnp.take_along_axis(listing, (jnp.arange(top)[None, :] + turn) % top, axis=1)


def shares(amount, total, most, lean, full):
    portions = [(1 << 20) // math.isqrt(standing ** lean) + 1 for standing in range(1, amount + 1)]
    largest = most if full else min(most, max(-(-total // amount), total * portions[0] // sum(portions)))
    least = 1 if total - largest >= amount - 1 else 0
    given, rest = [largest] + [least] * (amount - 1), total - largest - least * (amount - 1)
    while rest > 0:
        free = [i for i in range(1, amount) if given[i] < largest] or [i for i in range(1, amount) if given[i] < most]
        pool, budget = sum([portions[i] for i in free]), rest
        for i in free:
            more = min(most - given[i], max(1, budget * portions[i] // pool), rest)
            given[i] = given[i] + more
            rest = rest - more
    return np.array(given)


def bell_draw(own_key, shape, scale, limit, shards=(), kind=jnp.bfloat16):
    drawn = scale * jax.random.normal(own_key, shape, jnp.float32)
    if shards:
        drawn = drawn * steps_of(own_key, shape, shards, -0.22, 0.18)
    return jnp.clip(drawn, -limit, limit).astype(kind)


def setup_inputs(seed: int = 0) -> dict:
    streams_of = jax.random.split(jax.random.key(seed), 23)
    tokens = bell_draw(streams_of[0], (TOKENS, D), 1.0, 6.0, ((0, 32),))
    cotangent = bell_draw(streams_of[1], (TOKENS, D), 1.0, 6.0, ((0, 32),))
    routes_keys = jax.random.split(jax.random.fold_in(streams_of[2], 1), LAYERS * TOKENS // GROUP_TOK)
    routes_turns = jax.random.permutation(jax.random.fold_in(streams_of[2], 3), LAYERS * TOKENS // GROUP_TOK)
    routes = jax.vmap(lambda own, number: shared_out(jax.random.fold_in(streams_of[2], 2), own, number, GROUP_TOK, EXPERTS, TOPK, CAP, 1))(routes_keys, routes_turns).reshape((LAYERS, TOKENS, TOPK))
    gate_weights = jnp.clip(0.05 + 0.2 * jax.random.uniform(streams_of[3], (LAYERS, TOKENS, TOPK), jnp.float32) ** steps_of(streams_of[3], (LAYERS, TOKENS, TOPK), ((1, 8),), -0.2, 0.2), 0.05, 0.25)
    norm_gains = jnp.clip(1.0 + 0.1 * jax.random.normal(streams_of[4], (LAYERS, 2, D), jnp.float32), 0.5, 1.5)
    norm_gains_first = bell_draw(streams_of[5], (LAYERS, 2, D), (0.5 * TOKENS ** 0.5 * (5.0 / SEQ_LEN) ** 0.25), 128.0, ((2, 32),), jnp.float32)
    norm_gains_second = jnp.clip(jnp.exp(math.log(6476.3447) - 1.3862944 * jax.random.uniform(streams_of[6], (LAYERS, 2, D), jnp.float32) ** steps_of(streams_of[6], (LAYERS, 2, D), ((2, 32),), -0.2, 0.2)), 1619.0862, 6476.3447)
    query_weight = bell_draw(streams_of[7], (LAYERS, D, HEADS * HD), D ** -0.5, 0.1875, ((1, 8), (2, 4)), jnp.float32)
    query_first = bell_draw(streams_of[8], (LAYERS, D, HEADS * HD), (1.3 * (5.0 * TOKENS / SEQ_LEN) ** 0.5), 96.0, ((1, 8), (2, 4)), jnp.float32)
    query_second = jnp.clip(jnp.exp(math.log(4608.0) - 1.3862944 * jax.random.uniform(streams_of[9], (LAYERS, D, HEADS * HD), jnp.float32) ** steps_of(streams_of[9], (LAYERS, D, HEADS * HD), ((1, 8), (2, 4)), -0.2, 0.2)), 1152.0, 4608.0)
    keyval_weight = bell_draw(streams_of[10], (LAYERS, D, 2 * KV * HD), D ** -0.5, 0.1875, ((1, 8), (2, 4)), jnp.float32)
    keyval_first = bell_draw(streams_of[11], (LAYERS, D, 2 * KV * HD), (1.3 * (5.0 * TOKENS / SEQ_LEN) ** 0.5), 96.0, ((1, 8), (2, 4)), jnp.float32)
    keyval_second = jnp.clip(jnp.exp(math.log(4608.0) - 1.3862944 * jax.random.uniform(streams_of[12], (LAYERS, D, 2 * KV * HD), jnp.float32) ** steps_of(streams_of[12], (LAYERS, D, 2 * KV * HD), ((1, 8), (2, 4)), -0.2, 0.2)), 1152.0, 4608.0)
    output_weight = bell_draw(streams_of[13], (LAYERS, HEADS * HD, D), (HEADS * HD // 64) ** -0.5, 1.5, ((1, 4), (2, 8)), jnp.float32)
    output_first = bell_draw(streams_of[14], (LAYERS, HEADS * HD, D), (0.165 * (5.0 * TOKENS / SEQ_LEN) ** 0.5), 12.0, ((1, 4), (2, 8)), jnp.float32)
    output_second = jnp.clip(jnp.exp(math.log(72.0) - 1.3907487 * jax.random.uniform(streams_of[15], (LAYERS, HEADS * HD, D), jnp.float32) ** steps_of(streams_of[15], (LAYERS, HEADS * HD, D), ((1, 4), (2, 8)), -0.2, 0.2)), 17.92, 72.0)
    expert_in = bell_draw(streams_of[16], (LAYERS, EXPERTS, D, 2 * FFE), D ** -0.5, 0.1875, ((1, 4), (2, 8)), jnp.float32)
    expert_in_first = bell_draw(streams_of[17], (LAYERS, EXPERTS, D, 2 * FFE), (0.0275 * TOKENS ** 0.5), 20.0, ((1, 4), (2, 8)), jnp.float32)
    expert_in_second = jnp.clip(jnp.exp(math.log(204.8) - 1.4271164 * jax.random.uniform(streams_of[18], (LAYERS, EXPERTS, D, 2 * FFE), jnp.float32) ** steps_of(streams_of[18], (LAYERS, EXPERTS, D, 2 * FFE), ((1, 4), (2, 8)), -0.2, 0.2)), 49.152, 204.8)
    expert_down = bell_draw(streams_of[19], (LAYERS, EXPERTS, FFE, D), (FFE // 16) ** -0.5, 1.0, ((1, 4), (2, 8)), jnp.float32)
    expert_down_first = bell_draw(streams_of[20], (LAYERS, EXPERTS, FFE, D), (0.005 * TOKENS ** 0.5), 4.0, ((1, 4), (2, 8)), jnp.float32)
    expert_down_second = jnp.clip(jnp.exp(math.log(6.5536) - 1.3862944 * jax.random.uniform(streams_of[21], (LAYERS, EXPERTS, FFE, D), jnp.float32) ** steps_of(streams_of[21], (LAYERS, EXPERTS, FFE, D), ((1, 4), (2, 8)), -0.2, 0.2)), 1.6384, 6.5536)
    return {"tokens": tokens, "cotangent": cotangent, "routes": routes, "gate_weights": gate_weights, "norm_gains": norm_gains, "norm_gains_first": norm_gains_first, "norm_gains_second": norm_gains_second, "query_weight": query_weight, "query_first": query_first, "query_second": query_second, "keyval_weight": keyval_weight, "keyval_first": keyval_first, "keyval_second": keyval_second, "output_weight": output_weight, "output_first": output_first, "output_second": output_second, "expert_in": expert_in, "expert_in_first": expert_in_first, "expert_in_second": expert_in_second, "expert_down": expert_down, "expert_down_first": expert_down_first, "expert_down_second": expert_down_second}


NORM_EPS = 1e-05
ROPE_BASE = 10000.0
BETA_ONE = 0.9
BETA_TWO = 0.95
ADAM_EPS = 1e-08
LEARN_RATE = 0.1
WEIGHT_DECAY = 0.1
MASK_FILL = -1e+30
HIGHEST = lax.Precision.HIGHEST

@jax.custom_vjp
def low(v):
    return lax.optimization_barrier(v.astype(jnp.bfloat16)).astype(jnp.float32)

@jax.custom_vjp
def low_back(v):
    return v

def low_keep(v):
    return (low(v), None)

def low_pass(kept, grad):
    return (grad,)

def back_keep(v):
    return (v, None)

def back_low(kept, grad):
    return (low(grad),)
low.defvjp(low_keep, low_pass)
low_back.defvjp(back_keep, back_low)

def round_both(values):
    return low(low_back(values))

def rope_tables(length, width):
    half_width = width // 2
    position = jnp.arange(length, dtype=jnp.int32).astype(jnp.float32)
    exponent = jnp.arange(half_width, dtype=jnp.int32).astype(jnp.float32) * (-2.0 / width)
    frequency = jnp.exp(exponent * math.log(ROPE_BASE))
    angle = position[:, None] * frequency[None, :]
    return (jnp.cos(angle), jnp.sin(angle))

def rotate(values, cosine, sine_table):
    half_width = values.shape[-1] // 2
    first_half = values[..., :half_width]
    second_half = values[..., half_width:]
    cos_wide = cosine[None, :, None, :]
    sin_wide = sine_table[None, :, None, :]
    return jnp.concatenate([first_half * cos_wide - second_half * sin_wide, second_half * cos_wide + first_half * sin_wide], axis=-1)

def rms_scale(values):
    return lax.rsqrt(lax.optimization_barrier(jnp.mean(values * values, axis=-1, keepdims=True)) + NORM_EPS)

@jax.checkpoint
def attend_sequence(parts):
    queries, keys, values = parts
    scale_factor = 1.0 / math.sqrt(queries.shape[-1])
    scores = low_back(jnp.einsum('tkgd,ukd->kgtu', queries, keys, precision=HIGHEST) * scale_factor)
    length = queries.shape[0]
    row_index = lax.broadcasted_iota(jnp.int32, (length, length), 0)
    column_index = lax.broadcasted_iota(jnp.int32, (length, length), 1)
    scores = jnp.where(column_index <= row_index, scores, MASK_FILL)
    total = jax.nn.logsumexp(scores, axis=-1, keepdims=True)
    probability = low(jnp.exp(scores - total))
    return jnp.einsum('kgtu,ukd->tkgd', probability, values, precision=HIGHEST)

def attention(normed, query_w, keyval_w):
    row_count = normed.shape[0]
    seq_count = row_count // SEQ_LEN
    group_size = HEADS // KV
    query_lin = jnp.dot(normed, query_w, precision=HIGHEST).reshape(seq_count, SEQ_LEN, HEADS, HD)
    keyval_lin = jnp.dot(normed, keyval_w, precision=HIGHEST).reshape(seq_count, SEQ_LEN, KV, 2, HD)
    cosine, sine_table = rope_tables(SEQ_LEN, HD)
    queries = low(rotate(low_back(query_lin), cosine, sine_table)).reshape(seq_count, SEQ_LEN, KV, group_size, HD)
    keys = low(rotate(low_back(keyval_lin[:, :, :, 0]), cosine, sine_table))
    values = round_both(keyval_lin[:, :, :, 1])
    heads = lax.map(attend_sequence, (queries, keys, values))
    return round_both(heads.reshape(row_count, HEADS * HD))

def expert_group(parts, in_layer, down_layer):
    normed, route_rows, gate_rows = parts
    row_count = normed.shape[0]
    token_ids = jnp.arange(row_count, dtype=jnp.int32)

    def one_expert(summed, expert_parts):
        expert_id, in_one, down_one = expert_parts
        match = route_rows == expert_id
        chosen = jnp.any(match, axis=-1)
        weight = lax.optimization_barrier(jnp.sum(jnp.where(match, gate_rows, 0.0), axis=-1))
        slot = jnp.cumsum(chosen.astype(jnp.int32)) - 1
        target = jnp.where(chosen, slot, CAP).astype(jnp.int32)
        index = jnp.zeros((CAP,), jnp.int32).at[target].set(token_ids, mode='drop')
        slot_weight = jnp.zeros((CAP,), jnp.float32).at[target].set(weight, mode='drop')
        slot_rows = normed[index]
        hidden_lin = low_back(jnp.dot(slot_rows, in_one, precision=HIGHEST))
        gate_lin = hidden_lin[:, :FFE]
        up_lin = hidden_lin[:, FFE:]
        active = low(gate_lin * jax.nn.sigmoid(gate_lin) * up_lin)
        expert_out = low_back(jnp.dot(active, down_one, precision=HIGHEST))
        summed = summed.at[index].add(slot_weight[:, None] * expert_out)
        return (summed, None)
    expert_ids = jnp.arange(EXPERTS, dtype=jnp.int32)
    summed, unused = lax.scan(jax.checkpoint(one_expert), jnp.zeros((row_count, D), jnp.float32), (expert_ids, in_layer, down_layer))
    return summed

def forward(stream, gains, query_w, keyval_w, output_w, in_w, down_w, routes, gate_weights):
    row_count = stream.shape[0]
    groups = row_count // GROUP_TOK
    for layer_index in range(LAYERS):
        unit_one = stream * rms_scale(stream)
        normed = low(unit_one * gains[layer_index, 0])
        heads = attention(normed, query_w[layer_index], keyval_w[layer_index])
        stream = stream + low_back(jnp.dot(heads, output_w[layer_index], precision=HIGHEST))
        unit_two = stream * rms_scale(stream)
        normed_two = low(unit_two * gains[layer_index, 1])
        in_layer = in_w[layer_index]
        down_layer = down_w[layer_index]
        group_fn = jax.checkpoint(lambda parts: expert_group(parts, in_layer, down_layer))
        mixed = lax.map(group_fn, (normed_two.reshape(groups, GROUP_TOK, D), routes[layer_index].reshape(groups, GROUP_TOK, TOPK), gate_weights[layer_index].reshape(groups, GROUP_TOK, TOPK)))
        stream = stream + low_back(mixed.reshape(row_count, D))
    return stream

def adam_update(master, first_moment, second_moment, gradient, decay_rate):
    first_new = BETA_ONE * first_moment + (1.0 - BETA_ONE) * gradient
    second_new = BETA_TWO * second_moment + (1.0 - BETA_TWO) * gradient * gradient
    first_fixed = first_new / (1.0 - BETA_ONE ** STEP)
    second_fixed = second_new / (1.0 - BETA_TWO ** STEP)
    master_new = master - LEARN_RATE * (first_fixed / (jnp.sqrt(second_fixed) + ADAM_EPS) + decay_rate * master)
    return (master_new, first_new, second_new)

def adam_change(first_moment, second_moment, gradient):
    first_new = BETA_ONE * first_moment + (1.0 - BETA_ONE) * gradient
    second_new = BETA_TWO * second_moment + (1.0 - BETA_TWO) * gradient * gradient
    first_fixed = first_new / (1.0 - BETA_ONE ** STEP)
    second_fixed = second_new / (1.0 - BETA_TWO ** STEP)
    change = -LEARN_RATE * (first_fixed / (jnp.sqrt(second_fixed) + ADAM_EPS))
    return (change, first_new, second_new)

def to_low(master):
    return lax.optimization_barrier(master.astype(jnp.bfloat16)).astype(jnp.float32)

def reference(tokens, cotangent, routes, gate_weights, norm_gains, norm_gains_first, norm_gains_second, query_weight, query_first, query_second, keyval_weight, keyval_first, keyval_second, output_weight, output_first, output_second, expert_in, expert_in_first, expert_in_second, expert_down, expert_down_first, expert_down_second):

    def forward_all(stream, gains, query_w, keyval_w, output_w, in_w, down_w):
        return forward(stream, gains, query_w, keyval_w, output_w, in_w, down_w, routes, gate_weights)
    block_out, pullback = jax.vjp(forward_all, tokens.astype(jnp.float32), norm_gains, to_low(query_weight), to_low(keyval_weight), to_low(output_weight), to_low(expert_in), to_low(expert_down))
    grads = pullback(cotangent.astype(jnp.float32))
    gains_new = adam_change(norm_gains_first, norm_gains_second, grads[1])
    query_new = adam_update(query_weight, query_first, query_second, grads[2], WEIGHT_DECAY)
    keyval_new = adam_update(keyval_weight, keyval_first, keyval_second, grads[3], WEIGHT_DECAY)
    output_new = adam_update(output_weight, output_first, output_second, grads[4], WEIGHT_DECAY)
    in_new = adam_update(expert_in, expert_in_first, expert_in_second, grads[5], WEIGHT_DECAY)
    down_new = adam_update(expert_down, expert_down_first, expert_down_second, grads[6], WEIGHT_DECAY)
    return (block_out, grads[0], gains_new[0], gains_new[1], gains_new[2], query_new[0], query_new[1], query_new[2], keyval_new[0], keyval_new[1], keyval_new[2], output_new[0], output_new[1], output_new[2], in_new[0], in_new[1], in_new[2], down_new[0], down_new[1], down_new[2])
```

```python
import functools
import math

import jax
import jax.numpy as jnp
import numpy as np
from jax import lax
from jax.experimental import pallas as pl
from jax.experimental.pallas import tpu as pltpu
from jax.sharding import PartitionSpec as P

D = 1024
HEADS = 16
KV = 8
HD = 64
FFE = 512
SEQ_LEN = 512
STEP = 10
PIECES = 2
QBLK = 256

NORM_EPS = 1e-05
ROPE_BASE = 10000.0
BETA_ONE = 0.9
BETA_TWO = 0.95
ADAM_EPS = 1e-08
LEARN_RATE = 0.1
WEIGHT_DECAY = 0.1
MASK_FILL = -1e30
SCALE = 1.0 / math.sqrt(HD)

bf16 = jnp.bfloat16
f32 = jnp.float32
ANY = pl.BlockSpec(memory_space=pl.ANY)
SMEM = pl.BlockSpec(memory_space=pltpu.SMEM)
VMEM = pl.BlockSpec(memory_space=pltpu.VMEM)


def dot(a, b):
    return jnp.dot(a, b, preferred_element_type=f32)


def dot_t(a, b):
    return lax.dot_general(a, b, (((1,), (1,)), ((), ())), preferred_element_type=f32)


def t_dot(a, b):
    return lax.dot_general(a, b, (((0,), (0,)), ((), ())), preferred_element_type=f32)


def rope_tables():
    half = HD // 2
    position = np.arange(SEQ_LEN, dtype=np.float32)
    exponent = np.arange(half, dtype=np.float32) * np.float32(-2.0 / HD)
    frequency = np.exp(exponent * np.float32(math.log(ROPE_BASE))).astype(np.float32)
    angle = (position[:, None] * frequency[None, :]).astype(np.float32)
    cosine = np.cos(angle).astype(np.float32)
    sine = np.sin(angle).astype(np.float32)
    return np.tile(cosine, (1, 4)), np.concatenate([-sine, sine, -sine, sine], axis=1)


def adam_update(master, first_moment, second_moment, gradient, decay_rate):
    first_new = BETA_ONE * first_moment + (1.0 - BETA_ONE) * gradient
    second_new = BETA_TWO * second_moment + (1.0 - BETA_TWO) * gradient * gradient
    first_fixed = first_new / (1.0 - BETA_ONE**STEP)
    second_fixed = second_new / (1.0 - BETA_TWO**STEP)
    master_new = master - LEARN_RATE * (
        first_fixed / (jnp.sqrt(second_fixed) + ADAM_EPS) + decay_rate * master
    )
    return (master_new, first_new, second_new)


def adam_change(first_moment, second_moment, gradient):
    first_new = BETA_ONE * first_moment + (1.0 - BETA_ONE) * gradient
    second_new = BETA_TWO * second_moment + (1.0 - BETA_TWO) * gradient * gradient
    first_fixed = first_new / (1.0 - BETA_ONE**STEP)
    second_fixed = second_new / (1.0 - BETA_TWO**STEP)
    change = -LEARN_RATE * (first_fixed / (jnp.sqrt(second_fixed) + ADAM_EPS))
    return (change, first_new, second_new)


def rms_scale(values):
    return lax.rsqrt(jnp.mean(values * values, axis=-1, keepdims=True) + NORM_EPS)


def weight_copies(place_ref, pieces, w_ref, sems, nz, nt, outward):
    rows, cols = D // (2 * nz), D // nt
    z, core, t = place_ref[0], place_ref[1], place_ref[2]
    copies = []
    for c in range(2):
        for k in range(nt):
            for j in range(nz):
                row = pl.multiple_of(((z ^ j) * 2 + (core ^ c)) * rows, rows)
                col = pl.multiple_of((t ^ k) * cols, cols)
                whole = w_ref.at[:, pl.ds(row, rows), pl.ds(col, cols)]
                part = pieces[c * nt + k].at[j]
                sem = sems.at[(c * nt + k) * nz + j]
                src, dst = (whole, part) if outward else (part, whole)
                copies.append(pltpu.make_async_copy(src, dst, sem))
    return copies


def rotate(x, cosine, sine, first_half):
    width = x.shape[-1]
    swapped = jnp.where(
        first_half, pltpu.roll(x, width - HD // 2, 1), pltpu.roll(x, HD // 2, 1)
    )
    return x * cosine + swapped * sine


def attend_forward_kernel(nz, nt, place_ref, tokens_ref, gains_ref, cos_ref, sin_ref, *rest):
    pieces = rest[: 2 * nt]
    s1_ref, n2_ref, q_ref, kv_ref, o_ref, lse_ref = rest[2 * nt : 2 * nt + 6]
    w_ref, qlin_ref, kvlin_ref, sems = rest[2 * nt + 6 :]
    length = tokens_ref.shape[0]
    copies = weight_copies(place_ref, pieces, w_ref, sems, nz, nt, False)
    for copy in copies:
        copy.start()
    stream = tokens_ref[...].astype(f32)
    n1 = (stream * rms_scale(stream) * gains_ref[0:1, :]).astype(bf16)
    for copy in copies:
        copy.wait()
    qlin_ref[...] = dot(n1, w_ref[0])
    kvlin_ref[...] = dot(n1, w_ref[1])
    lse_ref[...] = jnp.zeros_like(lse_ref)

    def group(g, carry):
        part = pl.ds(pl.multiple_of(g * 128, 128), 128)
        lane = lax.broadcasted_iota(jnp.int32, (length, 128), 1)
        low = lane < HD
        first_half = (lane & (HD // 2)) == 0
        cosine, sine = cos_ref[...], sin_ref[...]
        q = rotate(qlin_ref[:, part], cosine, sine, first_half)
        kv = kvlin_ref[:, part]
        kv = jnp.where(low, rotate(kv, cosine, sine, first_half), kv)
        q_ref[:, part] = q.astype(bf16)
        kv_ref[:, part] = kv.astype(bf16)
        vk = pltpu.roll(kv, HD, 1).astype(bf16)
        kv = kv.astype(bf16)
        heads = (
            (jnp.where(low, q, 0.0).astype(bf16), kv, vk),
            (jnp.where(low, 0.0, q).astype(bf16), vk, kv),
        )
        for b in range(length // QBLK):
            rows = slice(b * QBLK, (b + 1) * QBLK)
            keys = (b + 1) * QBLK
            row = lax.broadcasted_iota(jnp.int32, (QBLK, keys), 0) + b * QBLK
            column = lax.broadcasted_iota(jnp.int32, (QBLK, keys), 1)
            seen = column <= row
            outs = []
            lses = lse_ref[rows, :]
            lane_b = lax.broadcasted_iota(jnp.int32, (QBLK, 128), 1)
            for h, (qh, key_side, value_side) in enumerate(heads):
                scores = dot_t(qh[rows], key_side[:keys]) * SCALE
                scores = jnp.where(seen, scores, MASK_FILL)
                top = jnp.max(scores, axis=-1, keepdims=True)
                e = jnp.exp(scores - top)
                total = jnp.sum(e, axis=-1, keepdims=True)
                p = (e * (1.0 / total)).astype(bf16)
                outs.append(dot(p, value_side[:keys]))
                lses = jnp.where(lane_b == 2 * g + h, top + jnp.log(total), lses)
            lse_ref[rows, :] = lses
            o_ref[rows, part] = jnp.where(lane_b < HD, outs[0], outs[1]).astype(bf16)
        return carry

    lax.fori_loop(0, D // 128, group, 0)
    s1 = tokens_ref[...].astype(f32) + dot_t(o_ref[...], w_ref[2])
    s1_ref[...] = s1
    n2_ref[...] = (s1 * rms_scale(s1) * gains_ref[1:2, :]).astype(bf16)


def attend_forward(mesh_sizes, place, tokens, gains, pieces):
    nz, nt = mesh_sizes
    length = tokens.shape[0]
    cosine, sine = rope_tables()
    return pl.pallas_call(
        functools.partial(attend_forward_kernel, nz, nt),
        out_shape=(
            jax.ShapeDtypeStruct((length, D), f32),
            jax.ShapeDtypeStruct((length, D), bf16),
            jax.ShapeDtypeStruct((length, D), bf16),
            jax.ShapeDtypeStruct((length, D), bf16),
            jax.ShapeDtypeStruct((length, D), bf16),
            jax.ShapeDtypeStruct((length, 128), f32),
        ),
        in_specs=[SMEM] + [VMEM] * 4 + [ANY] * len(pieces),
        out_specs=[VMEM] * 6,
        scratch_shapes=[
            pltpu.VMEM((3, D, D), bf16),
            pltpu.VMEM((length, D), f32),
            pltpu.VMEM((length, D), f32),
            pltpu.SemaphoreType.DMA((2 * nt * nz,)),
        ],
        compiler_params=pltpu.CompilerParams(vmem_limit_bytes=48 * 2**20),
        cost_estimate=pl.CostEstimate(flops=12 * 10**9, bytes_accessed=16 * 2**20, transcendentals=4 * 2**20),
        name="attend_forward",
    )(place, tokens, gains, jnp.asarray(cosine), jnp.asarray(sine), *pieces)


def attend_backward_kernel(
    nz, nt, place_ref, tokens_ref, da_ref, gains_ref, cos_ref, sin_ref, q_ref, kv_ref, o_ref, lse_ref, *rest
):
    pieces = rest[: 2 * nt]
    dn1_ref = rest[2 * nt]
    grads = rest[2 * nt + 1 : 4 * nt + 1]
    w_ref, gw_ref, do_ref, dq_ref, dkv_ref, lse_t_ref, sems = rest[4 * nt + 1 :]
    length = tokens_ref.shape[0]
    copies = weight_copies(place_ref, pieces, w_ref, sems, nz, nt, False)
    for copy in copies:
        copy.start()
    da = da_ref[...]
    gw_ref[2] = t_dot(da, o_ref[...]).astype(bf16)
    lse_t_ref[...] = lse_ref[...].T
    for copy in copies:
        copy.wait()
    do_ref[...] = dot(da, w_ref[2]).astype(bf16)

    def group(g, carry):
        part = pl.ds(pl.multiple_of(g * 128, 128), 128)
        lane = lax.broadcasted_iota(jnp.int32, (length, 128), 1)
        low = lane < HD
        first_half = (lane & (HD // 2)) == 0
        cosine, sine = cos_ref[...], sin_ref[...]
        q = q_ref[:, part].astype(f32)
        kv = kv_ref[:, part].astype(f32)
        do = do_ref[:, part].astype(f32)
        vk = pltpu.roll(kv, HD, 1).astype(bf16)
        kv = kv.astype(bf16)
        q_low = jnp.where(low, q, 0.0).astype(bf16)
        q_high = jnp.where(low, 0.0, q).astype(bf16)
        q_moved = jnp.where(low, pltpu.roll(q, HD, 1), 0.0).astype(bf16)
        do_low = jnp.where(low, do, 0.0).astype(bf16)
        do_high = jnp.where(low, 0.0, do).astype(bf16)
        do_moved = jnp.where(low, 0.0, pltpu.roll(do, HD, 1)).astype(bf16)
        heads = (
            (q_low, kv, vk, do_low, q_low, do_moved),
            (q_high, vk, kv, do_high, q_moved, do_high),
        )
        blocks = length // QBLK
        dkv = [jnp.zeros((QBLK, 128), f32) for _ in range(blocks)]
        dqs = []
        for b in range(blocks):
            rows = slice(b * QBLK, (b + 1) * QBLK)
            keys = (b + 1) * QBLK
            row = lax.broadcasted_iota(jnp.int32, (keys, QBLK), 0)
            column = lax.broadcasted_iota(jnp.int32, (keys, QBLK), 1) + b * QBLK
            seen = row <= column
            both = []
            for h, (qh, key_side, value_side, doh, q_for_k, do_for_v) in enumerate(heads):
                scores = dot_t(key_side[:keys], qh[rows]) * SCALE
                scores = jnp.where(seen, scores, MASK_FILL)
                e = jnp.exp(scores - lse_t_ref[pl.ds(2 * g + h, 1), rows])
                dp = dot_t(value_side[:keys], doh[rows])
                mean = jnp.sum(e * dp, axis=0, keepdims=True)
                dz = (e * (dp - mean)).astype(bf16)
                both.append(t_dot(dz, key_side[:keys]))
                add = dot(dz, q_for_k[rows]) + dot(e.astype(bf16), do_for_v[rows])
                for i in range(b + 1):
                    dkv[i] = dkv[i] + add[i * QBLK : (i + 1) * QBLK]
            lane_b = lax.broadcasted_iota(jnp.int32, (QBLK, 128), 1)
            dqs.append(jnp.where(lane_b < HD, both[0], both[1]))
        dq = jnp.concatenate(dqs, axis=0) * SCALE
        dkv_all = jnp.concatenate(dkv, axis=0)
        dq_ref[:, part] = rotate(dq, cosine, -sine, first_half).astype(bf16)
        dk = rotate(dkv_all * SCALE, cosine, -sine, first_half)
        dkv_ref[:, part] = jnp.where(low, dk, dkv_all).astype(bf16)
        return carry

    lax.fori_loop(0, D // 128, group, 0)
    stream = tokens_ref[...].astype(f32)
    n1 = (stream * rms_scale(stream) * gains_ref[0:1, :]).astype(bf16)
    gw_ref[0] = t_dot(n1, dq_ref[...]).astype(bf16)
    gw_ref[1] = t_dot(n1, dkv_ref[...]).astype(bf16)
    outward = weight_copies(place_ref, grads, gw_ref, sems, nz, nt, True)
    for copy in outward:
        copy.start()
    dn1_ref[...] = dot_t(dq_ref[...], w_ref[0]) + dot_t(dkv_ref[...], w_ref[1])
    for copy in outward:
        copy.wait()


def attend_backward(mesh_sizes, place, tokens, da, gains, q, kv, o, lse, pieces):
    nz, nt = mesh_sizes
    length = tokens.shape[0]
    cosine, sine = rope_tables()
    rows, cols = D // (2 * nz), D // nt
    part = jax.ShapeDtypeStruct((nz, 3, rows, cols), bf16)
    out = pl.pallas_call(
        functools.partial(attend_backward_kernel, nz, nt),
        out_shape=(jax.ShapeDtypeStruct((length, D), f32),) + (part,) * (2 * nt),
        in_specs=[SMEM] + [VMEM] * 9 + [ANY] * len(pieces),
        out_specs=[VMEM] + [ANY] * (2 * nt),
        scratch_shapes=[
            pltpu.VMEM((3, D, D), bf16),
            pltpu.VMEM((3, D, D), bf16),
            pltpu.VMEM((length, D), bf16),
            pltpu.VMEM((length, D), bf16),
            pltpu.VMEM((length, D), bf16),
            pltpu.VMEM((128, length), f32),
            pltpu.SemaphoreType.DMA((2 * nt * nz,)),
        ],
        compiler_params=pltpu.CompilerParams(vmem_limit_bytes=52 * 2**20),
        cost_estimate=pl.CostEstimate(flops=20 * 10**9, bytes_accessed=24 * 2**20, transcendentals=4 * 2**20),
        name="attend_backward",
    )(place, tokens, da, gains, jnp.asarray(cosine), jnp.asarray(sine), q, kv, o, lse, *pieces)
    return out[0], out[1:]


def experts_kernel(first, last, count, n2_parts, dm_parts, *rest):
    tiles = count
    n2_parts, rest = rest[:tiles], rest[tiles:]
    dm_parts, rest = rest[:tiles], rest[tiles:]
    c_ref, win_ref, wdown_ref = rest[:3]
    rest = rest[3:]
    if not first:
        m_before, d_before = rest[:2]
        rest = rest[2:]
    m_ref, d_ref, gw_ref = rest[:3]
    n2_buf, dm_buf, n2_t, dm_t, m_acc, d_acc, gin, gdown, sems = rest[3:]
    i, e = pl.program_id(0), pl.program_id(1)
    slot = lax.rem(i, 2)
    experts = win_ref.shape[1]

    def start(tile):
        for j in range(tiles):

            @pl.when(tile == j)
            def _():
                pltpu.make_async_copy(n2_parts[j], n2_buf.at[j % 2], sems.at[0, j % 2]).start()
                pltpu.make_async_copy(dm_parts[j], dm_buf.at[j % 2], sems.at[1, j % 2]).start()

    @pl.when(e == 0)
    def _():
        @pl.when(i == 0)
        def _():
            start(0)

        for s in range(2):

            @pl.when(slot == s)
            def _():
                pltpu.make_async_copy(n2_parts[s], n2_buf.at[s], sems.at[0, s]).wait()
                pltpu.make_async_copy(dm_parts[s], dm_buf.at[s], sems.at[1, s]).wait()

        start(i + 1)
        n2_t[...] = n2_buf[slot].T
        dm_t[...] = dm_buf[slot].T
        if first:
            m_acc[...] = jnp.zeros_like(m_acc)
            d_acc[...] = jnp.zeros_like(d_acc)
        else:
            m_acc[...] = m_before[...]
            d_acc[...] = d_before[...]

    @pl.when(i == 0)
    def _():
        gin[e] = jnp.zeros(gin.shape[1:], f32)
        gdown[e] = jnp.zeros(gdown.shape[1:], f32)

    win = win_ref[:, e].reshape(D, D)
    wdown = wdown_ref[:, e].reshape(FFE, D)
    lane = lax.broadcasted_iota(jnp.int32, c_ref.shape, 1)
    c = jnp.sum(jnp.where(lane == e, c_ref[...], 0.0), axis=1, keepdims=True)
    hidden = dot(n2_buf[slot], win)
    gate, up = hidden[:, :FFE], hidden[:, FFE:]
    sigma = jax.nn.sigmoid(gate)
    silu = gate * sigma
    active = (c * silu * up).astype(bf16)
    m_acc[...] += dot(active, wdown)
    gdown[e] += dot(dm_t[...], active)
    da = c * dot_t(dm_buf[slot], wdown)
    dgate = da * up * (sigma + silu * (1.0 - sigma))
    dup = da * silu
    dh = jnp.concatenate([dgate.astype(bf16), dup.astype(bf16)], axis=1)
    gin[e] += dot(n2_t[...], dh)
    d_acc[...] += dot_t(dh, win)

    @pl.when(e == experts - 1)
    def _():
        m_ref[...] = m_acc[...].astype(m_ref.dtype)
        d_ref[...] = d_acc[...].astype(d_ref.dtype)

    @pl.when(i == tiles - 1)
    def _():
        nz, _, cores, rows, _ = gw_ref.shape
        rin = D // (nz * cores)
        gw_ref[:, 0, :, :rin, :] = gin[e].astype(bf16).reshape(nz, cores, rin, D)
        gw_ref[:, 0, :, rin:, :] = gdown[e].T.astype(bf16).reshape(nz, cores, rows - rin, D)


def experts_step(n2_parts, dm_parts, c, weights, before, last):
    tiles, rows = len(n2_parts), n2_parts[0].shape[0]
    nz, experts, cores, wrows, _ = weights.shape
    rin, rdown = D // (nz * cores), FFE // (nz * cores)
    first = before is None
    out_type = bf16 if last else f32
    tile_spec = pl.BlockSpec((rows, D), lambda i, e: (i, 0))
    once = pl.Buffered(1)
    in_specs = (
        [ANY] * (2 * tiles)
        + [
            pl.BlockSpec((rows, experts), lambda i, e: (i, 0)),
            pl.BlockSpec((nz, experts, cores, rin, D), lambda i, e: (0, 0, 0, 0, 0), pipeline_mode=once),
            pl.BlockSpec(
                (nz, experts, cores, rdown, D), lambda i, e: (0, 0, 0, rin // rdown, 0), pipeline_mode=once
            ),
        ]
        + ([] if first else [tile_spec, tile_spec])
    )
    out_specs = (
        tile_spec,
        tile_spec,
        pl.BlockSpec(
            (nz, 1, cores, wrows, D), lambda i, e: (0, jnp.where(i == tiles - 1, e, 0), 0, 0, 0)
        ),
    )
    return pl.pallas_call(
        functools.partial(experts_kernel, first, last, tiles, None, None),
        grid=(tiles, experts),
        out_shape=(
            jax.ShapeDtypeStruct((tiles * rows, D), out_type),
            jax.ShapeDtypeStruct((tiles * rows, D), out_type),
            jax.ShapeDtypeStruct(weights.shape, bf16),
        ),
        in_specs=in_specs,
        out_specs=out_specs,
        scratch_shapes=[
            pltpu.VMEM((2, rows, D), bf16),
            pltpu.VMEM((2, rows, D), bf16),
            pltpu.VMEM((D, rows), bf16),
            pltpu.VMEM((D, rows), bf16),
            pltpu.VMEM((rows, D), f32),
            pltpu.VMEM((rows, D), f32),
            pltpu.VMEM((experts, D, D), f32),
            pltpu.VMEM((experts, D, FFE), f32),
            pltpu.SemaphoreType.DMA((2, 2)),
        ],
        compiler_params=pltpu.CompilerParams(
            vmem_limit_bytes=60 * 2**20, dimension_semantics=("arbitrary", "arbitrary")
        ),
        cost_estimate=pl.CostEstimate(
            flops=tiles * rows * experts * 12 * D * FFE * 3 // 2,
            bytes_accessed=64 * 2**20,
            transcendentals=tiles * rows * experts * FFE,
        ),
        name="experts",
    )(*n2_parts, *dm_parts, c, weights, weights, *([] if first else before))


def on_device(
    ndp,
    nt,
    tokens,
    cotangent,
    routes,
    gate_weights,
    norm_gains,
    norm_gains_first,
    norm_gains_second,
    query_weight,
    query_first,
    query_second,
    keyval_weight,
    keyval_first,
    keyval_second,
    output_weight,
    output_first,
    output_second,
    expert_in,
    expert_in_first,
    expert_in_second,
    expert_down,
    expert_down_first,
    expert_down_second,
):
    nz = ndp // 2
    place_dp = lax.axis_index("dp")
    t = lax.axis_index("tensor")
    z, core = place_dp // 2, place_dp % 2
    place = jnp.stack([z, core, t]).astype(jnp.int32)
    rows = tokens.shape[0]
    sharers = max(1, SEQ_LEN // rows)

    def swap_core(x):
        return lax.ppermute(x, "dp", [(i, i ^ 1) for i in range(ndp)])

    def swap_z(x, j):
        return lax.ppermute(x, "dp", [(i, i ^ (2 * j)) for i in range(ndp)])

    def swap_t(x, k):
        return lax.ppermute(x, "tensor", [(i, i ^ k) for i in range(nt)])

    def spread_t(x):
        return [x] + [swap_t(x, k) for k in range(1, nt)]

    def spread_z(x):
        return [x] + [swap_z(x, j) for j in range(1, nz)]

    own = jnp.stack(
        [query_weight[0].astype(bf16), keyval_weight[0].astype(bf16), output_weight[0].T.astype(bf16)]
    )
    column = jnp.stack(spread_z(own))
    pieces = spread_t(column)
    pieces = pieces + [swap_core(piece) for piece in pieces]
    gains_z = jnp.stack(spread_z(norm_gains[0]))
    gains_t = jnp.stack(spread_t(gains_z))
    gains_all = jnp.stack([gains_t, swap_core(gains_t)])
    ids = jnp.arange(2 * nz * nt, dtype=jnp.int32)
    spot = (((ids // nt) % 2 ^ core) * nt + (ids % nt ^ t)) * nz + (ids // nt // 2 ^ z)
    gains = jnp.take(gains_all.reshape(2 * nz * nt, 2, -1), spot, axis=0)
    gains = gains.transpose(1, 0, 2).reshape(2, D)

    low = jnp.concatenate([expert_in[0].astype(bf16), expert_down[0].astype(bf16)], axis=1)
    half = low.shape[0] // 2
    mine = lax.dynamic_slice_in_dim(low, core * half, half, 0)
    theirs = lax.dynamic_slice_in_dim(low, (1 - core) * half, half, 0)
    got = swap_core(theirs)
    is_zero = core == 0
    shard = jnp.stack([jnp.where(is_zero, mine, got), jnp.where(is_zero, got, mine)], axis=1)
    groups = [[2 * i + c for i in range(nz)] for c in range(2)]
    per = half // PIECES
    weights = [
        lax.all_gather(shard[i * per : (i + 1) * per], "dp", axis=0, tiled=False, axis_index_groups=groups)
        for i in range(PIECES)
    ]

    dm_own = spread_t(cotangent)
    dm_parts = dm_own + [swap_core(part) for part in dm_own]

    ids = t * 2 * half + jnp.arange(2 * half, dtype=jnp.int32)
    chosen = routes[0].T[None, :, :] == ids[:, None, None]
    c_all = jnp.sum(jnp.where(chosen, gate_weights[0].T[None, :, :], 0.0), axis=1)
    c_mine = lax.dynamic_slice_in_dim(c_all, core * half, half, 0)
    c_got = swap_core(lax.dynamic_slice_in_dim(c_all, (1 - core) * half, half, 0))
    c_both = jnp.stack([c_mine, c_got]).reshape(2, half, nt, rows)
    order = jnp.arange(nt, dtype=jnp.int32) ^ t
    c_both = jnp.take(c_both, order, axis=2)
    c_rows = c_both.transpose(0, 2, 3, 1).reshape(2 * nt * rows, half)

    sequence = tokens
    if sharers > 1:
        seq_groups = [list(range(i, i + sharers)) for i in range(0, nt, sharers)]
        sequence = lax.all_gather(tokens, "tensor", axis=0, tiled=True, axis_index_groups=seq_groups)
    first_row = (t % sharers) * rows
    s1, n2, q, kv, o, lse = attend_forward((nz, nt), place, sequence, gains, pieces)
    if sharers > 1:
        s1 = lax.dynamic_slice_in_dim(s1, first_row, rows, 0)
        n2 = lax.dynamic_slice_in_dim(n2, first_row, rows, 0)

    n2_own = spread_t(n2)
    n2_parts = n2_own + [swap_core(part) for part in n2_own]
    before = None
    expert_grads = []
    for i in range(PIECES):
        m_sum, d_sum, gw = experts_step(
            n2_parts,
            dm_parts,
            c_rows[:, i * per : (i + 1) * per],
            weights[i],
            before,
            i == PIECES - 1,
        )
        before = (m_sum, d_sum)
        expert_grads.append(
            lax.psum_scatter(gw, "dp", scatter_dimension=0, tiled=False, axis_index_groups=groups)
        )

    def collect(partial_sums):
        block = nt * rows
        both = partial_sums[:block] + swap_core(partial_sums[block:])
        total = both[:rows].astype(f32)
        for k in range(1, nt):
            total = total + swap_t(both[k * rows : (k + 1) * rows], k).astype(f32)
        return total

    dn2 = collect(d_sum)
    block_out = s1 + collect(m_sum)

    grad = cotangent.astype(f32)
    inverse = rms_scale(s1)
    unit = s1 * inverse
    gain_two = jnp.sum(dn2 * unit, axis=0)
    scaled = dn2 * gains[1]
    gs1 = grad + inverse * (scaled - unit * jnp.mean(scaled * unit, axis=-1, keepdims=True))

    da = gs1.astype(bf16)
    if sharers > 1:
        da = lax.all_gather(da, "tensor", axis=0, tiled=True, axis_index_groups=seq_groups)
    dn1, gw_parts = attend_backward((nz, nt), place, sequence, da, gains, q, kv, o, lse, pieces)
    if sharers > 1:
        dn1 = lax.dynamic_slice_in_dim(dn1, first_row, rows, 0)

    stream = tokens.astype(f32)
    inverse = rms_scale(stream)
    unit = stream * inverse
    gain_one = jnp.sum(dn1 * unit, axis=0)
    scaled = dn1 * gains[0]
    input_grad = gs1 + inverse * (scaled - unit * jnp.mean(scaled * unit, axis=-1, keepdims=True))

    by_t = [gw_parts[k] + swap_core(gw_parts[nt + k]) for k in range(nt)]
    by_z = by_t[0].astype(f32)
    for k in range(1, nt):
        by_z = by_z + swap_t(by_t[k], k).astype(f32)
    by_z = by_z.astype(bf16)
    small = by_z[0].astype(f32)
    for j in range(1, nz):
        small = small + swap_z(by_z[j], j).astype(f32)
    small = small * (1.0 / sharers)

    gg = jnp.stack([gain_one, gain_two])
    gg = gg + swap_core(gg)
    gg = sum(spread_t(gg)[1:], gg)
    gg = sum(spread_z(gg)[1:], gg)
    width = norm_gains.shape[2]
    gg = lax.dynamic_slice_in_dim(gg, (place_dp * nt + t) * width, width, 1)[None]

    by_core = [[], []]
    for got in expert_grads:
        mine = lax.dynamic_index_in_dim(got, core, 1, keepdims=False)
        recv = swap_core(lax.dynamic_index_in_dim(got, 1 - core, 1, keepdims=False))
        by_core[0].append(jnp.where(is_zero, mine, recv))
        by_core[1].append(jnp.where(is_zero, recv, mine))
    expert_grad = jnp.concatenate(by_core[0] + by_core[1], axis=0).astype(f32)[None]
    rin = expert_in.shape[2]

    gains_new = adam_change(norm_gains_first, norm_gains_second, gg)
    query_new = adam_update(query_weight, query_first, query_second, small[0:1], WEIGHT_DECAY)
    keyval_new = adam_update(keyval_weight, keyval_first, keyval_second, small[1:2], WEIGHT_DECAY)
    output_new = adam_update(output_weight, output_first, output_second, small[2].T[None], WEIGHT_DECAY)
    in_new = adam_update(
        expert_in, expert_in_first, expert_in_second, expert_grad[:, :, :rin], WEIGHT_DECAY
    )
    down_new = adam_update(
        expert_down, expert_down_first, expert_down_second, expert_grad[:, :, rin:], WEIGHT_DECAY
    )
    return (block_out, input_grad) + gains_new + query_new + keyval_new + output_new + in_new + down_new


def solution(mesh):
    rows = P(("dp", "tensor"), None)
    by_rows = P(None, "dp", None)
    gains = P(None, None, ("dp", "tensor"))
    proj = P(None, "dp", "tensor")
    out_proj = P(None, "tensor", "dp")
    expert = P(None, "tensor", "dp", None)
    params = (gains,) * 3 + (proj,) * 6 + (out_proj,) * 3 + (expert,) * 6
    return jax.shard_map(
        functools.partial(on_device, mesh.shape["dp"], mesh.shape["tensor"]),
        mesh=mesh,
        in_specs=(rows, rows, by_rows, by_rows) + params,
        out_specs=(rows, rows) + params,
        check_vma=False,
    )
```

```python
import functools
import math

import jax
import jax.numpy as jnp
import numpy as np
from jax import lax
from jax.experimental import pallas as pl
from jax.experimental.pallas import tpu as pltpu
from jax.sharding import PartitionSpec as P

D = 1024
HD = 64
FFE = 512
SEQ_LEN = 512
STEP = 10
CALLS = (((0, 2),), ((2, 3), (3, 4)))
GATHERS = ((0, 2), (2, 3), (3, 4))
QBLK = 256
SUB = 256
CHUNK = 256
SLOTS = 2560
AHEAD = 4
HELD = 3072

NORM_EPS = 1e-05
ROPE_BASE = 10000.0
BETA_ONE = 0.9
BETA_TWO = 0.95
ADAM_EPS = 1e-08
LEARN_RATE = 0.1
WEIGHT_DECAY = 0.1
MASK_FILL = -1e30
SCALE = 1.0 / math.sqrt(HD)

bf16 = jnp.bfloat16
f32 = jnp.float32
ANY = pl.BlockSpec(memory_space=pl.ANY)
COST = pl.CostEstimate(flops=1, bytes_accessed=1, transcendentals=0)
HBM = pl.BlockSpec(memory_space=pltpu.HBM)
SMEM = pl.BlockSpec(memory_space=pltpu.SMEM)
VMEM = pl.BlockSpec(memory_space=pltpu.VMEM)


def dot(a, b):
    return jnp.dot(a, b, preferred_element_type=f32)


def dot_t(a, b):
    return lax.dot_general(a, b, (((1,), (1,)), ((), ())), preferred_element_type=f32)


def t_dot(a, b):
    return lax.dot_general(a, b, (((0,), (0,)), ((), ())), preferred_element_type=f32)


def rope_tables():
    half = HD // 2
    position = np.arange(SEQ_LEN, dtype=np.float32)
    exponent = np.arange(half, dtype=np.float32) * np.float32(-2.0 / HD)
    frequency = np.exp(exponent * np.float32(math.log(ROPE_BASE))).astype(np.float32)
    angle = (position[:, None] * frequency[None, :]).astype(np.float32)
    cosine = np.cos(angle).astype(np.float32)
    sine = np.sin(angle).astype(np.float32)
    return np.tile(cosine, (1, 4)), np.concatenate([-sine, sine, -sine, sine], axis=1)


def adam_update(master, first_moment, second_moment, gradient, decay_rate):
    first_new = BETA_ONE * first_moment + (1.0 - BETA_ONE) * gradient
    second_new = BETA_TWO * second_moment + (1.0 - BETA_TWO) * gradient * gradient
    first_fixed = first_new / (1.0 - BETA_ONE**STEP)
    second_fixed = second_new / (1.0 - BETA_TWO**STEP)
    master_new = master - LEARN_RATE * (
        first_fixed / (jnp.sqrt(second_fixed) + ADAM_EPS) + decay_rate * master
    )
    return (master_new, first_new, second_new)


def adam_change(first_moment, second_moment, gradient):
    first_new = BETA_ONE * first_moment + (1.0 - BETA_ONE) * gradient
    second_new = BETA_TWO * second_moment + (1.0 - BETA_TWO) * gradient * gradient
    first_fixed = first_new / (1.0 - BETA_ONE**STEP)
    second_fixed = second_new / (1.0 - BETA_TWO**STEP)
    change = -LEARN_RATE * (first_fixed / (jnp.sqrt(second_fixed) + ADAM_EPS))
    return (change, first_new, second_new)


def rms_scale(values):
    return lax.rsqrt(jnp.mean(values * values, axis=-1, keepdims=True) + NORM_EPS)


def weight_spots(place_ref, nz, nt):
    rows, cols = D // (2 * nz), D // nt
    z, core, t = place_ref[0], place_ref[1], place_ref[2]
    for c in range(2):
        for k in range(nt):
            for j in range(nz):
                row = pl.multiple_of(((z ^ j) * 2 + (core ^ c)) * rows, rows)
                col = pl.multiple_of((t ^ k) * cols, cols)
                yield c, k, j, (pl.ds(row, rows), pl.ds(col, cols))


def gather_copies(place_ref, pieces, first, w_ref, sem, nz, nt):
    rows = D // (2 * nz)
    return [
        pltpu.make_async_copy(
            pieces[c * nt + k].at[j, (first + member) * rows : (first + member + 1) * rows, :],
            w_ref.at[(member,) + spot],
            sem.at[((c * nt + k) * nz + j) * w_ref.shape[0] + member],
        )
        for c, k, j, spot in weight_spots(place_ref, nz, nt)
        for member in range(w_ref.shape[0])
    ]


def rotate(x, cosine, sine, first_half):
    width = x.shape[-1]
    swapped = jnp.where(
        first_half, pltpu.roll(x, width - HD // 2, 1), pltpu.roll(x, HD // 2, 1)
    )
    return x * cosine + swapped * sine


def join_gains(parts, width):
    owners = parts.shape[0]
    both = jnp.sum(parts[:, :, :128].astype(f32), axis=1)
    lane = lax.broadcasted_iota(jnp.int32, (owners, 128), 1)
    owner = lax.broadcasted_iota(jnp.int32, (owners, D), 0)
    mine = lax.broadcasted_iota(jnp.int32, (owners, D), 1) // width == owner
    out = []
    for values in (both, pltpu.roll(both, 128 - width, 1)):
        values = jnp.where(lane < width, values, 0.0)
        shift = width
        while shift < 128:
            values = values + pltpu.roll(values, shift, 1)
            shift *= 2
        wide = jnp.concatenate([values] * (D // 128), axis=1)
        out.append(jnp.sum(jnp.where(mine, wide, 0.0), axis=0, keepdims=True))
    return jnp.concatenate(out, axis=0)


def attend_forward_kernel(nz, nt, place_ref, tokens_ref, cos_ref, sin_ref, *rest):
    pieces = rest[: 2 * nt]
    q_ref, kv_ref, o_ref, lse_ref, w_ref, gains_ref = rest[2 * nt : 2 * nt + 6]
    qlin_ref, kvlin_ref, parts_ref, sems, gain_sems = rest[2 * nt + 6 :]
    length = tokens_ref.shape[0]
    rows = D // (2 * nz)
    z, core, t = place_ref[0], place_ref[1], place_ref[2]
    gain_copies = [
        pltpu.make_async_copy(
            pieces[c * nt + k].at[j, 2 * rows :, :],
            parts_ref.at[((z ^ j) * 2 + (core ^ c)) * nt + (t ^ k)],
            gain_sems.at[(c * nt + k) * nz + j],
        )
        for c in range(2)
        for k in range(nt)
        for j in range(nz)
    ]
    for copy in gain_copies:
        copy.start()
    copies = gather_copies(place_ref, pieces, 0, w_ref, sems, nz, nt)
    for copy in copies:
        copy.start()
    lse_ref[...] = jnp.zeros_like(lse_ref)
    for copy in gain_copies:
        copy.wait()
    gains_ref[...] = join_gains(parts_ref[...], D // (2 * nz * nt))
    stream = tokens_ref[...].astype(f32)
    n1 = (stream * rms_scale(stream) * gains_ref[0:1, :]).astype(bf16)
    for copy in copies:
        copy.wait()
    qlin_ref[...] = dot(n1, w_ref[0])
    kvlin_ref[...] = dot(n1, w_ref[1])

    def group(g, carry):
        part = pl.ds(pl.multiple_of(g * 128, 128), 128)
        lane = lax.broadcasted_iota(jnp.int32, (length, 128), 1)
        low = lane < HD
        first_half = (lane & (HD // 2)) == 0
        cosine, sine = cos_ref[...], sin_ref[...]
        q = rotate(qlin_ref[:, part], cosine, sine, first_half)
        kv = kvlin_ref[:, part]
        kv = jnp.where(low, rotate(kv, cosine, sine, first_half), kv)
        q_ref[:, part] = q.astype(bf16)
        kv_ref[:, part] = kv.astype(bf16)
        vk = pltpu.roll(kv, HD, 1).astype(bf16)
        kv = kv.astype(bf16)
        heads = (
            (jnp.where(low, q, 0.0).astype(bf16), kv, vk),
            (jnp.where(low, 0.0, q).astype(bf16), vk, kv),
        )
        for b in range(length // QBLK):
            rows = slice(b * QBLK, (b + 1) * QBLK)
            keys = (b + 1) * QBLK
            row = lax.broadcasted_iota(jnp.int32, (QBLK, keys), 0) + b * QBLK
            column = lax.broadcasted_iota(jnp.int32, (QBLK, keys), 1)
            seen = column <= row
            outs = []
            lses = lse_ref[rows, :]
            lane_b = lax.broadcasted_iota(jnp.int32, (QBLK, 128), 1)
            for h, (qh, key_side, value_side) in enumerate(heads):
                scores = dot_t(qh[rows], key_side[:keys]) * SCALE
                scores = jnp.where(seen, scores, MASK_FILL)
                top = jnp.max(scores, axis=-1, keepdims=True)
                e = jnp.exp(scores - top)
                total = jnp.sum(e, axis=-1, keepdims=True)
                p = (e * (1.0 / total)).astype(bf16)
                outs.append(dot(p, value_side[:keys]))
                lses = jnp.where(lane_b == 2 * g + h, top + jnp.log(total), lses)
            lse_ref[rows, :] = lses
            o_ref[rows, part] = jnp.where(lane_b < HD, outs[0], outs[1]).astype(bf16)
        return carry

    lax.fori_loop(0, D // 128, group, 0)


def attend_forward(mesh_sizes, place, tokens, pieces):
    nz, nt = mesh_sizes
    length = tokens.shape[0]
    cosine, sine = rope_tables()
    return pl.pallas_call(
        functools.partial(attend_forward_kernel, nz, nt),
        out_shape=(
            jax.ShapeDtypeStruct((length, D), bf16),
            jax.ShapeDtypeStruct((length, D), bf16),
            jax.ShapeDtypeStruct((length, D), bf16),
            jax.ShapeDtypeStruct((length, 128), f32),
            jax.ShapeDtypeStruct((2, D, D), bf16),
            jax.ShapeDtypeStruct((2, D), f32),
        ),
        in_specs=[SMEM] + [VMEM] * 3 + [ANY] * len(pieces),
        out_specs=[VMEM] * 6,
        scratch_shapes=[
            pltpu.VMEM((length, D), f32),
            pltpu.VMEM((length, D), f32),
            pltpu.VMEM((2 * nz * nt, 16, D // nt), bf16),
            pltpu.SemaphoreType.DMA((2 * nt * nz * 2,)),
            pltpu.SemaphoreType.DMA((2 * nt * nz,)),
        ],
        compiler_params=pltpu.CompilerParams(vmem_limit_bytes=40 * 2**20),
        cost_estimate=COST,
        name="attend_forward",
    )(place, tokens, jnp.asarray(cosine), jnp.asarray(sine), *pieces)


def attend_out_kernel(nz, nt, place_ref, tokens_ref, gains_ref, o_ref, *rest):
    pieces = rest[: 2 * nt]
    s1_ref, n2_ref, w_ref, sems = rest[2 * nt :]
    copies = gather_copies(place_ref, pieces, 0, w_ref, sems, nz, nt)
    for copy in copies:
        copy.start()
    for copy in copies:
        copy.wait()
    s1 = tokens_ref[...].astype(f32) + dot_t(o_ref[...], w_ref[0])
    s1_ref[...] = s1
    n2_ref[...] = (s1 * rms_scale(s1) * gains_ref[1:2, :]).astype(bf16)


def attend_out(mesh_sizes, place, tokens, gains, o, pieces):
    nz, nt = mesh_sizes
    length = tokens.shape[0]
    return pl.pallas_call(
        functools.partial(attend_out_kernel, nz, nt),
        out_shape=(
            jax.ShapeDtypeStruct((length, D), f32),
            jax.ShapeDtypeStruct((length, D), bf16),
            jax.ShapeDtypeStruct((1, D, D), bf16),
        ),
        in_specs=[SMEM] + [VMEM] * 3 + [ANY] * len(pieces),
        out_specs=[VMEM] * 3,
        scratch_shapes=[pltpu.SemaphoreType.DMA((2 * nt * nz,))],
        compiler_params=pltpu.CompilerParams(vmem_limit_bytes=32 * 2**20),
        cost_estimate=COST,
        name="attend_out",
    )(place, tokens, gains, o, *pieces)


def attend_backward_kernel(
    nz, nt, place_ref, tokens_ref, da_ref, gains_ref, gain_two_ref, cos_ref, sin_ref, q_ref, kv_ref, o_ref,
    lse_ref, w_ref, wo_ref, dn1_ref, own_ref, other_ref, gw_ref, gg_ref, do_ref, dq_ref, dkv_ref, lse_t_ref, sems
):
    length = tokens_ref.shape[0]
    rows, cols = D // (2 * nz), D // nt
    sides = (own_ref, other_ref)

    def member_copies(members):
        return [
            pltpu.make_async_copy(
                gw_ref.at[(member,) + spot],
                sides[c].at[k, j, member * rows : (member + 1) * rows, :],
                sems.at[member, (c * nt + k) * nz + j],
            )
            for member in members
            for c, k, j, spot in weight_spots(place_ref, nz, nt)
        ]

    gw_ref[2] = t_dot(da_ref[...], o_ref[...]).astype(bf16)
    first = member_copies((2,))
    for copy in first:
        copy.start()
    do_ref[...] = dot(da_ref[...], wo_ref[0]).astype(bf16)
    lse_t_ref[...] = lse_ref[...].T

    def group(g, carry):
        part = pl.ds(pl.multiple_of(g * 128, 128), 128)
        lane = lax.broadcasted_iota(jnp.int32, (length, 128), 1)
        low = lane < HD
        first_half = (lane & (HD // 2)) == 0
        cosine, sine = cos_ref[...], sin_ref[...]
        q = q_ref[:, part].astype(f32)
        kv = kv_ref[:, part].astype(f32)
        do = do_ref[:, part].astype(f32)
        vk = pltpu.roll(kv, HD, 1).astype(bf16)
        kv = kv.astype(bf16)
        q_low = jnp.where(low, q, 0.0).astype(bf16)
        q_high = jnp.where(low, 0.0, q).astype(bf16)
        q_moved = jnp.where(low, pltpu.roll(q, HD, 1), 0.0).astype(bf16)
        do_low = jnp.where(low, do, 0.0).astype(bf16)
        do_high = jnp.where(low, 0.0, do).astype(bf16)
        do_moved = jnp.where(low, 0.0, pltpu.roll(do, HD, 1)).astype(bf16)
        heads = (
            (q_low, kv, vk, do_low, q_low, do_moved),
            (q_high, vk, kv, do_high, q_moved, do_high),
        )
        blocks = length // QBLK
        dkv = [jnp.zeros((QBLK, 128), f32) for _ in range(blocks)]
        dqs = []
        for b in range(blocks):
            rows = slice(b * QBLK, (b + 1) * QBLK)
            keys = (b + 1) * QBLK
            row = lax.broadcasted_iota(jnp.int32, (keys, QBLK), 0)
            column = lax.broadcasted_iota(jnp.int32, (keys, QBLK), 1) + b * QBLK
            seen = row <= column
            both = []
            for h, (qh, key_side, value_side, doh, q_for_k, do_for_v) in enumerate(heads):
                scores = dot_t(key_side[:keys], qh[rows]) * SCALE
                scores = jnp.where(seen, scores, MASK_FILL)
                e = jnp.exp(scores - lse_t_ref[pl.ds(2 * g + h, 1), rows])
                dp = dot_t(value_side[:keys], doh[rows])
                mean = jnp.sum(e * dp, axis=0, keepdims=True)
                dz = (e * (dp - mean)).astype(bf16)
                both.append(t_dot(dz, key_side[:keys]))
                add = dot(dz, q_for_k[rows]) + dot(e.astype(bf16), do_for_v[rows])
                for i in range(b + 1):
                    dkv[i] = dkv[i] + add[i * QBLK : (i + 1) * QBLK]
            lane_b = lax.broadcasted_iota(jnp.int32, (QBLK, 128), 1)
            dqs.append(jnp.where(lane_b < HD, both[0], both[1]))
        dq = jnp.concatenate(dqs, axis=0) * SCALE
        dkv_all = jnp.concatenate(dkv, axis=0)
        dq_ref[:, part] = rotate(dq, cosine, -sine, first_half).astype(bf16)
        dk = rotate(dkv_all * SCALE, cosine, -sine, first_half)
        dkv_ref[:, part] = jnp.where(low, dk, dkv_all).astype(bf16)
        return carry

    lax.fori_loop(0, D // 128, group, 0)
    stream = tokens_ref[...].astype(f32)
    unit = stream * rms_scale(stream)
    n1 = (unit * gains_ref[0:1, :]).astype(bf16)
    gw_ref[0] = t_dot(n1, dq_ref[...]).astype(bf16)
    gw_ref[1] = t_dot(n1, dkv_ref[...]).astype(bf16)
    second = member_copies((0, 1))
    for copy in second:
        copy.start()
    dn1 = dot_t(dq_ref[...], w_ref[0]) + dot_t(dkv_ref[...], w_ref[1])
    dn1_ref[...] = dn1
    gain_one = jnp.sum(dn1 * unit, axis=0, keepdims=True)
    gg_ref[...] = jnp.zeros_like(gg_ref)
    for i in range(nt):
        gg_ref[i : i + 1, :] = gain_one[:, i * cols : (i + 1) * cols].astype(bf16)
        gg_ref[nt + i : nt + i + 1, :] = gain_two_ref[:, i * cols : (i + 1) * cols].astype(bf16)
    third = [
        pltpu.make_async_copy(gg_ref, sides[c].at[k, j, 3 * rows :, :], sems.at[3, (c * nt + k) * nz + j])
        for c in range(2)
        for k in range(nt)
        for j in range(nz)
    ]
    for copy in third:
        copy.start()
    for copy in first + second + third:
        copy.wait()


def attend_backward(mesh_sizes, place, tokens, da, gains, gain_two, q, kv, o, lse, weights, out_weight):
    nz, nt = mesh_sizes
    length = tokens.shape[0]
    cosine, sine = rope_tables()
    part = jax.ShapeDtypeStruct((nt, nz, 3 * D // (2 * nz) + 16, D // nt), bf16)
    return pl.pallas_call(
        functools.partial(attend_backward_kernel, nz, nt),
        out_shape=(jax.ShapeDtypeStruct((length, D), f32), part, part),
        in_specs=[SMEM] + [VMEM] * 12,
        out_specs=[VMEM, ANY, ANY],
        scratch_shapes=[
            pltpu.VMEM((3, D, D), bf16),
            pltpu.VMEM((16, D // nt), bf16),
            pltpu.VMEM((length, D), bf16),
            pltpu.VMEM((length, D), bf16),
            pltpu.VMEM((length, D), bf16),
            pltpu.VMEM((128, length), f32),
            pltpu.SemaphoreType.DMA((4, 2 * nt * nz)),
        ],
        compiler_params=pltpu.CompilerParams(vmem_limit_bytes=48 * 2**20),
        cost_estimate=COST,
        name="attend_backward",
    )(
        place, tokens, da, gains, gain_two, jnp.asarray(cosine), jnp.asarray(sine), q, kv, o, lse, weights, out_weight
    )


def gather_kernel(starts, experts, offs_ref, pos_ref, c_ref, *rest):
    tiles = len(starts) - 1
    n2_parts, dm_parts, rest = rest[:tiles], rest[tiles : 2 * tiles], rest[2 * tiles :]
    n2_out, dm_out, c_out, n2_in, dm_in, n2_slots, dm_slots, c_slots, in_sems, out_sems = rest
    subs = starts[-1] // SUB

    def block_copies(s):
        j = max(i for i in range(tiles) if starts[i] <= s * SUB)
        spot = pl.ds(s * SUB - starts[j], SUB)
        return (
            pltpu.make_async_copy(n2_parts[j].at[spot], n2_in.at[s % AHEAD], in_sems.at[0, s % AHEAD]),
            pltpu.make_async_copy(dm_parts[j].at[spot], dm_in.at[s % AHEAD], in_sems.at[1, s % AHEAD]),
        )

    def flush(e, chunk):
        spot = pl.ds(pl.multiple_of(chunk * CHUNK, CHUNK), CHUNK)
        return [
            pltpu.make_async_copy(slots.at[e, spot, :], out.at[e, spot, :], out_sems.at[i, e, chunk])
            for i, (slots, out) in enumerate(((n2_slots, n2_out), (dm_slots, dm_out), (c_slots, c_out)))
        ]

    for s in range(AHEAD - 1):
        for copy in block_copies(s):
            copy.start()

    def block(s, carry):
        for ahead in range(AHEAD - 1, subs):

            @pl.when(s + AHEAD - 1 == ahead)
            def _():
                for copy in block_copies(ahead):
                    copy.start()

        slot = lax.rem(s, AHEAD)
        pltpu.make_async_copy(n2_parts[0].at[pl.ds(0, SUB)], n2_in.at[slot], in_sems.at[0, slot]).wait()
        pltpu.make_async_copy(dm_parts[0].at[pl.ds(0, SUB)], dm_in.at[slot], in_sems.at[1, slot]).wait()
        begin = [offs_ref[e * (subs + 1) + s] for e in range(experts)]
        end = [offs_ref[e * (subs + 1) + s + 1] for e in range(experts)]
        most = functools.reduce(jnp.maximum, [end[e] - begin[e] for e in range(experts)])

        def fill(count):
            slots = lax.broadcasted_iota(jnp.int32, (count, SUB), 0).astype(f32)
            picks = []
            for e in range(experts):
                spot = pl.ds(pl.multiple_of(begin[e], 16), count)
                hit = slots == pos_ref[pl.ds(e * subs + s, 1), :]
                picks.append(jnp.where(hit, 1.0, 0.0).astype(bf16))
                c = jnp.sum(jnp.where(hit, c_ref[pl.ds(e * subs + s, 1), :], 0.0), axis=1, keepdims=True)
                c_slots[e, spot, :] = jnp.broadcast_to(c, (count, 128))
            pick = jnp.concatenate(picks, axis=0)
            for source, target in ((n2_in, n2_slots), (dm_in, dm_slots)):
                rows = dot(pick, source[slot]).astype(bf16)
                for e in range(experts):
                    spot = pl.ds(pl.multiple_of(begin[e], 16), count)
                    target[e, spot, :] = rows[e * count : (e + 1) * count]

        @pl.when(most <= SUB // 2)
        def _():
            fill(SUB // 2)

        @pl.when(most > SUB // 2)
        def _():
            fill(SUB)

        for e in range(experts):

            @pl.when(end[e] // CHUNK > begin[e] // CHUNK)
            def _():
                for copy in flush(e, begin[e] // CHUNK):
                    copy.start()

        return carry

    lax.fori_loop(0, subs, block, 0)
    for e in range(experts):
        total = offs_ref[e * (subs + 1) + subs]
        tail = pl.ds(pl.multiple_of(total, 16), CHUNK)
        n2_slots[e, tail, :] = jnp.zeros((CHUNK, D), bf16)
        dm_slots[e, tail, :] = jnp.zeros((CHUNK, D), bf16)
        c_slots[e, tail, :] = jnp.zeros((CHUNK, 128), f32)
        for copy in flush(e, total // CHUNK):
            copy.start()
    for e in range(experts):

        def drain(chunk, carry):
            for copy in flush(e, chunk):
                copy.wait()
            return carry

        lax.fori_loop(0, offs_ref[e * (subs + 1) + subs] // CHUNK + 1, drain, 0)


def gather(n2_parts, dm_parts, offs, pos, c):
    starts = [0]
    for n2_part in n2_parts:
        starts.append(starts[-1] + n2_part.shape[0])
    experts = pos.shape[0] * SUB // starts[-1]
    rows = jax.ShapeDtypeStruct((experts, SLOTS, D), bf16)
    return pl.pallas_call(
        functools.partial(gather_kernel, tuple(starts), experts),
        out_shape=(rows, rows, jax.ShapeDtypeStruct((experts, SLOTS, 128), f32)),
        in_specs=[SMEM, VMEM, VMEM] + [HBM] * (2 * len(n2_parts)),
        out_specs=(HBM, HBM, HBM),
        scratch_shapes=[
            pltpu.VMEM((AHEAD, SUB, D), bf16),
            pltpu.VMEM((AHEAD, SUB, D), bf16),
            pltpu.VMEM((experts, SLOTS, D), bf16),
            pltpu.VMEM((experts, SLOTS, D), bf16),
            pltpu.VMEM((experts, SLOTS, 128), f32),
            pltpu.SemaphoreType.DMA((2, AHEAD)),
            pltpu.SemaphoreType.DMA((3, experts, SLOTS // CHUNK)),
        ],
        compiler_params=pltpu.CompilerParams(vmem_limit_bytes=62 * 2**20),
        cost_estimate=COST,
        name="gather_rows",
    )(offs, pos, c, *n2_parts, *dm_parts)


def experts_kernel(first, subs, sources, kept, place_ref, offs_ref, n2_ref, dm_ref, c_ref, *rest):
    arrays = 1 + sources[-1][0]
    weights, rest = rest[:arrays], rest[arrays + kept :]
    m_ref, d_ref, gw_ref = rest[:3]
    win_buf, wdown_buf, n2_in, dm_in, c_in, m_out, d_out, zeros, gin, gdown, w_sems, in_sems, out_sems = rest[3:]
    e = pl.program_id(0)
    nz, cores, _, wrows, _ = gw_ref.shape
    rin, rdown = D // (nz * cores), FFE // (nz * cores)
    core = place_ref[1]
    total = offs_ref[(first + e) * (subs + 1) + subs]
    chunks = jnp.maximum((total + CHUNK - 1) // CHUNK, 1)

    def weight_copies(index):
        i, place = sources[index]
        slot = index % 2
        return [
            pltpu.make_async_copy(
                weights[i].at[:, side, place, spot, :], buf.at[slot, :, core ^ side], w_sems.at[2 * side + j, slot]
            )
            for side in range(2)
            for j, (spot, buf) in enumerate(((slice(0, rin), win_buf), (slice(rin, wrows), wdown_buf)))
        ]

    def in_copies(k, slot):
        spot = pl.ds(pl.multiple_of(k * CHUNK, CHUNK), CHUNK)
        return [
            pltpu.make_async_copy(source.at[first + e, spot, :], target.at[slot], in_sems.at[i, slot])
            for i, (source, target) in enumerate(((n2_ref, n2_in), (dm_ref, dm_in), (c_ref, c_in)))
        ]

    def out_copies(k, slot):
        spot = pl.ds(pl.multiple_of(k * CHUNK, CHUNK), CHUNK)
        return (
            pltpu.make_async_copy(m_out.at[slot], m_ref.at[e, spot, :], out_sems.at[0, slot]),
            pltpu.make_async_copy(d_out.at[slot], d_ref.at[e, spot, :], out_sems.at[1, slot]),
        )

    for copy in in_copies(0, 0):
        copy.start()

    @pl.when(e == 0)
    def _():
        for copy in weight_copies(0):
            copy.start()
        zeros[...] = jnp.zeros_like(zeros)

    for index in range(len(sources)):

        @pl.when(e == index)
        def _():
            for copy in weight_copies(index):
                copy.wait()
            if index + 1 < len(sources):
                for copy in weight_copies(index + 1):
                    copy.start()

    at = lax.rem(e, 2)

    def one_chunk(k, carry):
        slot = lax.rem(k, 2)
        for copy in in_copies(k, slot):
            copy.wait()

        @pl.when(k + 1 < chunks)
        def _():
            for copy in in_copies(k + 1, 1 - slot):
                copy.start()

        @pl.when(k >= 2)
        def _():
            for copy in out_copies(k - 2, slot):
                copy.wait()

        win = win_buf[at].reshape(D, D)
        wdown = wdown_buf[at].reshape(FFE, D)
        n2, dm, c = n2_in[slot], dm_in[slot], c_in[slot][:, 0:1]
        hidden = dot(n2, win)
        gate, up = hidden[:, :FFE], hidden[:, FFE:]
        sigma = jax.nn.sigmoid(gate)
        silu = gate * sigma
        active = (c * silu * up).astype(bf16)
        m_out[slot] = dot(active, wdown).astype(bf16)
        gdown[...] = jnp.where(k == 0, 0.0, gdown[...]) + dot(active.T, dm)
        da = c * dot_t(dm, wdown)
        dgate = da * up * (sigma + silu * (1.0 - sigma))
        dup = da * silu
        dh = jnp.concatenate([dgate.astype(bf16), dup.astype(bf16)], axis=1)
        gin[...] = jnp.where(k == 0, 0.0, gin[...]) + dot(n2.T, dh)
        d_out[slot] = dot_t(dh, win).astype(bf16)
        for copy in out_copies(k, slot):
            copy.start()
        return carry

    lax.fori_loop(0, chunks, one_chunk, 0)
    spot = pl.ds(pl.multiple_of(chunks * CHUNK, CHUNK), CHUNK)
    ends = (
        pltpu.make_async_copy(zeros, m_ref.at[e, spot, :], out_sems.at[0, 2]),
        pltpu.make_async_copy(zeros, d_ref.at[e, spot, :], out_sems.at[1, 2]),
    )
    for copy in ends:
        copy.start()
    for j in range(nz):
        for side in range(2):
            owner = 2 * j + (core ^ side)
            at_in, at_down = pl.multiple_of(owner * rin, rin), pl.multiple_of(owner * rdown, rdown)
            gw_ref[j, side, 0, :rin, :] = gin[pl.ds(at_in, rin), :].astype(bf16)
            gw_ref[j, side, 0, rin:, :] = gdown[pl.ds(at_down, rdown), :].astype(bf16)
    for copy in ends:
        copy.wait()
    for back in (1, 2):

        @pl.when(chunks >= back)
        def _():
            for copy in out_copies(chunks - back, lax.rem(chunks - back, 2)):
                copy.wait()


def experts_step(place, slots, offs, first, weights, sources, before, spot, count):
    nz, cores, _, wrows, _ = weights[0].shape
    experts = len(sources)
    rin, rdown = D // (nz * cores), FFE // (nz * cores)
    part = jax.ShapeDtypeStruct((experts, HELD, D), bf16)
    kept = [] if before is None else [before]
    subs = offs.shape[1] - 1
    return pl.pallas_call(
        functools.partial(experts_kernel, first, subs, sources, len(kept)),
        grid=(experts,),
        out_shape=(part, part, jax.ShapeDtypeStruct((nz, cores, count, wrows, D), bf16)),
        in_specs=[SMEM, SMEM] + [HBM] * (3 + len(weights) + len(kept)),
        out_specs=(HBM, HBM, pl.BlockSpec((nz, cores, 1, wrows, D), lambda e: (0, 0, spot + e, 0, 0))),
        scratch_shapes=[
            pltpu.VMEM((2, nz, cores, rin, D), bf16),
            pltpu.VMEM((2, nz, cores, rdown, D), bf16),
            pltpu.VMEM((2, CHUNK, D), bf16),
            pltpu.VMEM((2, CHUNK, D), bf16),
            pltpu.VMEM((2, CHUNK, 128), f32),
            pltpu.VMEM((2, CHUNK, D), bf16),
            pltpu.VMEM((2, CHUNK, D), bf16),
            pltpu.VMEM((CHUNK, D), bf16),
            pltpu.VMEM((D, D), f32),
            pltpu.VMEM((FFE, D), f32),
            pltpu.SemaphoreType.DMA((4, 2)),
            pltpu.SemaphoreType.DMA((3, 2)),
            pltpu.SemaphoreType.DMA((2, 3)),
        ],
        input_output_aliases={5 + len(weights): 2} if kept else {},
        compiler_params=pltpu.CompilerParams(
            vmem_limit_bytes=60 * 2**20, dimension_semantics=("arbitrary",)
        ),
        cost_estimate=COST,
        name="experts",
    )(place, offs.reshape(-1), *slots, *weights, *kept)


def scatter_kernel(halves, sources, experts, subs, offs_ref, pos_ref, *rest):
    arrays = 1 + sources[-1][1]
    parts, rest = rest[:arrays], rest[arrays:]
    outs, (slots, sems) = rest[: len(halves)], rest[len(halves) :]
    i, steps = pl.program_id(0), subs // 2
    low = min(halves) * steps
    high = low + len(halves) * steps

    @pl.when(i == 0)
    def _():
        def each(act):
            for spot, (e, array, index) in enumerate(sources):

                def one(chunk, carry):
                    rows = pl.ds(pl.multiple_of(chunk * CHUNK, CHUNK), CHUNK)
                    act(pltpu.make_async_copy(parts[array].at[index, rows, :], slots.at[spot, rows, :], sems.at[spot, chunk]))
                    return carry

                begin = offs_ref[e * (subs + 1) + low] // CHUNK
                end = (offs_ref[e * (subs + 1) + high] + CHUNK - 1) // CHUNK + 1
                lax.fori_loop(begin, end, one, 0)

        each(lambda copy: copy.start())
        each(lambda copy: copy.wait())

    block = lax.rem(i + halves[0] * steps, subs)
    lane = lax.broadcasted_iota(jnp.int32, (SUB, SUB), 1).astype(f32)
    picks = [jnp.where(lane == pos_ref[:, e : e + 1], 1.0, 0.0).astype(bf16) for e, _, _ in sources]
    windows = [
        slots[spot, pl.ds(pl.multiple_of(offs_ref[e * (subs + 1) + block], 16), SUB), :]
        for spot, (e, _, _) in enumerate(sources)
    ]
    total = dot(jnp.concatenate(picks, axis=1), jnp.concatenate(windows, axis=0))
    for j, out_ref in enumerate(outs):

        @pl.when(i // steps == j)
        def _():
            out_ref[...] = total.astype(bf16)


def scatter(offs, pos_columns, parts, halves):
    tokens, experts = pos_columns.shape
    sources = [
        (first + index, i, index) for i, (part, first) in enumerate(parts) for index in range(part.shape[0])
    ]
    subs = tokens // SUB
    steps = subs // 2
    shift = halves[0] * steps
    blocks = [
        pl.BlockSpec((SUB, D), lambda i, j=j: (jnp.clip(i - j * steps, 0, steps - 1), 0))
        for j in range(len(halves))
    ]
    return pl.pallas_call(
        functools.partial(scatter_kernel, halves, sources, experts, subs),
        grid=(len(halves) * steps,),
        out_shape=[jax.ShapeDtypeStruct((steps * SUB, D), bf16)] * len(halves),
        in_specs=[SMEM, pl.BlockSpec((SUB, experts), lambda i: (lax.rem(i + shift, subs), 0))]
        + [HBM] * len(parts),
        out_specs=blocks,
        scratch_shapes=[
            pltpu.VMEM((len(sources), HELD, D), bf16),
            pltpu.SemaphoreType.DMA((len(sources), HELD // CHUNK)),
        ],
        compiler_params=pltpu.CompilerParams(
            vmem_limit_bytes=60 * 2**20, dimension_semantics=("arbitrary",)
        ),
        cost_estimate=COST,
        name="scatter_rows",
    )(offs.reshape(-1), pos_columns, *[part for part, _ in parts])


def adam_kernel(per, place_ref, mine_ref, recv_ref, *rest):
    states, news = rest[:6], rest[-6:]
    here = pl.program_id(0) // per == place_ref[1]
    grad = jnp.where(here, mine_ref[0, 0], recv_ref[0]).astype(f32)
    rin = states[0].shape[2]
    for i, part in ((0, grad[:rin]), (3, grad[rin:])):
        masters = [ref[0, 0] for ref in states[i : i + 3]]
        for ref, new in zip(news[i : i + 3], adam_update(*masters, part, WEIGHT_DECAY)):
            ref[0, 0] = new


def adam_experts(place, a, mine, recv, states, before):
    experts, rin = states[0].shape[1:3]
    rdown = states[3].shape[2]
    per = recv.shape[0]
    half = experts // 2
    spec = [
        pl.BlockSpec((1, 1, r, D), lambda i, place: (0, i // per * half + a + i % per, 0, 0))
        for r in (rin, rdown)
    ]
    specs = [spec[0]] * 3 + [spec[1]] * 3
    kept = [] if before is None else list(before)
    return pl.pallas_call(
        functools.partial(adam_kernel, per),
        grid_spec=pltpu.PrefetchScalarGridSpec(
            num_scalar_prefetch=1,
            grid=(2 * per,),
            in_specs=[
                pl.BlockSpec((1, 1, rin + rdown, D), lambda i, place: (0, i % per, 0, 0)),
                pl.BlockSpec((1, rin + rdown, D), lambda i, place: (i % per, 0, 0)),
            ]
            + specs
            + [HBM] * len(kept),
            out_specs=specs,
        ),
        out_shape=[jax.ShapeDtypeStruct(state.shape, f32) for state in states],
        input_output_aliases={9 + i: i for i in range(len(kept))},
        compiler_params=pltpu.CompilerParams(
            vmem_limit_bytes=60 * 2**20, dimension_semantics=("arbitrary",)
        ),
        cost_estimate=COST,
        name="adam_experts",
    )(place, mine, recv, *states, *kept)


def on_device(
    ndp,
    nt,
    tokens,
    cotangent,
    routes,
    gate_weights,
    norm_gains,
    norm_gains_first,
    norm_gains_second,
    query_weight,
    query_first,
    query_second,
    keyval_weight,
    keyval_first,
    keyval_second,
    output_weight,
    output_first,
    output_second,
    expert_in,
    expert_in_first,
    expert_in_second,
    expert_down,
    expert_down_first,
    expert_down_second,
):
    nz = ndp // 2
    place_dp = lax.axis_index("dp")
    t = lax.axis_index("tensor")
    z, core = place_dp // 2, place_dp % 2
    place = jnp.stack([z, core, t]).astype(jnp.int32)
    rows = tokens.shape[0]
    sharers = max(1, SEQ_LEN // rows)

    def swap_core(x):
        return lax.ppermute(x, "dp", [(i, i ^ 1) for i in range(ndp)])

    def swap_z(x, j):
        return lax.ppermute(x, "dp", [(i, i ^ (2 * j)) for i in range(ndp)])

    def swap_t(x, k):
        return lax.ppermute(x, "tensor", [(i, i ^ k) for i in range(nt)])

    def spread_t(x):
        return [x] + [swap_t(x, k) for k in range(1, nt)]

    def spread_z(x):
        return [x] + [swap_z(x, j) for j in range(1, nz)]

    def after(x, *others):
        return lax.optimization_barrier((x,) + others)[0]

    def near(x):
        return [swap_t(x, k) for k in range(1, nt)] if nt != 4 else [swap_t(x, 1), swap_t(x, 2)]

    def far(x, others):
        mid = x.shape[0] // 2
        return [] if nt != 4 else [swap_t(others[0][:mid], 2), swap_t(others[1][mid:], 1)]

    width = norm_gains.shape[2]
    wrows, wcols = query_weight.shape[1:]
    high = lax.reduce_precision(norm_gains[0], 8, 7)
    middle = lax.reduce_precision(norm_gains[0] - high, 8, 7)
    gain_rows = jnp.stack([high, middle, norm_gains[0] - high - middle]).astype(bf16).reshape(3, 2 * width)
    own = jnp.concatenate(
        [
            query_weight[0].astype(bf16),
            keyval_weight[0].astype(bf16),
            jnp.pad(gain_rows, ((0, 13), (0, wcols - 2 * width))),
            output_weight[0].T.astype(bf16),
        ],
        axis=0,
    )
    own_z = spread_z(own)
    half = expert_in.shape[1] // 2
    groups = [[2 * i + c for i in range(nz)] for c in range(2)]

    def cut(quarters):
        return quarters[0] * half // 4, quarters[1] * half // 4

    def shard(a, b, *ready):
        masters = lax.optimization_barrier((expert_in, expert_down, own, *ready))[:2]

        def low(side):
            return jnp.concatenate(
                [lax.dynamic_slice_in_dim(w[0], side * half + a, b - a, 0).astype(bf16) for w in masters], axis=1
            )

        return jnp.stack([low(core), swap_core(low(1 - core))])

    spans = [cut(quarters) for quarters in GATHERS]
    spans = [(a, b) for a, b in spans if a < b]
    shards = [shard(*spans[0])]
    for a, b in spans[1:]:
        shards.append(shard(a, b, own_z[1]))
    own_z[1:], shards = lax.optimization_barrier((own_z[1:], shards))
    column = jnp.stack(own_z)
    held = {}
    for (a, b), part in zip(spans, shards):
        whole = lax.all_gather(after(part, column), "dp", axis=0, tiled=False, axis_index_groups=groups)
        held.update({i: (whole, i - a) for i in range(a, b)})
    pieces = spread_t(column[:, : 2 * wrows + 16])
    pieces_out = spread_t(after(column[:, 2 * wrows + 16 :], pieces[nt - 1]))
    dm_near = near(after(cotangent, *pieces_out[1:nt]))
    pieces = pieces + [swap_core(piece) for piece in pieces]
    pieces_out = pieces_out + [swap_core(piece) for piece in pieces_out]

    ids = t * 2 * half + jnp.arange(2 * half, dtype=jnp.int32)
    chosen = routes[0].T[None, :, :] == ids[:, None, None]
    c_all = jnp.sum(jnp.where(chosen, gate_weights[0].T[None, :, :], 0.0), axis=1)
    c_mine = lax.dynamic_slice_in_dim(c_all, core * half, half, 0)
    c_got = swap_core(lax.dynamic_slice_in_dim(c_all, (1 - core) * half, half, 0))
    c_both = jnp.stack([c_mine, c_got], axis=1).reshape(half, 2, nt, rows)
    c_both = jnp.take(c_both, jnp.arange(nt, dtype=jnp.int32) ^ t, axis=2)
    subs = 2 * nt * rows // SUB
    c_rows = c_both.reshape(half * subs, SUB)
    taken = c_rows != 0.0
    upto = lax.broadcasted_iota(jnp.int32, (SUB, SUB), 0) <= lax.broadcasted_iota(jnp.int32, (SUB, SUB), 1)
    rank = dot(taken.astype(bf16), upto.astype(bf16))
    pos = jnp.where(taken, rank - 1.0, -1.0)
    sizes = (rank[:, SUB - 1].astype(jnp.int32).reshape(half, subs) + 15) // 16 * 16
    offs = jnp.pad(jnp.cumsum(sizes, axis=1), ((0, 0), (1, 0)))
    pos_columns = pos.reshape(half, subs * SUB).T

    sequence = after(tokens, offs, pos, c_rows, pos_columns)
    if sharers > 1:
        seq_groups = [list(range(i, i + sharers)) for i in range(0, nt, sharers)]
        sequence = lax.all_gather(tokens, "tensor", axis=0, tiled=True, axis_index_groups=seq_groups)
    first_row = (t % sharers) * rows
    q, kv, o, lse, qkv_weights, gains = attend_forward((nz, nt), place, sequence, pieces)
    s1, n2, out_weight = attend_out((nz, nt), place, sequence, gains, o, pieces_out)
    if sharers > 1:
        s1 = lax.dynamic_slice_in_dim(s1, first_row, rows, 0)
        n2 = lax.dynamic_slice_in_dim(n2, first_row, rows, 0)

    n2_near = near(n2)
    n2_own = [n2] + n2_near + far(n2, n2_near)
    dm_near = list(lax.optimization_barrier((*dm_near, *n2_near))[: len(dm_near)])
    dm_own = [cotangent] + dm_near + far(cotangent, dm_near)
    dm_parts = dm_own + [swap_core(part) for part in dm_own]
    n2_parts = n2_own + [swap_core(part) for part in n2_own]
    slots = gather(n2_parts, dm_parts, offs.reshape(-1), pos, c_rows)
    m_parts, d_parts, expert_grads = [], [], []
    for calls in CALLS:
        start, stop = cut((calls[0][0], calls[-1][1]))
        gw = None
        for quarters in calls:
            a, b = cut(quarters)
            if a == b:
                continue
            arrays, sources = [], []
            for i in range(a, b):
                array, index = held[i]
                if not arrays or arrays[-1] is not array:
                    arrays.append(array)
                sources.append((len(arrays) - 1, index))
            m_part, d_part, gw = experts_step(
                place, slots, offs, a, arrays, tuple(sources), gw, a - start, stop - start
            )
            m_parts.append((m_part, a))
            d_parts.append((d_part, a))
        grad = lax.psum_scatter(gw, "dp", scatter_dimension=0, tiled=False, axis_index_groups=groups)
        expert_grads.append((start, grad))

    def both_cores(own, other):
        both = [
            own[k * rows : (k + 1) * rows].astype(f32) + other[k * rows : (k + 1) * rows].astype(f32)
            for k in range(nt)
        ]
        return both[0], [part.astype(bf16) for part in both[1:]]

    def to_tokens(parts, last=()):
        if nt != 4:
            return [swap_t(parts[k], k) for k in range(1, nt)], parts[nt - 1]
        mid = parts[3].shape[0] // 2
        by_x, by_y = swap_t(parts[3][:mid], 1), swap_t(parts[3][mid:], 2)
        x_first, y_last = swap_t(parts[1][:mid], 1), swap_t(parts[2][mid:], 2)
        by_x, by_y, *_ = lax.optimization_barrier((by_x, by_y, *last))
        x_part = (parts[1][mid:].astype(f32) + by_y.astype(f32)).astype(bf16)
        y_part = (parts[2][:mid].astype(f32) + by_x.astype(f32)).astype(bf16)
        return [x_first, swap_t(x_part, 1), swap_t(y_part, 2), y_last], y_part

    def collect(total, received):
        if nt != 4:
            for part in received:
                total = total + part.astype(f32)
            return total
        x_first, x_last, y_first, y_last = (part.astype(f32) for part in received)
        return total + jnp.concatenate([x_first + y_first, x_last + y_last], axis=0)

    (d_other,) = scatter(offs, pos_columns, d_parts, (1,))
    (d_own,) = scatter(offs, pos_columns, d_parts, (0,))
    d_own, d_sent = both_cores(d_own, swap_core(d_other))
    d_received, d_last = to_tokens([None] + d_sent)
    dn2 = collect(d_own, d_received)
    m_pos = after(pos_columns, d_last)
    m_other, m_own = scatter(offs, m_pos, m_parts, (1, 0))
    m_other = jnp.concatenate([swap_core(m_other[k * rows : (k + 1) * rows]) for k in range(nt)])
    m_own, m_sent = both_cores(m_own, m_other)

    grad = cotangent.astype(f32)
    inverse = rms_scale(s1)
    unit = s1 * inverse
    gain_two = jnp.sum(dn2 * unit, axis=0)
    scaled = dn2 * gains[1]
    gs1 = grad + inverse * (scaled - unit * jnp.mean(scaled * unit, axis=-1, keepdims=True))

    da, *m_sent = lax.optimization_barrier((gs1.astype(bf16), *m_sent))
    m_received = [swap_t(part, k + 1) for k, part in enumerate(m_sent)]
    if sharers > 1:
        da = lax.all_gather(da, "tensor", axis=0, tiled=True, axis_index_groups=seq_groups)
    dn1, grads_own, grads_other = attend_backward(
        (nz, nt), place, sequence, da, gains, gain_two[None] * sharers, q, kv, o, lse, qkv_weights, out_weight
    )
    block_out = m_own + s1
    for part in m_received:
        block_out = block_out + part.astype(f32)
    if sharers > 1:
        dn1 = lax.dynamic_slice_in_dim(dn1, first_row, rows, 0)

    stream = tokens.astype(f32)
    inverse = rms_scale(stream)
    unit = stream * inverse
    scaled = dn1 * gains[0]
    input_grad = gs1 + inverse * (scaled - unit * jnp.mean(scaled * unit, axis=-1, keepdims=True))

    grads_other = after(grads_other, *m_received)
    both = (grads_own.astype(f32) + swap_core(grads_other).astype(f32)).astype(bf16)
    received, _ = to_tokens([both[k] for k in range(nt)])

    states = [expert_in, expert_in_first, expert_in_second, expert_down, expert_down_first, expert_down_second]
    experts_new = None
    for start, got in expert_grads[:-1]:
        experts_new = adam_experts(place, start, got, swap_core(got[1]), states, experts_new)
    block_out, experts_new, received = lax.optimization_barrier((block_out, experts_new, received))

    total = collect(both[0].astype(f32), received)
    owned = total[0]
    sent = [total[j].astype(bf16) for j in range(1, nz)]
    received = [swap_z(part, j + 1) for j, part in enumerate(sent)]
    for start, got in expert_grads[-1:]:
        got = after(got, *sent, *experts_new)
        experts_new = adam_experts(place, start, got, swap_core(got[1]), states, experts_new)
    received, experts_new = lax.optimization_barrier((received, experts_new))
    for part in received:
        owned = owned + part.astype(f32)
    owned = owned * (1.0 / sharers)
    query_grad, keyval_grad, out_grad = (owned[i * wrows : (i + 1) * wrows] for i in range(3))
    gg = owned[3 * wrows : 3 * wrows + 2 * nt].reshape(1, 2, D)
    gg = lax.dynamic_slice_in_dim(gg, (place_dp * nt + t) * width, width, 2)

    gains_new = adam_change(norm_gains_first, norm_gains_second, gg)
    query_new = adam_update(query_weight, query_first, query_second, query_grad[None], WEIGHT_DECAY)
    keyval_new = adam_update(keyval_weight, keyval_first, keyval_second, keyval_grad[None], WEIGHT_DECAY)
    output_new = adam_update(output_weight, output_first, output_second, out_grad.T[None], WEIGHT_DECAY)
    return (block_out, input_grad) + gains_new + query_new + keyval_new + output_new + tuple(experts_new)


def solution(mesh):
    rows = P(("dp", "tensor"), None)
    by_rows = P(None, "dp", None)
    gains = P(None, None, ("dp", "tensor"))
    proj = P(None, "dp", "tensor")
    out_proj = P(None, "tensor", "dp")
    expert = P(None, "tensor", "dp", None)
    params = (gains,) * 3 + (proj,) * 6 + (out_proj,) * 3 + (expert,) * 6
    return jax.shard_map(
        functools.partial(on_device, mesh.shape["dp"], mesh.shape["tensor"]),
        mesh=mesh,
        in_specs=(rows, rows, by_rows, by_rows) + params,
        out_specs=(rows, rows) + params,
        check_vma=False,
    )
```

```python
import functools
import math

import jax
import jax.numpy as jnp
import numpy as np
from jax import lax
from jax.experimental import pallas as pl
from jax.experimental.pallas import tpu as pltpu
from jax.sharding import PartitionSpec as P

D = 1024
HD = 64
FFE = 512
SEQ_LEN = 512
STEP = 10
CALLS = (((0, 2),), ((2, 3), (3, 4)))
GATHERS = ((0, 3), (3, 4))
QBLK = 256
SUB = 256
CHUNK = 256
SLOTS = 2560
DEEP = 8
PAIR = 2
HELD = 3072

NORM_EPS = 1e-05
ROPE_BASE = 10000.0
BETA_ONE = 0.9
BETA_TWO = 0.95
ADAM_EPS = 1e-08
LEARN_RATE = 0.1
WEIGHT_DECAY = 0.1
MASK_FILL = -1e30
SCALE = 1.0 / math.sqrt(HD)

bf16 = jnp.bfloat16
f32 = jnp.float32
ANY = pl.BlockSpec(memory_space=pl.ANY)
COST = pl.CostEstimate(flops=1, bytes_accessed=1, transcendentals=0)
HBM = pl.BlockSpec(memory_space=pltpu.HBM)
SMEM = pl.BlockSpec(memory_space=pltpu.SMEM)
VMEM = pl.BlockSpec(memory_space=pltpu.VMEM)


def dot(a, b):
    return jnp.dot(a, b, preferred_element_type=f32)


def dot_t(a, b):
    return lax.dot_general(a, b, (((1,), (1,)), ((), ())), preferred_element_type=f32)


def t_dot(a, b):
    return lax.dot_general(a, b, (((0,), (0,)), ((), ())), preferred_element_type=f32)


def rope_tables():
    half = HD // 2
    position = np.arange(SEQ_LEN, dtype=np.float32)
    exponent = np.arange(half, dtype=np.float32) * np.float32(-2.0 / HD)
    frequency = np.exp(exponent * np.float32(math.log(ROPE_BASE))).astype(np.float32)
    angle = (position[:, None] * frequency[None, :]).astype(np.float32)
    cosine = np.cos(angle).astype(np.float32)
    sine = np.sin(angle).astype(np.float32)
    return np.tile(cosine, (1, 4)), np.concatenate([-sine, sine, -sine, sine], axis=1)


def adam_update(master, first_moment, second_moment, gradient, decay_rate):
    first_new = BETA_ONE * first_moment + (1.0 - BETA_ONE) * gradient
    second_new = BETA_TWO * second_moment + (1.0 - BETA_TWO) * gradient * gradient
    first_fixed = first_new / (1.0 - BETA_ONE**STEP)
    second_fixed = second_new / (1.0 - BETA_TWO**STEP)
    master_new = master - LEARN_RATE * (
        first_fixed / (jnp.sqrt(second_fixed) + ADAM_EPS) + decay_rate * master
    )
    return (master_new, first_new, second_new)


def adam_change(first_moment, second_moment, gradient):
    first_new = BETA_ONE * first_moment + (1.0 - BETA_ONE) * gradient
    second_new = BETA_TWO * second_moment + (1.0 - BETA_TWO) * gradient * gradient
    first_fixed = first_new / (1.0 - BETA_ONE**STEP)
    second_fixed = second_new / (1.0 - BETA_TWO**STEP)
    change = -LEARN_RATE * (first_fixed / (jnp.sqrt(second_fixed) + ADAM_EPS))
    return (change, first_new, second_new)


def sum_received(received, nt):
    received = [part.astype(f32) for part in received]
    if nt != 4:
        return functools.reduce(jnp.add, received)
    x_first, x_last, y_first, y_last = received
    return jnp.concatenate([x_first + y_first, x_last + y_last], axis=0)


def rms_scale(values):
    return lax.rsqrt(jnp.mean(values * values, axis=-1, keepdims=True) + NORM_EPS)


def weight_spots(place_ref, nz, nt, relative):
    rows, cols = D // (2 * nz), D // nt
    z, core, t = place_ref[0], place_ref[1], place_ref[2]
    for c in range(2):
        for k in range(nt):
            for j in range(nz):
                row = pl.multiple_of(((z ^ j if relative else j) * 2 + (core ^ c)) * rows, rows)
                col = pl.multiple_of((t ^ k) * cols, cols)
                yield c, k, j, (pl.ds(row, rows), pl.ds(col, cols))


def gather_copies(place_ref, pieces, first, w_ref, sem, nz, nt):
    rows = D // (2 * nz)
    return [
        pltpu.make_async_copy(
            pieces[c * nt + k].at[j, (first + member) * rows : (first + member + 1) * rows, :],
            w_ref.at[(member,) + spot],
            sem.at[((c * nt + k) * nz + j) * w_ref.shape[0] + member],
        )
        for c, k, j, spot in weight_spots(place_ref, nz, nt, False)
        for member in range(w_ref.shape[0])
    ]


def rotate(x, cosine, sine, first_half):
    width = x.shape[-1]
    swapped = jnp.where(
        first_half, pltpu.roll(x, width - HD // 2, 1), pltpu.roll(x, HD // 2, 1)
    )
    return x * cosine + swapped * sine


def join_gains(parts, width):
    owners = parts.shape[0]
    both = jnp.sum(parts[:, :, :128].astype(f32), axis=1)
    lane = lax.broadcasted_iota(jnp.int32, (owners, 128), 1)
    owner = lax.broadcasted_iota(jnp.int32, (owners, D), 0)
    mine = lax.broadcasted_iota(jnp.int32, (owners, D), 1) // width == owner
    out = []
    for values in (both, pltpu.roll(both, 128 - width, 1)):
        values = jnp.where(lane < width, values, 0.0)
        shift = width
        while shift < 128:
            values = values + pltpu.roll(values, shift, 1)
            shift *= 2
        wide = jnp.concatenate([values] * (D // 128), axis=1)
        out.append(jnp.sum(jnp.where(mine, wide, 0.0), axis=0, keepdims=True))
    return jnp.concatenate(out, axis=0)


def attend_forward_kernel(nz, nt, place_ref, tokens_ref, cos_ref, sin_ref, *rest):
    pieces = rest[: 2 * nt]
    q_ref, kv_ref, o_ref, lse_ref, w_ref, gains_ref = rest[2 * nt : 2 * nt + 6]
    qlin_ref, kvlin_ref, parts_ref, sems, gain_sems = rest[2 * nt + 6 :]
    length = tokens_ref.shape[0]
    rows = D // (2 * nz)
    core, t = place_ref[1], place_ref[2]
    gain_copies = [
        pltpu.make_async_copy(
            pieces[c * nt + k].at[j, 2 * rows :, :],
            parts_ref.at[(j * 2 + (core ^ c)) * nt + (t ^ k)],
            gain_sems.at[(c * nt + k) * nz + j],
        )
        for c in range(2)
        for k in range(nt)
        for j in range(nz)
    ]
    for copy in gain_copies:
        copy.start()
    copies = gather_copies(place_ref, pieces, 0, w_ref, sems, nz, nt)
    for copy in copies:
        copy.start()
    lse_ref[...] = jnp.zeros_like(lse_ref)
    for copy in gain_copies:
        copy.wait()
    gains_ref[...] = join_gains(parts_ref[...], D // (2 * nz * nt))
    stream = tokens_ref[...].astype(f32)
    n1 = (stream * rms_scale(stream) * gains_ref[0:1, :]).astype(bf16)
    for copy in copies:
        copy.wait()
    qlin_ref[...] = dot(n1, w_ref[0])
    kvlin_ref[...] = dot(n1, w_ref[1])

    def group(g, carry):
        part = pl.ds(pl.multiple_of(g * 128, 128), 128)
        lane = lax.broadcasted_iota(jnp.int32, (length, 128), 1)
        low = lane < HD
        first_half = (lane & (HD // 2)) == 0
        cosine, sine = cos_ref[...], sin_ref[...]
        q = rotate(qlin_ref[:, part], cosine, sine, first_half)
        kv = kvlin_ref[:, part]
        kv = jnp.where(low, rotate(kv, cosine, sine, first_half), kv)
        q_ref[:, part] = q.astype(bf16)
        kv_ref[:, part] = kv.astype(bf16)
        vk = pltpu.roll(kv, HD, 1).astype(bf16)
        kv = kv.astype(bf16)
        heads = (
            (jnp.where(low, q * SCALE, 0.0).astype(bf16), kv, vk),
            (jnp.where(low, 0.0, q * SCALE).astype(bf16), vk, kv),
        )
        row = lax.broadcasted_iota(jnp.int32, (QBLK, QBLK), 0)
        column = lax.broadcasted_iota(jnp.int32, (QBLK, QBLK), 1)
        seen = column <= row
        for b in range(length // QBLK):
            rows = slice(b * QBLK, (b + 1) * QBLK)
            keys = (b + 1) * QBLK
            outs = []
            lses = lse_ref[rows, :]
            lane_b = lax.broadcasted_iota(jnp.int32, (QBLK, 128), 1)
            for h, (qh, key_side, value_side) in enumerate(heads):
                scores = jnp.where(seen, dot_t(qh[rows], key_side[rows]), MASK_FILL)
                if b > 0:
                    scores = jnp.concatenate([dot_t(qh[rows], key_side[: b * QBLK]), scores], axis=1)
                top = jnp.max(scores, axis=-1, keepdims=True)
                e = jnp.exp(scores - top)
                total = jnp.sum(e, axis=-1, keepdims=True)
                outs.append(dot(e.astype(bf16), value_side[:keys]) * (1.0 / total))
                lses = jnp.where(lane_b == 2 * g + h, top + jnp.log(total), lses)
            lse_ref[rows, :] = lses
            o_ref[rows, part] = jnp.where(lane_b < HD, outs[0], outs[1]).astype(bf16)
        return carry

    lax.fori_loop(0, D // 128, group, 0)


def attend_forward(mesh_sizes, place, tokens, pieces):
    nz, nt = mesh_sizes
    length = tokens.shape[0]
    cosine, sine = rope_tables()
    return pl.pallas_call(
        functools.partial(attend_forward_kernel, nz, nt),
        out_shape=(
            jax.ShapeDtypeStruct((length, D), bf16),
            jax.ShapeDtypeStruct((length, D), bf16),
            jax.ShapeDtypeStruct((length, D), bf16),
            jax.ShapeDtypeStruct((length, 128), f32),
            jax.ShapeDtypeStruct((2, D, D), bf16),
            jax.ShapeDtypeStruct((2, D), f32),
        ),
        in_specs=[SMEM] + [VMEM] * 3 + [ANY] * len(pieces),
        out_specs=[VMEM] * 6,
        scratch_shapes=[
            pltpu.VMEM((length, D), f32),
            pltpu.VMEM((length, D), f32),
            pltpu.VMEM((2 * nz * nt, 16, D // nt), bf16),
            pltpu.SemaphoreType.DMA((2 * nt * nz * 2,)),
            pltpu.SemaphoreType.DMA((2 * nt * nz,)),
        ],
        compiler_params=pltpu.CompilerParams(vmem_limit_bytes=40 * 2**20),
        cost_estimate=pl.CostEstimate(flops=25 * 10**9, bytes_accessed=12 * 2**20, transcendentals=4 * 2**20),
        name="attend_forward",
    )(place, tokens, jnp.asarray(cosine), jnp.asarray(sine), *pieces)


def attend_out_kernel(nz, nt, place_ref, tokens_ref, gains_ref, o_ref, *rest):
    pieces = rest[: 2 * nt]
    s1_ref, n2_ref, w_ref, sems = rest[2 * nt :]
    copies = gather_copies(place_ref, pieces, 0, w_ref, sems, nz, nt)
    for copy in copies:
        copy.start()
    for copy in copies:
        copy.wait()
    s1 = tokens_ref[...].astype(f32) + dot_t(o_ref[...], w_ref[0])
    s1_ref[...] = s1
    n2_ref[...] = (s1 * rms_scale(s1) * gains_ref[1:2, :]).astype(bf16)


def attend_out(mesh_sizes, place, tokens, gains, o, pieces):
    nz, nt = mesh_sizes
    length = tokens.shape[0]
    return pl.pallas_call(
        functools.partial(attend_out_kernel, nz, nt),
        out_shape=(
            jax.ShapeDtypeStruct((length, D), f32),
            jax.ShapeDtypeStruct((length, D), bf16),
            jax.ShapeDtypeStruct((1, D, D), bf16),
        ),
        in_specs=[SMEM] + [VMEM] * 3 + [ANY] * len(pieces),
        out_specs=[VMEM] * 3,
        scratch_shapes=[pltpu.SemaphoreType.DMA((2 * nt * nz,))],
        compiler_params=pltpu.CompilerParams(vmem_limit_bytes=32 * 2**20),
        cost_estimate=COST,
        name="attend_out",
    )(place, tokens, gains, o, *pieces)


def norm_backward(grad, stream, gain, given):
    inverse = rms_scale(stream)
    unit = stream * inverse
    scaled = grad * gain
    through = inverse * (scaled - unit * jnp.mean(scaled * unit, axis=-1, keepdims=True))
    return given + through, jnp.sum(grad * unit, axis=0, keepdims=True)


def attend_backward_kernel(nz, nt, whole, place_ref, tokens_ref, gains_ref, cos_ref, sin_ref, q_ref, kv_ref, o_ref, *rest):
    lse_ref, w_ref, wo_ref, rest = rest[0], rest[1], rest[2], rest[3:]
    da_ref, gain_two_ref, rest = rest[0], rest[1], rest[2:]
    if whole:
        gs1_ref, rest = rest[0], rest[1:]
    out_ref, own_ref, others, rest = rest[0], rest[1], rest[2 : 2 + nt], rest[2 + nt :]
    gw_ref, gg_ref, do_ref, dq_ref, dkv_ref, lse_t_ref, sems = rest
    length = tokens_ref.shape[0]
    rows, cols = D // (2 * nz), D // nt
    sides = ([own_ref.at[k] for k in range(nt)], others)
    da, gain_two = da_ref[...], gain_two_ref[...]

    def member_copies(members):
        return [
            pltpu.make_async_copy(
                gw_ref.at[(member,) + spot],
                sides[c][k].at[j, member * rows : (member + 1) * rows, :],
                sems.at[member, (c * nt + k) * nz + j],
            )
            for member in members
            for c, k, j, spot in weight_spots(place_ref, nz, nt, True)
        ]

    gw_ref[2] = t_dot(da, o_ref[...]).astype(bf16)
    first = member_copies((2,))
    for copy in first:
        copy.start()
    do_ref[...] = dot(da, wo_ref[0]).astype(bf16)
    lse_t_ref[...] = lse_ref[...].T

    def group(g, carry):
        part = pl.ds(pl.multiple_of(g * 128, 128), 128)
        lane = lax.broadcasted_iota(jnp.int32, (length, 128), 1)
        low = lane < HD
        first_half = (lane & (HD // 2)) == 0
        cosine, sine = cos_ref[...], sin_ref[...]
        q = q_ref[:, part].astype(f32)
        kv = kv_ref[:, part].astype(f32)
        do = do_ref[:, part].astype(f32)
        vk = pltpu.roll(kv, HD, 1).astype(bf16)
        kv = kv.astype(bf16)
        q_low = jnp.where(low, q, 0.0).astype(bf16)
        scaled_low = jnp.where(low, q * SCALE, 0.0).astype(bf16)
        scaled_high = jnp.where(low, 0.0, q * SCALE).astype(bf16)
        q_moved = jnp.where(low, pltpu.roll(q, HD, 1), 0.0).astype(bf16)
        do_low = jnp.where(low, do, 0.0).astype(bf16)
        do_high = jnp.where(low, 0.0, do).astype(bf16)
        do_moved = jnp.where(low, 0.0, pltpu.roll(do, HD, 1)).astype(bf16)
        heads = (
            (scaled_low, kv, vk, do_low, q_low, do_moved),
            (scaled_high, vk, kv, do_high, q_moved, do_high),
        )
        row = lax.broadcasted_iota(jnp.int32, (QBLK, QBLK), 0)
        column = lax.broadcasted_iota(jnp.int32, (QBLK, QBLK), 1)
        seen = row <= column
        blocks = length // QBLK
        dkv = [jnp.zeros((QBLK, 128), f32) for _ in range(blocks)]
        dqs = []
        for b in range(blocks):
            rows = slice(b * QBLK, (b + 1) * QBLK)
            keys = (b + 1) * QBLK
            both = []
            for h, (qh, key_side, value_side, doh, q_for_k, do_for_v) in enumerate(heads):
                scores = jnp.where(seen, dot_t(key_side[rows], qh[rows]), MASK_FILL)
                if b > 0:
                    scores = jnp.concatenate([dot_t(key_side[: b * QBLK], qh[rows]), scores], axis=0)
                e = jnp.exp(scores - lse_t_ref[pl.ds(2 * g + h, 1), rows])
                dp = dot_t(value_side[:keys], doh[rows])
                mean = jnp.sum(e * dp, axis=0, keepdims=True)
                dz = (e * (dp - mean)).astype(bf16)
                both.append(t_dot(dz, key_side[:keys]))
                add = dot(dz, q_for_k[rows]) + dot(e.astype(bf16), do_for_v[rows])
                for i in range(b + 1):
                    dkv[i] = dkv[i] + add[i * QBLK : (i + 1) * QBLK]
            lane_b = lax.broadcasted_iota(jnp.int32, (QBLK, 128), 1)
            dqs.append(jnp.where(lane_b < HD, both[0], both[1]))
        dq = jnp.concatenate(dqs, axis=0) * SCALE
        dkv_all = jnp.concatenate(dkv, axis=0)
        dq_ref[:, part] = rotate(dq, cosine, -sine, first_half).astype(bf16)
        dk = rotate(dkv_all * SCALE, cosine, -sine, first_half)
        dkv_ref[:, part] = jnp.where(low, dk, dkv_all).astype(bf16)
        return carry

    lax.fori_loop(0, D // 128, group, 0)
    stream = tokens_ref[...].astype(f32)
    n1 = (stream * rms_scale(stream) * gains_ref[0:1, :]).astype(bf16)
    gw_ref[0] = t_dot(n1, dq_ref[...]).astype(bf16)
    gw_ref[1] = t_dot(n1, dkv_ref[...]).astype(bf16)
    second = member_copies((0, 1))
    for copy in second:
        copy.start()
    dn1 = dot_t(dq_ref[...], w_ref[0]) + dot_t(dkv_ref[...], w_ref[1])
    input_grad, gain_one = norm_backward(dn1, stream, gains_ref[0:1, :], gs1_ref[...] if whole else 0.0)
    out_ref[...] = input_grad if whole else dn1
    gg_ref[...] = jnp.zeros_like(gg_ref)
    for i in range(nt):
        gg_ref[i : i + 1, :] = gain_one[:, i * cols : (i + 1) * cols].astype(bf16)
        gg_ref[nt + i : nt + i + 1, :] = gain_two[:, i * cols : (i + 1) * cols].astype(bf16)
    third = [
        pltpu.make_async_copy(gg_ref, sides[c][k].at[j, 3 * rows :, :], sems.at[3, (c * nt + k) * nz + j])
        for c in range(2)
        for k in range(nt)
        for j in range(nz)
    ]
    for copy in third:
        copy.start()
    for copy in first + second + third:
        copy.wait()


def attend_backward(mesh_sizes, whole, place, tokens, gains, q, kv, o, lse, weights, out_weight, *given):
    nz, nt = mesh_sizes
    length = tokens.shape[0]
    cosine, sine = rope_tables()
    part = (nz, 3 * D // (2 * nz) + 16, D // nt)
    out = pl.pallas_call(
        functools.partial(attend_backward_kernel, nz, nt, whole),
        out_shape=[jax.ShapeDtypeStruct((length, D), f32), jax.ShapeDtypeStruct((nt,) + part, bf16)]
        + [jax.ShapeDtypeStruct(part, bf16)] * nt,
        in_specs=[SMEM] + [VMEM] * (10 + len(given)),
        out_specs=[VMEM] + [ANY] * (1 + nt),
        scratch_shapes=[
            pltpu.VMEM((3, D, D), bf16),
            pltpu.VMEM((16, D // nt), bf16),
            pltpu.VMEM((length, D), bf16),
            pltpu.VMEM((length, D), bf16),
            pltpu.VMEM((length, D), bf16),
            pltpu.VMEM((128, length), f32),
            pltpu.SemaphoreType.DMA((4, 2 * nt * nz)),
        ],
        compiler_params=pltpu.CompilerParams(vmem_limit_bytes=60 * 2**20),
        cost_estimate=COST,
        name="attend_backward",
    )(
        place, tokens, gains, jnp.asarray(cosine), jnp.asarray(sine), q, kv, o, lse, weights, out_weight, *given
    )
    return out[0], out[1], out[2:]


def gather_kernel(starts, experts, with_c, offs_ref, pos_ref, *rest):
    tiles = len(starts) - 1
    if with_c:
        c_ref, rest = rest[0], rest[1:]
    parts, rest = rest[:tiles], rest[tiles:]
    outs, rest = rest[: 1 + with_c], rest[1 + with_c :]
    held, (buf, in_sems, out_sems) = rest[: 1 + with_c], rest[1 + with_c :]
    subs = starts[-1] // SUB

    def block_copy(s):
        j = max(i for i in range(tiles) if starts[i] <= s * SUB)
        return pltpu.make_async_copy(
            parts[j].at[pl.ds(s * SUB - starts[j], SUB)], buf.at[s % DEEP], in_sems.at[s % DEEP]
        )

    def flush(e, chunk):
        spot = pl.ds(pl.multiple_of(chunk * CHUNK, CHUNK), CHUNK)
        return [
            pltpu.make_async_copy(slots.at[e, spot, :], out.at[e, spot, :], out_sems.at[i, e, chunk])
            for i, (slots, out) in enumerate(zip(held, outs))
        ]

    for s in range(DEEP - 1):
        block_copy(s).start()

    def block(s, carry):
        for ahead in range(DEEP - 1, subs):

            @pl.when(s + DEEP - 1 == ahead)
            def _():
                block_copy(ahead).start()

        slot = lax.rem(s, DEEP)
        begin = [offs_ref[e * (subs + 1) + s] for e in range(experts)]
        end = [offs_ref[e * (subs + 1) + s + 1] for e in range(experts)]
        most = functools.reduce(jnp.maximum, [end[e] - begin[e] for e in range(experts)])
        pltpu.make_async_copy(parts[0].at[pl.ds(0, SUB)], buf.at[slot], in_sems.at[slot]).wait()

        def fill(count):
            slots = lax.broadcasted_iota(jnp.int32, (count, SUB), 0).astype(f32)
            spots = [pl.ds(pl.multiple_of(begin[e], 16), count) for e in range(experts)]
            picks = []
            for e in range(experts):
                hit = slots == pos_ref[pl.ds(e * subs + s, 1), :]
                picks.append(jnp.where(hit, 1.0, 0.0).astype(bf16))
                if with_c:
                    c = jnp.sum(jnp.where(hit, c_ref[pl.ds(e * subs + s, 1), :], 0.0), axis=1, keepdims=True)
                    held[1][e, spots[e], :] = jnp.broadcast_to(c, (count, 128))
            rows = dot(jnp.concatenate(picks, axis=0), buf[slot]).astype(bf16)
            for e in range(experts):
                held[0][e, spots[e], :] = rows[e * count : (e + 1) * count]

        @pl.when(most <= SUB // 2)
        def _():
            fill(SUB // 2)

        @pl.when(most > SUB // 2)
        def _():
            fill(SUB)

        for e in range(experts):

            @pl.when(end[e] // CHUNK > begin[e] // CHUNK)
            def _():
                for copy in flush(e, begin[e] // CHUNK):
                    copy.start()

        return carry

    lax.fori_loop(0, subs, block, 0)
    for e in range(experts):
        total = offs_ref[e * (subs + 1) + subs]
        tail = pl.ds(pl.multiple_of(total, 16), CHUNK)
        for slots in held:
            slots[e, tail, :] = jnp.zeros((CHUNK, slots.shape[2]), slots.dtype)
        for copy in flush(e, total // CHUNK):
            copy.start()
    for e in range(experts):

        def drain(chunk, carry):
            for copy in flush(e, chunk):
                copy.wait()
            return carry

        lax.fori_loop(0, offs_ref[e * (subs + 1) + subs] // CHUNK + 1, drain, 0)


def gather(parts, offs, pos, c=None):
    starts = [0]
    for part in parts:
        starts.append(starts[-1] + part.shape[0])
    experts = pos.shape[0] * SUB // starts[-1]
    with_c = c is not None
    held = [((experts, SLOTS, D), bf16)] + [((experts, SLOTS, 128), f32)] * with_c
    return pl.pallas_call(
        functools.partial(gather_kernel, tuple(starts), experts, with_c),
        out_shape=[jax.ShapeDtypeStruct(*kind) for kind in held],
        in_specs=[SMEM, VMEM] + [VMEM] * with_c + [HBM] * len(parts),
        out_specs=[HBM] * len(held),
        scratch_shapes=[pltpu.VMEM(*kind) for kind in held]
        + [
            pltpu.VMEM((DEEP, SUB, D), bf16),
            pltpu.SemaphoreType.DMA((DEEP,)),
            pltpu.SemaphoreType.DMA((1 + with_c, experts, SLOTS // CHUNK)),
        ],
        compiler_params=pltpu.CompilerParams(vmem_limit_bytes=62 * 2**20),
        cost_estimate=COST,
        name="gather_rows",
    )(offs, pos, *([c] if with_c else []), *parts)


def experts_kernel(first, subs, sources, kept, place_ref, offs_ref, n2_ref, dm_ref, c_ref, *rest):
    arrays = 1 + sources[-1][0]
    weights, rest = rest[:arrays], rest[arrays + kept :]
    m_ref, d_ref, gw_ref = rest[:3]
    win_buf, wdown_buf, n2_in, dm_in, c_in, m_out, d_out, zeros, gin, gdown, w_sems, in_sems, out_sems = rest[3:]
    e = pl.program_id(0)
    nz, cores, _, wrows, _ = gw_ref.shape
    rin, rdown = D // (nz * cores), FFE // (nz * cores)
    core = place_ref[1]
    total = offs_ref[(first + e) * (subs + 1) + subs]
    chunks = jnp.maximum((total + CHUNK - 1) // CHUNK, 1)

    def weight_copies(index):
        i, place = sources[index]
        slot = index % 2
        return [
            pltpu.make_async_copy(
                weights[i].at[:, side, place, spot, :], buf.at[slot, :, core ^ side], w_sems.at[2 * side + j, slot]
            )
            for side in range(2)
            for j, (spot, buf) in enumerate(((slice(0, rin), win_buf), (slice(rin, wrows), wdown_buf)))
        ]

    def in_copies(e, k, slot):
        spot = pl.ds(pl.multiple_of(k * CHUNK, CHUNK), CHUNK)
        return [
            pltpu.make_async_copy(source.at[first + e, spot, :], target.at[slot], in_sems.at[i, slot])
            for i, (source, target) in enumerate(((n2_ref, n2_in), (dm_ref, dm_in), (c_ref, c_in)))
        ]

    def out_copies(k, slot):
        spot = pl.ds(pl.multiple_of(k * CHUNK, CHUNK), CHUNK)
        return (
            pltpu.make_async_copy(m_out.at[slot], m_ref.at[e, spot, :], out_sems.at[0, slot]),
            pltpu.make_async_copy(d_out.at[slot], d_ref.at[e, spot, :], out_sems.at[1, slot]),
        )

    @pl.when(e == 0)
    def _():
        for copy in in_copies(e, 0, 0) + weight_copies(0):
            copy.start()
        zeros[...] = jnp.zeros_like(zeros)

    for index in range(len(sources)):

        @pl.when(e == index)
        def _():
            for copy in weight_copies(index):
                copy.wait()
            if index + 1 < len(sources):
                for copy in weight_copies(index + 1):
                    copy.start()

    at = lax.rem(e, 2)

    def one_chunk(k, carry):
        slot = lax.rem(k, 2)
        for copy in in_copies(e, k, slot):
            copy.wait()

        @pl.when(k + 1 < chunks)
        def _():
            for copy in in_copies(e, k + 1, 1 - slot):
                copy.start()

        @pl.when(k >= 2)
        def _():
            for copy in out_copies(k - 2, slot):
                copy.wait()

        win = win_buf[at].reshape(D, D)
        wdown = wdown_buf[at].reshape(FFE, D)
        n2, dm, c = n2_in[slot], dm_in[slot], c_in[slot][:, 0:1]
        hidden = dot(n2, win)
        gate, up = hidden[:, :FFE], hidden[:, FFE:]
        sigma = jax.nn.sigmoid(gate)
        silu = gate * sigma
        active = (c * silu * up).astype(bf16)
        m_out[slot] = dot(active, wdown).astype(bf16)
        gdown[...] = jnp.where(k == 0, 0.0, gdown[...]) + dot(active.T, dm)
        da = c * dot_t(dm, wdown)
        dgate = da * up * (sigma + silu * (1.0 - sigma))
        dup = da * silu
        dh = jnp.concatenate([dgate.astype(bf16), dup.astype(bf16)], axis=1)
        gin[...] = jnp.where(k == 0, 0.0, gin[...]) + dot(n2.T, dh)
        d_out[slot] = dot_t(dh, win).astype(bf16)
        for copy in out_copies(k, slot):
            copy.start()
        return carry

    lax.fori_loop(0, chunks, one_chunk, 0)

    @pl.when(e + 1 < len(sources))
    def _():
        for copy in in_copies(e + 1, 0, 0):
            copy.start()

    spot = pl.ds(pl.multiple_of(chunks * CHUNK, CHUNK), CHUNK)
    ends = (
        pltpu.make_async_copy(zeros, m_ref.at[e, spot, :], out_sems.at[0, 2]),
        pltpu.make_async_copy(zeros, d_ref.at[e, spot, :], out_sems.at[1, 2]),
    )
    for copy in ends:
        copy.start()
    for j in range(nz):
        for side in range(2):
            owner = 2 * j + (core ^ side)
            at_in, at_down = pl.multiple_of(owner * rin, rin), pl.multiple_of(owner * rdown, rdown)
            gw_ref[j, side, 0, :rin, :] = gin[pl.ds(at_in, rin), :].astype(bf16)
            gw_ref[j, side, 0, rin:, :] = gdown[pl.ds(at_down, rdown), :].astype(bf16)
    for copy in ends:
        copy.wait()
    for back in (1, 2):

        @pl.when(chunks >= back)
        def _():
            for copy in out_copies(chunks - back, lax.rem(chunks - back, 2)):
                copy.wait()


def experts_step(place, slots, offs, first, weights, sources, before, spot, count):
    nz, cores, _, wrows, _ = weights[0].shape
    experts = len(sources)
    rin, rdown = D // (nz * cores), FFE // (nz * cores)
    part = jax.ShapeDtypeStruct((experts, HELD, D), bf16)
    kept = [] if before is None else [before]
    subs = offs.shape[1] - 1
    return pl.pallas_call(
        functools.partial(experts_kernel, first, subs, sources, len(kept)),
        grid=(experts,),
        out_shape=(part, part, jax.ShapeDtypeStruct((nz, cores, count, wrows, D), bf16)),
        in_specs=[SMEM, SMEM] + [HBM] * (3 + len(weights) + len(kept)),
        out_specs=(HBM, HBM, pl.BlockSpec((nz, cores, 1, wrows, D), lambda e: (0, 0, spot + e, 0, 0))),
        scratch_shapes=[
            pltpu.VMEM((2, nz, cores, rin, D), bf16),
            pltpu.VMEM((2, nz, cores, rdown, D), bf16),
            pltpu.VMEM((2, CHUNK, D), bf16),
            pltpu.VMEM((2, CHUNK, D), bf16),
            pltpu.VMEM((2, CHUNK, 128), f32),
            pltpu.VMEM((2, CHUNK, D), bf16),
            pltpu.VMEM((2, CHUNK, D), bf16),
            pltpu.VMEM((CHUNK, D), bf16),
            pltpu.VMEM((D, D), f32),
            pltpu.VMEM((FFE, D), f32),
            pltpu.SemaphoreType.DMA((4, 2)),
            pltpu.SemaphoreType.DMA((3, 2)),
            pltpu.SemaphoreType.DMA((2, 3)),
        ],
        input_output_aliases={5 + len(weights): 2} if kept else {},
        compiler_params=pltpu.CompilerParams(
            vmem_limit_bytes=60 * 2**20, dimension_semantics=("arbitrary",)
        ),
        cost_estimate=COST,
        name="experts",
    )(place, offs.reshape(-1), *slots, *weights, *kept)


def scatter_kernel(halves, sources, experts, subs, offs_ref, pos_ref, *rest):
    arrays = 1 + sources[-1][1]
    parts, rest = rest[:arrays], rest[arrays:]
    outs, (slots, sems) = rest[: len(halves)], rest[len(halves) :]
    i, steps = pl.program_id(0), subs // (2 * PAIR)
    first = lax.rem(i * PAIR + halves[0] * (subs // 2), subs)

    half = subs // 2

    def each(low, high, act):
        for spot, (e, array, index) in enumerate(sources):

            def one(chunk, carry):
                rows = pl.ds(pl.multiple_of(chunk * CHUNK, CHUNK), CHUNK)
                act(pltpu.make_async_copy(parts[array].at[index, rows, :], slots.at[spot, rows, :], sems.at[spot, chunk]))
                return carry

            lax.fori_loop(*spans(e, low, high), one, 0)

    def spans(e, low, high):
        middle = offs_ref[e * (subs + 1) + half] // CHUNK
        last_low = (offs_ref[e * (subs + 1) + low] + CHUNK - 1) // CHUNK + 1
        begin = jnp.where(lax.rem(low, half) == 0, offs_ref[e * (subs + 1) + low] // CHUNK, last_low)
        end = (offs_ref[e * (subs + 1) + high] + CHUNK - 1) // CHUNK + 1
        if len(halves) == 2:
            early = jnp.asarray(low) < half
            begin = jnp.where(early, jnp.minimum(begin, middle), begin)
            end = jnp.where(early, jnp.minimum(end, middle), end)
        return begin, end

    @pl.when(i == 0)
    def _():
        for h in halves:
            each(h * half, (h + 1) * half, lambda copy: copy.start())

    each(first, first + PAIR, lambda copy: copy.wait())
    lane = lax.broadcasted_iota(jnp.int32, (SUB, SUB), 1).astype(f32)
    totals = []
    for p in range(PAIR):
        picks = [
            jnp.where(lane == pos_ref[p * SUB : (p + 1) * SUB, e : e + 1], 1.0, 0.0).astype(bf16) for e, _, _ in sources
        ]
        windows = [
            slots[spot, pl.ds(pl.multiple_of(offs_ref[e * (subs + 1) + first + p], 16), SUB), :]
            for spot, (e, _, _) in enumerate(sources)
        ]
        totals.append(dot(jnp.concatenate(picks, axis=1), jnp.concatenate(windows, axis=0)).astype(bf16))
    for j, out_ref in enumerate(outs):

        @pl.when(i // steps == j)
        def _():
            for p in range(PAIR):
                out_ref[p * SUB : (p + 1) * SUB, :] = totals[p]


def scatter(offs, pos_columns, parts, halves):
    tokens, experts = pos_columns.shape
    sources = [
        (first + index, i, index) for i, (part, first) in enumerate(parts) for index in range(part.shape[0])
    ]
    subs = tokens // SUB
    steps = subs // (2 * PAIR)
    shift = halves[0] * steps
    blocks = [
        pl.BlockSpec((PAIR * SUB, D), lambda i, j=j: (jnp.clip(i - j * steps, 0, steps - 1), 0))
        for j in range(len(halves))
    ]
    return pl.pallas_call(
        functools.partial(scatter_kernel, halves, sources, experts, subs),
        grid=(len(halves) * steps,),
        out_shape=[jax.ShapeDtypeStruct((tokens // 2, D), bf16)] * len(halves),
        in_specs=[SMEM, pl.BlockSpec((PAIR * SUB, experts), lambda i: (lax.rem(i + shift, 2 * steps), 0))]
        + [HBM] * len(parts),
        out_specs=blocks,
        scratch_shapes=[
            pltpu.VMEM((len(sources), HELD, D), bf16),
            pltpu.SemaphoreType.DMA((len(sources), HELD // CHUNK)),
        ],
        compiler_params=pltpu.CompilerParams(
            vmem_limit_bytes=60 * 2**20, dimension_semantics=("arbitrary",)
        ),
        cost_estimate=COST,
        name="scatter_rows",
    )(offs.reshape(-1), pos_columns, *[part for part, _ in parts])


def adam_kernel(per, place_ref, mine_ref, recv_ref, *rest):
    states, news = rest[:6], rest[-6:]
    here = pl.program_id(0) // per == place_ref[1]
    grad = jnp.where(here, mine_ref[0, 0], recv_ref[0]).astype(f32)
    rin = states[0].shape[2]
    for i, part in ((0, grad[:rin]), (3, grad[rin:])):
        masters = [ref[0, 0] for ref in states[i : i + 3]]
        for ref, new in zip(news[i : i + 3], adam_update(*masters, part, WEIGHT_DECAY)):
            ref[0, 0] = new


def adam_experts(place, a, mine, recv, states, before):
    experts, rin = states[0].shape[1:3]
    rdown = states[3].shape[2]
    per = recv.shape[0]
    half = experts // 2
    spec = [
        pl.BlockSpec((1, 1, r, D), lambda i, place: (0, i // per * half + a + i % per, 0, 0))
        for r in (rin, rdown)
    ]
    specs = [spec[0]] * 3 + [spec[1]] * 3
    kept = [] if before is None else list(before)
    return pl.pallas_call(
        functools.partial(adam_kernel, per),
        grid_spec=pltpu.PrefetchScalarGridSpec(
            num_scalar_prefetch=1,
            grid=(2 * per,),
            in_specs=[
                pl.BlockSpec((1, 1, rin + rdown, D), lambda i, place: (0, i % per, 0, 0)),
                pl.BlockSpec((1, rin + rdown, D), lambda i, place: (i % per, 0, 0)),
            ]
            + specs
            + [HBM] * len(kept),
            out_specs=specs,
        ),
        out_shape=[jax.ShapeDtypeStruct(state.shape, f32) for state in states],
        input_output_aliases={9 + i: i for i in range(len(kept))},
        compiler_params=pltpu.CompilerParams(
            vmem_limit_bytes=60 * 2**20, dimension_semantics=("arbitrary",)
        ),
        cost_estimate=COST,
        name="adam_experts",
    )(place, mine, recv, *states, *kept)


def adam_rest_kernel(scale, place_ref, mine_ref, *rest):
    count = len(rest) - 25
    received, states, news, (grad_ref,) = rest[:count], rest[count : count + 12], rest[count + 12 : count + 24], rest[-1:]
    total = mine_ref[...]
    for part in received:
        total = total + part[...].astype(f32)
    grad_ref[...] = total * scale
    rows, cols = states[0].shape[1:]
    width = states[9].shape[2]
    for i, turned in ((0, False), (1, False), (2, True)):
        part = grad_ref[i * rows : (i + 1) * rows, :]
        refs = slice(3 * i, 3 * i + 3)
        masters = [ref[0] for ref in states[refs]]
        for ref, new in zip(news[refs], adam_update(*masters, part.T if turned else part, WEIGHT_DECAY)):
            ref[0] = new
    start = place_ref[3] * width
    for i in range(2):
        row = grad_ref[pl.ds(3 * rows + i * (D // cols) + start // cols, 1), :]
        part = pltpu.roll(row, lax.rem(cols - lax.rem(start, cols), cols), 1)[:, :width]
        moments = [ref[0, i : i + 1, :] for ref in states[9:11]]
        for ref, new in zip(news[9:], adam_change(*moments, part)):
            ref[0, i : i + 1, :] = new


def adam_rest(place, scale, mine, received, states):
    return pl.pallas_call(
        functools.partial(adam_rest_kernel, scale),
        out_shape=[jax.ShapeDtypeStruct(state.shape, f32) for state in states],
        in_specs=[SMEM] + [VMEM] * (1 + len(received) + len(states)),
        out_specs=[VMEM] * len(states),
        scratch_shapes=[pltpu.VMEM(mine.shape, f32)],
        compiler_params=pltpu.CompilerParams(vmem_limit_bytes=32 * 2**20),
        cost_estimate=COST,
        name="adam_rest",
    )(place, mine, *received, *states)


def on_device(
    ndp,
    nt,
    tokens,
    cotangent,
    routes,
    gate_weights,
    norm_gains,
    norm_gains_first,
    norm_gains_second,
    query_weight,
    query_first,
    query_second,
    keyval_weight,
    keyval_first,
    keyval_second,
    output_weight,
    output_first,
    output_second,
    expert_in,
    expert_in_first,
    expert_in_second,
    expert_down,
    expert_down_first,
    expert_down_second,
):
    nz = ndp // 2
    place_dp = lax.axis_index("dp")
    t = lax.axis_index("tensor")
    z, core = place_dp // 2, place_dp % 2
    place = jnp.stack([z, core, t, place_dp * nt + t]).astype(jnp.int32)
    rows = tokens.shape[0]
    sharers = max(1, SEQ_LEN // rows)

    def swap_core(x):
        return lax.ppermute(x, "dp", [(i, i ^ 1) for i in range(ndp)])

    def swap_z(x, j):
        return lax.ppermute(x, "dp", [(i, i ^ (2 * j)) for i in range(ndp)])

    def swap_t(x, k):
        return lax.ppermute(x, "tensor", [(i, i ^ k) for i in range(nt)])

    def spread_t(x):
        return [x] + [swap_t(x, k) for k in range(1, nt)]

    def spread_z(x):
        return [x] + [swap_z(x, j) for j in range(1, nz)]

    def after(x, *others):
        return lax.optimization_barrier((x,) + others)[0]

    def near(x):
        return [swap_t(x, k) for k in range(1, nt)] if nt != 4 else [swap_t(x, 1), swap_t(x, 2)]

    def far(x, others):
        mid = x.shape[0] // 2
        return [] if nt != 4 else [swap_t(others[0][:mid], 2), swap_t(others[1][mid:], 1)]

    width = norm_gains.shape[2]
    wrows, wcols = query_weight.shape[1:]
    high = lax.reduce_precision(norm_gains[0], 8, 7)
    middle = lax.reduce_precision(norm_gains[0] - high, 8, 7)
    gain_rows = jnp.stack([high, middle, norm_gains[0] - high - middle]).astype(bf16).reshape(3, 2 * width)
    own = jnp.concatenate(
        [
            query_weight[0].astype(bf16),
            keyval_weight[0].astype(bf16),
            jnp.pad(gain_rows, ((0, 13), (0, wcols - 2 * width))),
            output_weight[0].T.astype(bf16),
        ],
        axis=0,
    )
    half = expert_in.shape[1] // 2
    groups = [[2 * i + c for i in range(nz)] for c in range(2)]

    def cut(quarters):
        return quarters[0] * half // 4, quarters[1] * half // 4

    def shard(a, b, *ready):
        masters = lax.optimization_barrier((expert_in, expert_down, own, *ready))[:2]

        def low(side):
            return jnp.concatenate(
                [lax.dynamic_slice_in_dim(w[0], side * half + a, b - a, 0).astype(bf16) for w in masters], axis=1
            )

        return jnp.stack([low(core), swap_core(low(1 - core))])

    spans = [cut(quarters) for quarters in GATHERS]
    spans = [(a, b) for a, b in spans if a < b]
    shards = [shard(*spans[0])]
    for a, b in spans[1:]:
        shards.append(shard(a, b))
    column = lax.all_gather(own, "dp", axis=0, tiled=False, axis_index_groups=groups)
    held = {}
    for (a, b), part in zip(spans, shards):
        whole = lax.all_gather(part, "dp", axis=0, tiled=False, axis_index_groups=groups)
        held.update({i: (whole, i - a) for i in range(a, b)})
    dm_near = near(cotangent)
    dm_far = far(cotangent, dm_near)
    pieces = spread_t(after(column[:, : 2 * wrows + 16], *dm_near))
    pieces_out = spread_t(after(column[:, 2 * wrows + 16 :], *pieces[1:], *dm_far))
    pieces = pieces + [swap_core(piece) for piece in pieces]
    pieces_out = pieces_out + [swap_core(piece) for piece in pieces_out]

    ids = t * 2 * half + jnp.arange(2 * half, dtype=jnp.int32)
    chosen = routes[0].T[None, :, :] == ids[:, None, None]
    c_all = jnp.sum(jnp.where(chosen, gate_weights[0].T[None, :, :], 0.0), axis=1)
    c_mine = lax.dynamic_slice_in_dim(c_all, core * half, half, 0)
    c_got = swap_core(lax.dynamic_slice_in_dim(c_all, (1 - core) * half, half, 0))
    c_both = jnp.stack([c_mine, c_got], axis=1).reshape(half, 2, nt, rows)
    c_both = jnp.take(c_both, jnp.arange(nt, dtype=jnp.int32) ^ t, axis=2)
    subs = 2 * nt * rows // SUB
    c_rows = c_both.reshape(half * subs, SUB)
    taken = c_rows != 0.0
    upto = lax.broadcasted_iota(jnp.int32, (SUB, SUB), 0) <= lax.broadcasted_iota(jnp.int32, (SUB, SUB), 1)
    rank = dot(taken.astype(bf16), upto.astype(bf16))
    pos = jnp.where(taken, rank - 1.0, -1.0)
    sizes = (rank[:, SUB - 1].astype(jnp.int32).reshape(half, subs) + 15) // 16 * 16
    offs = jnp.pad(jnp.cumsum(sizes, axis=1), ((0, 0), (1, 0)))
    pos_columns = pos.reshape(half, subs * SUB).T

    sequence = after(tokens, offs, pos, c_rows, pos_columns)
    if sharers > 1:
        seq_groups = [list(range(i, i + sharers)) for i in range(0, nt, sharers)]
        sequence = lax.all_gather(tokens, "tensor", axis=0, tiled=True, axis_index_groups=seq_groups)
    first_row = (t % sharers) * rows
    q, kv, o, lse, qkv_weights, gains = attend_forward((nz, nt), place, sequence, pieces)
    s1, n2, out_weight = attend_out((nz, nt), place, sequence, gains, o, pieces_out)
    if sharers > 1:
        s1 = lax.dynamic_slice_in_dim(s1, first_row, rows, 0)
        n2 = lax.dynamic_slice_in_dim(n2, first_row, rows, 0)

    n2_near = near(n2)
    n2_far = far(n2, n2_near)
    n2_own = [n2] + n2_near
    dm_own = [cotangent] + dm_near + dm_far
    dm_parts = dm_own + [swap_core(part) for part in dm_own]
    dm_slots, c_slots = gather(dm_parts, offs.reshape(-1), pos, c_rows)
    dm_slots, c_slots, *n2_far = lax.optimization_barrier((dm_slots, c_slots, *n2_far))
    n2_own = n2_own + n2_far
    n2_parts = n2_own + [swap_core(part) for part in n2_own]
    (n2_slots,) = gather(n2_parts, offs.reshape(-1), pos)
    slots = (n2_slots, dm_slots, c_slots)
    m_parts, d_parts, expert_grads = [], [], []
    for calls in CALLS:
        start, stop = cut((calls[0][0], calls[-1][1]))
        gw = None
        for quarters in calls:
            a, b = cut(quarters)
            if a == b:
                continue
            arrays, sources = [], []
            for i in range(a, b):
                array, index = held[i]
                if not arrays or arrays[-1] is not array:
                    arrays.append(array)
                sources.append((len(arrays) - 1, index))
            m_part, d_part, gw = experts_step(
                place, slots, offs, a, arrays, tuple(sources), gw, a - start, stop - start
            )
            m_parts.append((m_part, a))
            d_parts.append((d_part, a))
        grad = lax.psum_scatter(gw, "dp", scatter_dimension=0, tiled=False, axis_index_groups=groups)
        expert_grads.append((start, grad))

    def both_cores(own, other):
        both = [
            own[k * rows : (k + 1) * rows].astype(f32) + other[k * rows : (k + 1) * rows].astype(f32)
            for k in range(nt)
        ]
        return both[0], [part.astype(bf16) for part in both[1:]]

    def to_tokens(parts, last=()):
        if nt != 4:
            return [swap_t(parts[k], k) for k in range(1, nt)], parts[1:]
        mid = parts[3].shape[0] // 2
        by_x, by_y = swap_t(parts[3][:mid], 1), swap_t(parts[3][mid:], 2)
        x_first, y_last = swap_t(parts[1][:mid], 1), swap_t(parts[2][mid:], 2)
        by_x, by_y, *_ = lax.optimization_barrier((by_x, by_y, *last))
        x_part = (parts[1][mid:].astype(f32) + by_y.astype(f32)).astype(bf16)
        y_part = (parts[2][:mid].astype(f32) + by_x.astype(f32)).astype(bf16)
        return [x_first, swap_t(x_part, 1), swap_t(y_part, 2), y_last], (x_part, y_part)

    (d_other,) = scatter(offs, pos_columns, d_parts, (1,))
    (d_own,) = scatter(offs, pos_columns, d_parts, (0,))
    d_own, d_sent = both_cores(d_own, swap_core(d_other))
    def to_owners(parts, meanwhile):
        if nt != 4:
            return sum_received([swap_t(parts[k], k) for k in range(1, nt)], nt), meanwhile
        mid = parts[3].shape[0] // 2
        by_x = swap_t(jnp.concatenate([parts[3][:mid], parts[1][:mid]]), 1)
        by_y = swap_t(jnp.concatenate([parts[3][mid:], parts[2][mid:]]), 2)
        by_x, by_y, meanwhile = lax.optimization_barrier((by_x, by_y, meanwhile))
        x_last = swap_t((parts[1][mid:].astype(f32) + by_y[:mid].astype(f32)).astype(bf16), 1)
        y_first = swap_t((parts[2][:mid].astype(f32) + by_x[:mid].astype(f32)).astype(bf16), 2)
        return sum_received([by_x[mid:], x_last, y_first, by_y[mid:]], nt), meanwhile

    d_received, d_last = to_tokens([None] + d_sent)
    m_pos = after(pos_columns, *d_last)
    m_other, m_own = scatter(offs, m_pos, m_parts, (1, 0))
    m_other = jnp.concatenate([swap_core(m_other[k * rows : (k + 1) * rows]) for k in range(nt)])
    m_own, m_sent = both_cores(m_own, m_other)

    whole = sharers == 1
    gs1, gain_two = norm_backward(d_own + sum_received(d_received, nt), s1, gains[1:2], cotangent.astype(f32))
    da, *m_sent = lax.optimization_barrier((gs1.astype(bf16), *m_sent))
    if nt == 4:
        mid = rows // 2
        m_step = [swap_t(m_sent[2][:mid], 1), swap_t(m_sent[2][mid:], 2)]
        m_step += [swap_t(m_sent[0][:mid], 1), swap_t(m_sent[1][mid:], 2)]
    else:
        m_step = [swap_t(part, k + 1) for k, part in enumerate(m_sent)]
    if not whole:
        da = lax.all_gather(da, "tensor", axis=0, tiled=True, axis_index_groups=seq_groups)
    input_grad, grads_own, grads_other = attend_backward(
        (nz, nt), whole, place, sequence, gains, q, kv, o, lse, qkv_weights, out_weight,
        da, gain_two * sharers, *([gs1] if whole else []),
    )
    if not whole:
        dn1 = lax.dynamic_slice_in_dim(input_grad, first_row, rows, 0)
        input_grad, _ = norm_backward(dn1, tokens.astype(f32), gains[0], gs1)

    grads_other, m_step = lax.optimization_barrier((grads_other, m_step))
    swapped = [swap_core(part) for part in grads_other]
    both = [(grads_own[k].astype(f32) + swapped[k].astype(f32)).astype(bf16) for k in range(nt)]
    if nt == 4:
        by_x, by_y, x_first, y_last = m_step
        by_x, by_y, *_ = lax.optimization_barrier((by_x, by_y, grads_own))
        x_last = swap_t((m_sent[0][mid:].astype(f32) + by_y.astype(f32)).astype(bf16), 1)
        y_first = swap_t((m_sent[1][:mid].astype(f32) + by_x.astype(f32)).astype(bf16), 2)
        m_step = [x_first, x_last, y_first, y_last]
    block_out = s1 + m_own + sum_received(m_step, nt)
    states = [expert_in, expert_in_first, expert_in_second, expert_down, expert_down_first, expert_down_second]
    experts_new = None
    for start, got in expert_grads[:-1]:
        got = after(got, grads_own)
        experts_new = adam_experts(place, start, got, swap_core(got[1]), states, experts_new)
    received, (experts_new, block_out) = to_owners(both, (experts_new, block_out))
    total = both[0].astype(f32) + received
    owned = total[0]
    sent = [total[j].astype(bf16) for j in range(1, nz)]
    received = [swap_z(part, j + 1) for j, part in enumerate(sent)]
    for start, got in expert_grads[-1:]:
        got = after(got, *sent, *experts_new)
        experts_new = adam_experts(place, start, got, swap_core(got[1]), states, experts_new)
    received, experts_new = lax.optimization_barrier((received, experts_new))
    states = [query_weight, query_first, query_second, keyval_weight, keyval_first, keyval_second]
    states += [output_weight, output_first, output_second, norm_gains, norm_gains_first, norm_gains_second]
    rest_new = adam_rest(place, 1.0 / sharers, owned, received, states[:9] + states[10:] + states[9:10])
    return (block_out, input_grad, *rest_new[9:], *rest_new[:9], *experts_new)


def solution(mesh):
    rows = P(("dp", "tensor"), None)
    by_rows = P(None, "dp", None)
    gains = P(None, None, ("dp", "tensor"))
    proj = P(None, "dp", "tensor")
    out_proj = P(None, "tensor", "dp")
    expert = P(None, "tensor", "dp", None)
    params = (gains,) * 3 + (proj,) * 6 + (out_proj,) * 3 + (expert,) * 6
    return jax.shard_map(
        functools.partial(on_device, mesh.shape["dp"], mesh.shape["tensor"]),
        mesh=mesh,
        in_specs=(rows, rows, by_rows, by_rows) + params,
        out_specs=(rows, rows) + params,
        check_vma=False,
    )
```

```python
import functools
import math

import jax
import jax.numpy as jnp
import numpy as np
from jax import lax
from jax.experimental import pallas as pl
from jax.experimental.pallas import tpu as pltpu
from jax.sharding import PartitionSpec as P

D = 1024
HD = 64
FFE = 512
SEQ_LEN = 512
STEP = 10
CALLS = (((0, 2),), ((2, 3), (3, 4)))
GATHERS = ((0, 3), (3, 4))
QBLK = 256
SUB = 256
CHUNK = 256
SLOTS = 2560
DEEP = 8
PAIR = 2
HELD = 3072

NORM_EPS = 1e-05
ROPE_BASE = 10000.0
BETA_ONE = 0.9
BETA_TWO = 0.95
ADAM_EPS = 1e-08
LEARN_RATE = 0.1
WEIGHT_DECAY = 0.1
MASK_FILL = -1e30
SCALE = 1.0 / math.sqrt(HD)

bf16 = jnp.bfloat16
f32 = jnp.float32
ANY = pl.BlockSpec(memory_space=pl.ANY)
COST = pl.CostEstimate(flops=1, bytes_accessed=1, transcendentals=0)
HBM = pl.BlockSpec(memory_space=pltpu.HBM)
SMEM = pl.BlockSpec(memory_space=pltpu.SMEM)
VMEM = pl.BlockSpec(memory_space=pltpu.VMEM)


def dot(a, b):
    return jnp.dot(a, b, preferred_element_type=f32)


def dot_t(a, b):
    return lax.dot_general(a, b, (((1,), (1,)), ((), ())), preferred_element_type=f32)


def t_dot(a, b):
    return lax.dot_general(a, b, (((0,), (0,)), ((), ())), preferred_element_type=f32)


def rope_tables():
    half = HD // 2
    position = np.arange(SEQ_LEN, dtype=np.float32)
    exponent = np.arange(half, dtype=np.float32) * np.float32(-2.0 / HD)
    frequency = np.exp(exponent * np.float32(math.log(ROPE_BASE))).astype(np.float32)
    angle = (position[:, None] * frequency[None, :]).astype(np.float32)
    cosine = np.cos(angle).astype(np.float32)
    sine = np.sin(angle).astype(np.float32)
    return np.tile(cosine, (1, 4)), np.concatenate([-sine, sine, -sine, sine], axis=1)


def adam_update(master, first_moment, second_moment, gradient, decay_rate):
    first_new = BETA_ONE * first_moment + (1.0 - BETA_ONE) * gradient
    second_new = BETA_TWO * second_moment + (1.0 - BETA_TWO) * gradient * gradient
    first_fixed = first_new / (1.0 - BETA_ONE**STEP)
    second_fixed = second_new / (1.0 - BETA_TWO**STEP)
    master_new = master - LEARN_RATE * (
        first_fixed / (jnp.sqrt(second_fixed) + ADAM_EPS) + decay_rate * master
    )
    return (master_new, first_new, second_new)


def adam_change(first_moment, second_moment, gradient):
    first_new = BETA_ONE * first_moment + (1.0 - BETA_ONE) * gradient
    second_new = BETA_TWO * second_moment + (1.0 - BETA_TWO) * gradient * gradient
    first_fixed = first_new / (1.0 - BETA_ONE**STEP)
    second_fixed = second_new / (1.0 - BETA_TWO**STEP)
    change = -LEARN_RATE * (first_fixed / (jnp.sqrt(second_fixed) + ADAM_EPS))
    return (change, first_new, second_new)


def sum_received(received, nt):
    received = [part.astype(f32) for part in received]
    if nt != 4:
        return functools.reduce(jnp.add, received)
    x_first, x_last, y_first, y_last = received
    return jnp.concatenate([x_first + y_first, x_last + y_last], axis=0)


def rms_scale(values):
    return lax.rsqrt(jnp.mean(values * values, axis=-1, keepdims=True) + NORM_EPS)


def weight_spots(place_ref, nz, nt, relative):
    rows, cols = D // (2 * nz), D // nt
    z, core, t = place_ref[0], place_ref[1], place_ref[2]
    for c in range(2):
        for k in range(nt):
            for j in range(nz):
                row = pl.multiple_of(((z ^ j if relative else j) * 2 + (core ^ c)) * rows, rows)
                col = pl.multiple_of((t ^ k) * cols, cols)
                yield c, k, j, (pl.ds(row, rows), pl.ds(col, cols))


def gather_copies(place_ref, pieces, first, w_ref, sem, nz, nt):
    rows = D // (2 * nz)
    return [
        pltpu.make_async_copy(
            pieces[c * nt + k].at[j, (first + member) * rows : (first + member + 1) * rows, :],
            w_ref.at[(member,) + spot],
            sem.at[((c * nt + k) * nz + j) * w_ref.shape[0] + member],
        )
        for c, k, j, spot in weight_spots(place_ref, nz, nt, False)
        for member in range(w_ref.shape[0])
    ]


def rotate(x, cosine, sine, first_half):
    width = x.shape[-1]
    swapped = jnp.where(
        first_half, pltpu.roll(x, width - HD // 2, 1), pltpu.roll(x, HD // 2, 1)
    )
    return x * cosine + swapped * sine


def join_gains(parts, width):
    owners = parts.shape[0]
    both = jnp.sum(parts[:, :, :128].astype(f32), axis=1)
    lane = lax.broadcasted_iota(jnp.int32, (owners, 128), 1)
    owner = lax.broadcasted_iota(jnp.int32, (owners, D), 0)
    mine = lax.broadcasted_iota(jnp.int32, (owners, D), 1) // width == owner
    out = []
    for values in (both, pltpu.roll(both, 128 - width, 1)):
        values = jnp.where(lane < width, values, 0.0)
        shift = width
        while shift < 128:
            values = values + pltpu.roll(values, shift, 1)
            shift *= 2
        wide = jnp.concatenate([values] * (D // 128), axis=1)
        out.append(jnp.sum(jnp.where(mine, wide, 0.0), axis=0, keepdims=True))
    return jnp.concatenate(out, axis=0)


def attend_forward_kernel(nz, nt, place_ref, tokens_ref, cos_ref, sin_ref, *rest):
    pieces = rest[: 2 * nt]
    q_ref, kv_ref, o_ref, lse_ref, w_ref, gains_ref = rest[2 * nt : 2 * nt + 6]
    qlin_ref, kvlin_ref, parts_ref, sems, gain_sems = rest[2 * nt + 6 :]
    length = tokens_ref.shape[0]
    rows = D // (2 * nz)
    core, t = place_ref[1], place_ref[2]
    gain_copies = [
        pltpu.make_async_copy(
            pieces[c * nt + k].at[j, 2 * rows :, :],
            parts_ref.at[(j * 2 + (core ^ c)) * nt + (t ^ k)],
            gain_sems.at[(c * nt + k) * nz + j],
        )
        for c in range(2)
        for k in range(nt)
        for j in range(nz)
    ]
    for copy in gain_copies:
        copy.start()
    copies = gather_copies(place_ref, pieces, 0, w_ref, sems, nz, nt)
    for copy in copies:
        copy.start()
    lse_ref[...] = jnp.zeros_like(lse_ref)
    for copy in gain_copies:
        copy.wait()
    gains_ref[...] = join_gains(parts_ref[...], D // (2 * nz * nt))
    stream = tokens_ref[...].astype(f32)
    n1 = (stream * rms_scale(stream) * gains_ref[0:1, :]).astype(bf16)
    for copy in copies:
        copy.wait()
    qlin_ref[...] = dot(n1, w_ref[0])
    kvlin_ref[...] = dot(n1, w_ref[1])

    def group(g, carry):
        part = pl.ds(pl.multiple_of(g * 128, 128), 128)
        lane = lax.broadcasted_iota(jnp.int32, (length, 128), 1)
        low = lane < HD
        first_half = (lane & (HD // 2)) == 0
        cosine, sine = cos_ref[...], sin_ref[...]
        q = rotate(qlin_ref[:, part], cosine, sine, first_half)
        kv = kvlin_ref[:, part]
        kv = jnp.where(low, rotate(kv, cosine, sine, first_half), kv)
        q_ref[:, part] = q.astype(bf16)
        kv_ref[:, part] = kv.astype(bf16)
        vk = pltpu.roll(kv, HD, 1).astype(bf16)
        kv = kv.astype(bf16)
        heads = (
            (jnp.where(low, q * SCALE, 0.0).astype(bf16), kv, vk),
            (jnp.where(low, 0.0, q * SCALE).astype(bf16), vk, kv),
        )
        row = lax.broadcasted_iota(jnp.int32, (QBLK, QBLK), 0)
        column = lax.broadcasted_iota(jnp.int32, (QBLK, QBLK), 1)
        seen = column <= row
        for b in range(length // QBLK):
            rows = slice(b * QBLK, (b + 1) * QBLK)
            keys = (b + 1) * QBLK
            outs = []
            lses = lse_ref[rows, :]
            lane_b = lax.broadcasted_iota(jnp.int32, (QBLK, 128), 1)
            for h, (qh, key_side, value_side) in enumerate(heads):
                scores = jnp.where(seen, dot_t(qh[rows], key_side[rows]), MASK_FILL)
                if b > 0:
                    scores = jnp.concatenate([dot_t(qh[rows], key_side[: b * QBLK]), scores], axis=1)
                top = jnp.max(scores, axis=-1, keepdims=True)
                e = jnp.exp(scores - top)
                total = jnp.sum(e, axis=-1, keepdims=True)
                outs.append(dot(e.astype(bf16), value_side[:keys]) * (1.0 / total))
                lses = jnp.where(lane_b == 2 * g + h, top + jnp.log(total), lses)
            lse_ref[rows, :] = lses
            o_ref[rows, part] = jnp.where(lane_b < HD, outs[0], outs[1]).astype(bf16)
        return carry

    lax.fori_loop(0, D // 128, group, 0)


def attend_forward(mesh_sizes, place, tokens, pieces):
    nz, nt = mesh_sizes
    length = tokens.shape[0]
    cosine, sine = rope_tables()
    return pl.pallas_call(
        functools.partial(attend_forward_kernel, nz, nt),
        out_shape=(
            jax.ShapeDtypeStruct((length, D), bf16),
            jax.ShapeDtypeStruct((length, D), bf16),
            jax.ShapeDtypeStruct((length, D), bf16),
            jax.ShapeDtypeStruct((length, 128), f32),
            jax.ShapeDtypeStruct((2, D, D), bf16),
            jax.ShapeDtypeStruct((2, D), f32),
        ),
        in_specs=[SMEM] + [VMEM] * 3 + [ANY] * len(pieces),
        out_specs=[VMEM] * 6,
        scratch_shapes=[
            pltpu.VMEM((length, D), f32),
            pltpu.VMEM((length, D), f32),
            pltpu.VMEM((2 * nz * nt, 16, D // nt), bf16),
            pltpu.SemaphoreType.DMA((2 * nt * nz * 2,)),
            pltpu.SemaphoreType.DMA((2 * nt * nz,)),
        ],
        compiler_params=pltpu.CompilerParams(vmem_limit_bytes=40 * 2**20),
        cost_estimate=pl.CostEstimate(flops=25 * 10**9, bytes_accessed=12 * 2**20, transcendentals=4 * 2**20),
        name="attend_forward",
    )(place, tokens, jnp.asarray(cosine), jnp.asarray(sine), *pieces)


def attend_out_kernel(nz, nt, place_ref, tokens_ref, gains_ref, o_ref, *rest):
    pieces = rest[: 2 * nt]
    s1_ref, n2_ref, w_ref, sems = rest[2 * nt :]
    copies = gather_copies(place_ref, pieces, 0, w_ref, sems, nz, nt)
    for copy in copies:
        copy.start()
    for copy in copies:
        copy.wait()
    s1 = tokens_ref[...].astype(f32) + dot_t(o_ref[...], w_ref[0])
    s1_ref[...] = s1
    n2_ref[...] = (s1 * rms_scale(s1) * gains_ref[1:2, :]).astype(bf16)


def attend_out(mesh_sizes, place, tokens, gains, o, pieces):
    nz, nt = mesh_sizes
    length = tokens.shape[0]
    return pl.pallas_call(
        functools.partial(attend_out_kernel, nz, nt),
        out_shape=(
            jax.ShapeDtypeStruct((length, D), f32),
            jax.ShapeDtypeStruct((length, D), bf16),
            jax.ShapeDtypeStruct((1, D, D), bf16),
        ),
        in_specs=[SMEM] + [VMEM] * 3 + [ANY] * len(pieces),
        out_specs=[VMEM] * 3,
        scratch_shapes=[pltpu.SemaphoreType.DMA((2 * nt * nz,))],
        compiler_params=pltpu.CompilerParams(vmem_limit_bytes=32 * 2**20),
        cost_estimate=COST,
        name="attend_out",
    )(place, tokens, gains, o, *pieces)


def norm_backward(grad, stream, gain, given):
    inverse = rms_scale(stream)
    unit = stream * inverse
    scaled = grad * gain
    through = inverse * (scaled - unit * jnp.mean(scaled * unit, axis=-1, keepdims=True))
    return given + through, jnp.sum(grad * unit, axis=0, keepdims=True)


def attend_backward_kernel(nz, nt, whole, place_ref, tokens_ref, gains_ref, cos_ref, sin_ref, q_ref, kv_ref, o_ref, *rest):
    lse_ref, w_ref, wo_ref, rest = rest[0], rest[1], rest[2], rest[3:]
    da_ref, gain_two_ref, rest = rest[0], rest[1], rest[2:]
    if whole:
        gs1_ref, rest = rest[0], rest[1:]
    out_ref, own_ref, others, rest = rest[0], rest[1], rest[2 : 2 + nt], rest[2 + nt :]
    gw_ref, gg_ref, do_ref, dq_ref, dkv_ref, lse_t_ref, sems = rest
    length = tokens_ref.shape[0]
    rows, cols = D // (2 * nz), D // nt
    sides = ([own_ref.at[k] for k in range(nt)], others)
    da, gain_two = da_ref[...], gain_two_ref[...]

    def member_copies(members):
        return [
            pltpu.make_async_copy(
                gw_ref.at[(member,) + spot],
                sides[c][k].at[j, member * rows : (member + 1) * rows, :],
                sems.at[member, (c * nt + k) * nz + j],
            )
            for member in members
            for c, k, j, spot in weight_spots(place_ref, nz, nt, True)
        ]

    gw_ref[2] = t_dot(da, o_ref[...]).astype(bf16)
    first = member_copies((2,))
    for copy in first:
        copy.start()
    do_ref[...] = dot(da, wo_ref[0]).astype(bf16)
    lse_t_ref[...] = lse_ref[...].T

    def group(g, carry):
        part = pl.ds(pl.multiple_of(g * 128, 128), 128)
        lane = lax.broadcasted_iota(jnp.int32, (length, 128), 1)
        low = lane < HD
        first_half = (lane & (HD // 2)) == 0
        cosine, sine = cos_ref[...], sin_ref[...]
        q = q_ref[:, part].astype(f32)
        kv = kv_ref[:, part].astype(f32)
        do = do_ref[:, part].astype(f32)
        vk = pltpu.roll(kv, HD, 1).astype(bf16)
        kv = kv.astype(bf16)
        q_low = jnp.where(low, q, 0.0).astype(bf16)
        scaled_low = jnp.where(low, q * SCALE, 0.0).astype(bf16)
        scaled_high = jnp.where(low, 0.0, q * SCALE).astype(bf16)
        q_moved = jnp.where(low, pltpu.roll(q, HD, 1), 0.0).astype(bf16)
        do_low = jnp.where(low, do, 0.0).astype(bf16)
        do_high = jnp.where(low, 0.0, do).astype(bf16)
        do_moved = jnp.where(low, 0.0, pltpu.roll(do, HD, 1)).astype(bf16)
        heads = (
            (scaled_low, kv, vk, do_low, q_low, do_moved),
            (scaled_high, vk, kv, do_high, q_moved, do_high),
        )
        row = lax.broadcasted_iota(jnp.int32, (QBLK, QBLK), 0)
        column = lax.broadcasted_iota(jnp.int32, (QBLK, QBLK), 1)
        seen = row <= column
        blocks = length // QBLK
        dkv = [jnp.zeros((QBLK, 128), f32) for _ in range(blocks)]
        dqs = []
        for b in range(blocks):
            rows = slice(b * QBLK, (b + 1) * QBLK)
            keys = (b + 1) * QBLK
            both = []
            for h, (qh, key_side, value_side, doh, q_for_k, do_for_v) in enumerate(heads):
                scores = jnp.where(seen, dot_t(key_side[rows], qh[rows]), MASK_FILL)
                if b > 0:
                    scores = jnp.concatenate([dot_t(key_side[: b * QBLK], qh[rows]), scores], axis=0)
                e = jnp.exp(scores - lse_t_ref[pl.ds(2 * g + h, 1), rows])
                dp = dot_t(value_side[:keys], doh[rows])
                mean = jnp.sum(e * dp, axis=0, keepdims=True)
                dz = (e * (dp - mean)).astype(bf16)
                both.append(t_dot(key_side[:keys], dz))
                add = dot(dz, q_for_k[rows]) + dot(e.astype(bf16), do_for_v[rows])
                for i in range(b + 1):
                    dkv[i] = dkv[i] + add[i * QBLK : (i + 1) * QBLK]
            dqs.append(jnp.concatenate([both[0][:HD], both[1][HD:]], axis=0))
        dq = jnp.concatenate(dqs, axis=1).T * SCALE
        dkv_all = jnp.concatenate(dkv, axis=0)
        dq_ref[:, part] = rotate(dq, cosine, -sine, first_half).astype(bf16)
        dk = rotate(dkv_all * SCALE, cosine, -sine, first_half)
        dkv_ref[:, part] = jnp.where(low, dk, dkv_all).astype(bf16)
        return carry

    lax.fori_loop(0, D // 128, group, 0)
    stream = tokens_ref[...].astype(f32)
    n1 = (stream * rms_scale(stream) * gains_ref[0:1, :]).astype(bf16)
    gw_ref[0] = t_dot(n1, dq_ref[...]).astype(bf16)
    gw_ref[1] = t_dot(n1, dkv_ref[...]).astype(bf16)
    second = member_copies((0, 1))
    for copy in second:
        copy.start()
    dn1 = dot_t(dq_ref[...], w_ref[0]) + dot_t(dkv_ref[...], w_ref[1])
    input_grad, gain_one = norm_backward(dn1, stream, gains_ref[0:1, :], gs1_ref[...] if whole else 0.0)
    out_ref[...] = input_grad if whole else dn1
    gg_ref[...] = jnp.zeros_like(gg_ref)
    for i in range(nt):
        gg_ref[i : i + 1, :] = gain_one[:, i * cols : (i + 1) * cols].astype(bf16)
        gg_ref[nt + i : nt + i + 1, :] = gain_two[:, i * cols : (i + 1) * cols].astype(bf16)
    third = [
        pltpu.make_async_copy(gg_ref, sides[c][k].at[j, 3 * rows :, :], sems.at[3, (c * nt + k) * nz + j])
        for c in range(2)
        for k in range(nt)
        for j in range(nz)
    ]
    for copy in third:
        copy.start()
    for copy in first + second + third:
        copy.wait()


def attend_backward(mesh_sizes, whole, place, tokens, gains, q, kv, o, lse, weights, out_weight, *given):
    nz, nt = mesh_sizes
    length = tokens.shape[0]
    cosine, sine = rope_tables()
    part = (nz, 3 * D // (2 * nz) + 16, D // nt)
    out = pl.pallas_call(
        functools.partial(attend_backward_kernel, nz, nt, whole),
        out_shape=[jax.ShapeDtypeStruct((length, D), f32), jax.ShapeDtypeStruct((nt,) + part, bf16)]
        + [jax.ShapeDtypeStruct(part, bf16)] * nt,
        in_specs=[SMEM] + [VMEM] * (10 + len(given)),
        out_specs=[VMEM] + [ANY] * (1 + nt),
        scratch_shapes=[
            pltpu.VMEM((3, D, D), bf16),
            pltpu.VMEM((16, D // nt), bf16),
            pltpu.VMEM((length, D), bf16),
            pltpu.VMEM((length, D), bf16),
            pltpu.VMEM((length, D), bf16),
            pltpu.VMEM((128, length), f32),
            pltpu.SemaphoreType.DMA((4, 2 * nt * nz)),
        ],
        compiler_params=pltpu.CompilerParams(vmem_limit_bytes=60 * 2**20),
        cost_estimate=COST,
        name="attend_backward",
    )(
        place, tokens, gains, jnp.asarray(cosine), jnp.asarray(sine), q, kv, o, lse, weights, out_weight, *given
    )
    return out[0], out[1], out[2:]


def gather_kernel(starts, experts, with_c, offs_ref, pos_ref, *rest):
    tiles = len(starts) - 1
    if with_c:
        c_ref, rest = rest[0], rest[1:]
    parts, rest = rest[:tiles], rest[tiles:]
    outs, rest = rest[: 1 + with_c], rest[1 + with_c :]
    held, (buf, in_sems, out_sems) = rest[: 1 + with_c], rest[1 + with_c :]
    subs = starts[-1] // SUB

    def block_copy(s):
        j = max(i for i in range(tiles) if starts[i] <= s * SUB)
        return pltpu.make_async_copy(
            parts[j].at[pl.ds(s * SUB - starts[j], SUB)], buf.at[s % DEEP], in_sems.at[s % DEEP]
        )

    def flush(e, chunk):
        spot = pl.ds(pl.multiple_of(chunk * CHUNK, CHUNK), CHUNK)
        return [
            pltpu.make_async_copy(slots.at[e, spot, :], out.at[e, spot, :], out_sems.at[i, e, chunk])
            for i, (slots, out) in enumerate(zip(held, outs))
        ]

    for s in range(DEEP - 1):
        block_copy(s).start()

    def block(s, carry):
        for ahead in range(DEEP - 1, subs):

            @pl.when(s + DEEP - 1 == ahead)
            def _():
                block_copy(ahead).start()

        slot = lax.rem(s, DEEP)
        begin = [offs_ref[e * (subs + 1) + s] for e in range(experts)]
        end = [offs_ref[e * (subs + 1) + s + 1] for e in range(experts)]
        most = functools.reduce(jnp.maximum, [end[e] - begin[e] for e in range(experts)])
        pltpu.make_async_copy(parts[0].at[pl.ds(0, SUB)], buf.at[slot], in_sems.at[slot]).wait()

        def fill(count):
            slots = lax.broadcasted_iota(jnp.int32, (count, SUB), 0).astype(f32)
            spots = [pl.ds(pl.multiple_of(begin[e], 16), count) for e in range(experts)]
            picks = []
            for e in range(experts):
                hit = slots == pos_ref[pl.ds(e * subs + s, 1), :]
                picks.append(jnp.where(hit, 1.0, 0.0).astype(bf16))
                if with_c:
                    c = jnp.sum(jnp.where(hit, c_ref[pl.ds(e * subs + s, 1), :], 0.0), axis=1, keepdims=True)
                    held[1][e, spots[e], :] = jnp.broadcast_to(c, (count, 128))
            rows = dot(jnp.concatenate(picks, axis=0), buf[slot]).astype(bf16)
            for e in range(experts):
                held[0][e, spots[e], :] = rows[e * count : (e + 1) * count]

        @pl.when(most <= SUB // 2)
        def _():
            fill(SUB // 2)

        @pl.when(most > SUB // 2)
        def _():
            fill(SUB)

        for e in range(experts):

            @pl.when(end[e] // CHUNK > begin[e] // CHUNK)
            def _():
                for copy in flush(e, begin[e] // CHUNK):
                    copy.start()

        return carry

    lax.fori_loop(0, subs, block, 0)
    for e in range(experts):
        total = offs_ref[e * (subs + 1) + subs]
        tail = pl.ds(pl.multiple_of(total, 16), CHUNK)
        for slots in held:
            slots[e, tail, :] = jnp.zeros((CHUNK, slots.shape[2]), slots.dtype)
        for copy in flush(e, total // CHUNK):
            copy.start()
    for e in range(experts):

        def drain(chunk, carry):
            for copy in flush(e, chunk):
                copy.wait()
            return carry

        lax.fori_loop(0, offs_ref[e * (subs + 1) + subs] // CHUNK + 1, drain, 0)


def gather(parts, offs, pos, c=None):
    starts = [0]
    for part in parts:
        starts.append(starts[-1] + part.shape[0])
    experts = pos.shape[0] * SUB // starts[-1]
    with_c = c is not None
    held = [((experts, SLOTS, D), bf16)] + [((experts, SLOTS, 128), f32)] * with_c
    return pl.pallas_call(
        functools.partial(gather_kernel, tuple(starts), experts, with_c),
        out_shape=[jax.ShapeDtypeStruct(*kind) for kind in held],
        in_specs=[SMEM, VMEM] + [VMEM] * with_c + [HBM] * len(parts),
        out_specs=[HBM] * len(held),
        scratch_shapes=[pltpu.VMEM(*kind) for kind in held]
        + [
            pltpu.VMEM((DEEP, SUB, D), bf16),
            pltpu.SemaphoreType.DMA((DEEP,)),
            pltpu.SemaphoreType.DMA((1 + with_c, experts, SLOTS // CHUNK)),
        ],
        compiler_params=pltpu.CompilerParams(vmem_limit_bytes=62 * 2**20),
        cost_estimate=COST,
        name="gather_rows",
    )(offs, pos, *([c] if with_c else []), *parts)


def experts_kernel(first, subs, sources, kept, place_ref, offs_ref, n2_ref, dm_ref, c_ref, *rest):
    arrays = 1 + sources[-1][0]
    weights, rest = rest[:arrays], rest[arrays + kept :]
    m_ref, d_ref, gw_ref = rest[:3]
    win_buf, wdown_buf, n2_in, dm_in, c_in, m_out, d_out, zeros, gin, gdown, w_sems, in_sems, out_sems = rest[3:]
    e = pl.program_id(0)
    nz, cores, _, wrows, _ = gw_ref.shape
    rin, rdown = D // (nz * cores), FFE // (nz * cores)
    core = place_ref[1]
    total = offs_ref[(first + e) * (subs + 1) + subs]
    chunks = jnp.maximum((total + CHUNK - 1) // CHUNK, 1)

    def weight_copies(index):
        i, place = sources[index]
        slot = index % 2
        return [
            pltpu.make_async_copy(
                weights[i].at[:, side, place, spot, :], buf.at[slot, :, core ^ side], w_sems.at[2 * side + j, slot]
            )
            for side in range(2)
            for j, (spot, buf) in enumerate(((slice(0, rin), win_buf), (slice(rin, wrows), wdown_buf)))
        ]

    def in_copies(e, k, slot):
        spot = pl.ds(pl.multiple_of(k * CHUNK, CHUNK), CHUNK)
        return [
            pltpu.make_async_copy(source.at[first + e, spot, :], target.at[slot], in_sems.at[i, slot])
            for i, (source, target) in enumerate(((n2_ref, n2_in), (dm_ref, dm_in), (c_ref, c_in)))
        ]

    def out_copies(k, slot):
        spot = pl.ds(pl.multiple_of(k * CHUNK, CHUNK), CHUNK)
        return (
            pltpu.make_async_copy(m_out.at[slot], m_ref.at[e, spot, :], out_sems.at[0, slot]),
            pltpu.make_async_copy(d_out.at[slot], d_ref.at[e, spot, :], out_sems.at[1, slot]),
        )

    @pl.when(e == 0)
    def _():
        for copy in in_copies(e, 0, 0) + weight_copies(0):
            copy.start()
        zeros[...] = jnp.zeros_like(zeros)

    for index in range(len(sources)):

        @pl.when(e == index)
        def _():
            for copy in weight_copies(index):
                copy.wait()
            if index + 1 < len(sources):
                for copy in weight_copies(index + 1):
                    copy.start()

    at = lax.rem(e, 2)

    def one_chunk(k, carry):
        slot = lax.rem(k, 2)
        for copy in in_copies(e, k, slot):
            copy.wait()

        @pl.when(k + 1 < chunks)
        def _():
            for copy in in_copies(e, k + 1, 1 - slot):
                copy.start()

        @pl.when(k >= 2)
        def _():
            for copy in out_copies(k - 2, slot):
                copy.wait()

        win = win_buf[at].reshape(D, D)
        wdown = wdown_buf[at].reshape(FFE, D)
        n2, dm, c = n2_in[slot], dm_in[slot], c_in[slot][:, 0:1]
        hidden = dot(n2, win)
        gate, up = hidden[:, :FFE], hidden[:, FFE:]
        sigma = jax.nn.sigmoid(gate)
        silu = gate * sigma
        active = (c * silu * up).astype(bf16)
        m_out[slot] = dot(active, wdown).astype(bf16)
        gdown[...] = jnp.where(k == 0, 0.0, gdown[...]) + dot(active.T, dm)
        da = c * dot_t(dm, wdown)
        dgate = da * up * (sigma + silu * (1.0 - sigma))
        dup = da * silu
        dh = jnp.concatenate([dgate.astype(bf16), dup.astype(bf16)], axis=1)
        gin[...] = jnp.where(k == 0, 0.0, gin[...]) + dot(n2.T, dh)
        d_out[slot] = dot_t(dh, win).astype(bf16)
        for copy in out_copies(k, slot):
            copy.start()
        return carry

    lax.fori_loop(0, chunks, one_chunk, 0)

    @pl.when(e + 1 < len(sources))
    def _():
        for copy in in_copies(e + 1, 0, 0):
            copy.start()

    spot = pl.ds(pl.multiple_of(chunks * CHUNK, CHUNK), CHUNK)
    ends = (
        pltpu.make_async_copy(zeros, m_ref.at[e, spot, :], out_sems.at[0, 2]),
        pltpu.make_async_copy(zeros, d_ref.at[e, spot, :], out_sems.at[1, 2]),
    )
    for copy in ends:
        copy.start()
    for j in range(nz):
        for side in range(2):
            owner = 2 * j + (core ^ side)
            at_in, at_down = pl.multiple_of(owner * rin, rin), pl.multiple_of(owner * rdown, rdown)
            gw_ref[j, side, 0, :rin, :] = gin[pl.ds(at_in, rin), :].astype(bf16)
            gw_ref[j, side, 0, rin:, :] = gdown[pl.ds(at_down, rdown), :].astype(bf16)
    for copy in ends:
        copy.wait()
    for back in (1, 2):

        @pl.when(chunks >= back)
        def _():
            for copy in out_copies(chunks - back, lax.rem(chunks - back, 2)):
                copy.wait()


def experts_step(place, slots, offs, first, weights, sources, before, spot, count):
    nz, cores, _, wrows, _ = weights[0].shape
    experts = len(sources)
    rin, rdown = D // (nz * cores), FFE // (nz * cores)
    part = jax.ShapeDtypeStruct((experts, HELD, D), bf16)
    kept = [] if before is None else [before]
    subs = offs.shape[1] - 1
    return pl.pallas_call(
        functools.partial(experts_kernel, first, subs, sources, len(kept)),
        grid=(experts,),
        out_shape=(part, part, jax.ShapeDtypeStruct((nz, cores, count, wrows, D), bf16)),
        in_specs=[SMEM, SMEM] + [HBM] * (3 + len(weights) + len(kept)),
        out_specs=(HBM, HBM, pl.BlockSpec((nz, cores, 1, wrows, D), lambda e: (0, 0, spot + e, 0, 0))),
        scratch_shapes=[
            pltpu.VMEM((2, nz, cores, rin, D), bf16),
            pltpu.VMEM((2, nz, cores, rdown, D), bf16),
            pltpu.VMEM((2, CHUNK, D), bf16),
            pltpu.VMEM((2, CHUNK, D), bf16),
            pltpu.VMEM((2, CHUNK, 128), f32),
            pltpu.VMEM((2, CHUNK, D), bf16),
            pltpu.VMEM((2, CHUNK, D), bf16),
            pltpu.VMEM((CHUNK, D), bf16),
            pltpu.VMEM((D, D), f32),
            pltpu.VMEM((FFE, D), f32),
            pltpu.SemaphoreType.DMA((4, 2)),
            pltpu.SemaphoreType.DMA((3, 2)),
            pltpu.SemaphoreType.DMA((2, 3)),
        ],
        input_output_aliases={5 + len(weights): 2} if kept else {},
        compiler_params=pltpu.CompilerParams(
            vmem_limit_bytes=60 * 2**20, dimension_semantics=("arbitrary",)
        ),
        cost_estimate=COST,
        name="experts",
    )(place, offs.reshape(-1), *slots, *weights, *kept)


def scatter_kernel(halves, sources, experts, subs, offs_ref, pos_ref, *rest):
    arrays = 1 + sources[-1][1]
    parts, rest = rest[:arrays], rest[arrays:]
    outs, (slots, sems) = rest[: len(halves)], rest[len(halves) :]
    i, steps = pl.program_id(0), subs // (2 * PAIR)
    first = lax.rem(i * PAIR + halves[0] * (subs // 2), subs)

    half = subs // 2

    def each(low, high, act):
        for spot, (e, array, index) in enumerate(sources):

            def one(chunk, carry):
                rows = pl.ds(pl.multiple_of(chunk * CHUNK, CHUNK), CHUNK)
                act(pltpu.make_async_copy(parts[array].at[index, rows, :], slots.at[spot, rows, :], sems.at[spot, chunk]))
                return carry

            lax.fori_loop(*spans(e, low, high), one, 0)

    def spans(e, low, high):
        middle = offs_ref[e * (subs + 1) + half] // CHUNK
        last_low = (offs_ref[e * (subs + 1) + low] + CHUNK - 1) // CHUNK + 1
        begin = jnp.where(lax.rem(low, half) == 0, offs_ref[e * (subs + 1) + low] // CHUNK, last_low)
        end = (offs_ref[e * (subs + 1) + high] + CHUNK - 1) // CHUNK + 1
        if len(halves) == 2:
            early = jnp.asarray(low) < half
            begin = jnp.where(early, jnp.minimum(begin, middle), begin)
            end = jnp.where(early, jnp.minimum(end, middle), end)
        return begin, end

    @pl.when(i == 0)
    def _():
        for h in halves:
            each(h * half, (h + 1) * half, lambda copy: copy.start())

    each(first, first + PAIR, lambda copy: copy.wait())
    lane = lax.broadcasted_iota(jnp.int32, (SUB, SUB), 1).astype(f32)
    totals = []
    for p in range(PAIR):
        picks = [
            jnp.where(lane == pos_ref[p * SUB : (p + 1) * SUB, e : e + 1], 1.0, 0.0).astype(bf16) for e, _, _ in sources
        ]
        windows = [
            slots[spot, pl.ds(pl.multiple_of(offs_ref[e * (subs + 1) + first + p], 16), SUB), :]
            for spot, (e, _, _) in enumerate(sources)
        ]
        totals.append(dot(jnp.concatenate(picks, axis=1), jnp.concatenate(windows, axis=0)).astype(bf16))
    for j, out_ref in enumerate(outs):

        @pl.when(i // steps == j)
        def _():
            for p in range(PAIR):
                out_ref[p * SUB : (p + 1) * SUB, :] = totals[p]


def scatter(offs, pos_columns, parts, halves):
    tokens, experts = pos_columns.shape
    sources = [
        (first + index, i, index) for i, (part, first) in enumerate(parts) for index in range(part.shape[0])
    ]
    subs = tokens // SUB
    steps = subs // (2 * PAIR)
    shift = halves[0] * steps
    blocks = [
        pl.BlockSpec((PAIR * SUB, D), lambda i, j=j: (jnp.clip(i - j * steps, 0, steps - 1), 0))
        for j in range(len(halves))
    ]
    return pl.pallas_call(
        functools.partial(scatter_kernel, halves, sources, experts, subs),
        grid=(len(halves) * steps,),
        out_shape=[jax.ShapeDtypeStruct((tokens // 2, D), bf16)] * len(halves),
        in_specs=[SMEM, pl.BlockSpec((PAIR * SUB, experts), lambda i: (lax.rem(i + shift, 2 * steps), 0))]
        + [HBM] * len(parts),
        out_specs=blocks,
        scratch_shapes=[
            pltpu.VMEM((len(sources), HELD, D), bf16),
            pltpu.SemaphoreType.DMA((len(sources), HELD // CHUNK)),
        ],
        compiler_params=pltpu.CompilerParams(
            vmem_limit_bytes=60 * 2**20, dimension_semantics=("arbitrary",)
        ),
        cost_estimate=COST,
        name="scatter_rows",
    )(offs.reshape(-1), pos_columns, *[part for part, _ in parts])


def adam_kernel(per, place_ref, mine_ref, recv_ref, *rest):
    states, news = rest[:6], rest[-6:]
    here = pl.program_id(0) // per == place_ref[1]
    grad = jnp.where(here, mine_ref[0, 0], recv_ref[0]).astype(f32)
    rin = states[0].shape[2]
    for i, part in ((0, grad[:rin]), (3, grad[rin:])):
        masters = [ref[0, 0] for ref in states[i : i + 3]]
        for ref, new in zip(news[i : i + 3], adam_update(*masters, part, WEIGHT_DECAY)):
            ref[0, 0] = new


def adam_experts(place, a, mine, recv, states, before):
    experts, rin = states[0].shape[1:3]
    rdown = states[3].shape[2]
    per = recv.shape[0]
    half = experts // 2
    spec = [
        pl.BlockSpec((1, 1, r, D), lambda i, place: (0, i // per * half + a + i % per, 0, 0))
        for r in (rin, rdown)
    ]
    specs = [spec[0]] * 3 + [spec[1]] * 3
    kept = [] if before is None else list(before)
    return pl.pallas_call(
        functools.partial(adam_kernel, per),
        grid_spec=pltpu.PrefetchScalarGridSpec(
            num_scalar_prefetch=1,
            grid=(2 * per,),
            in_specs=[
                pl.BlockSpec((1, 1, rin + rdown, D), lambda i, place: (0, i % per, 0, 0)),
                pl.BlockSpec((1, rin + rdown, D), lambda i, place: (i % per, 0, 0)),
            ]
            + specs
            + [HBM] * len(kept),
            out_specs=specs,
        ),
        out_shape=[jax.ShapeDtypeStruct(state.shape, f32) for state in states],
        input_output_aliases={9 + i: i for i in range(len(kept))},
        compiler_params=pltpu.CompilerParams(
            vmem_limit_bytes=60 * 2**20, dimension_semantics=("arbitrary",)
        ),
        cost_estimate=COST,
        name="adam_experts",
    )(place, mine, recv, *states, *kept)


def adam_rest_kernel(scale, place_ref, mine_ref, *rest):
    count = len(rest) - 25
    received, states, news, (grad_ref,) = rest[:count], rest[count : count + 12], rest[count + 12 : count + 24], rest[-1:]
    total = mine_ref[...]
    for part in received:
        total = total + part[...].astype(f32)
    grad_ref[...] = total * scale
    rows, cols = states[0].shape[1:]
    width = states[9].shape[2]
    for i, turned in ((0, False), (1, False), (2, True)):
        part = grad_ref[i * rows : (i + 1) * rows, :]
        refs = slice(3 * i, 3 * i + 3)
        masters = [ref[0] for ref in states[refs]]
        for ref, new in zip(news[refs], adam_update(*masters, part.T if turned else part, WEIGHT_DECAY)):
            ref[0] = new
    start = place_ref[3] * width
    for i in range(2):
        row = grad_ref[pl.ds(3 * rows + i * (D // cols) + start // cols, 1), :]
        part = pltpu.roll(row, lax.rem(cols - lax.rem(start, cols), cols), 1)[:, :width]
        moments = [ref[0, i : i + 1, :] for ref in states[9:11]]
        for ref, new in zip(news[9:], adam_change(*moments, part)):
            ref[0, i : i + 1, :] = new


def adam_rest(place, scale, mine, received, states):
    return pl.pallas_call(
        functools.partial(adam_rest_kernel, scale),
        out_shape=[jax.ShapeDtypeStruct(state.shape, f32) for state in states],
        in_specs=[SMEM] + [VMEM] * (1 + len(received) + len(states)),
        out_specs=[VMEM] * len(states),
        scratch_shapes=[pltpu.VMEM(mine.shape, f32)],
        compiler_params=pltpu.CompilerParams(vmem_limit_bytes=32 * 2**20),
        cost_estimate=COST,
        name="adam_rest",
    )(place, mine, *received, *states)


def on_device(
    ndp,
    nt,
    tokens,
    cotangent,
    routes,
    gate_weights,
    norm_gains,
    norm_gains_first,
    norm_gains_second,
    query_weight,
    query_first,
    query_second,
    keyval_weight,
    keyval_first,
    keyval_second,
    output_weight,
    output_first,
    output_second,
    expert_in,
    expert_in_first,
    expert_in_second,
    expert_down,
    expert_down_first,
    expert_down_second,
):
    nz = ndp // 2
    place_dp = lax.axis_index("dp")
    t = lax.axis_index("tensor")
    z, core = place_dp // 2, place_dp % 2
    place = jnp.stack([z, core, t, place_dp * nt + t]).astype(jnp.int32)
    rows = tokens.shape[0]
    sharers = max(1, SEQ_LEN // rows)

    def swap_core(x):
        return lax.ppermute(x, "dp", [(i, i ^ 1) for i in range(ndp)])

    def swap_z(x, j):
        return lax.ppermute(x, "dp", [(i, i ^ (2 * j)) for i in range(ndp)])

    def swap_t(x, k):
        return lax.ppermute(x, "tensor", [(i, i ^ k) for i in range(nt)])

    def spread_t(x):
        return [x] + [swap_t(x, k) for k in range(1, nt)]

    def spread_z(x):
        return [x] + [swap_z(x, j) for j in range(1, nz)]

    def after(x, *others):
        return lax.optimization_barrier((x,) + others)[0]

    def near(x):
        return [swap_t(x, k) for k in range(1, nt)] if nt != 4 else [swap_t(x, 1), swap_t(x, 2)]

    def far(x, others):
        mid = x.shape[0] // 2
        return [] if nt != 4 else [swap_t(others[0][:mid], 2), swap_t(others[1][mid:], 1)]

    width = norm_gains.shape[2]
    wrows, wcols = query_weight.shape[1:]
    high = lax.reduce_precision(norm_gains[0], 8, 7)
    middle = lax.reduce_precision(norm_gains[0] - high, 8, 7)
    gain_rows = jnp.stack([high, middle, norm_gains[0] - high - middle]).astype(bf16).reshape(3, 2 * width)
    own = jnp.concatenate(
        [
            query_weight[0].astype(bf16),
            keyval_weight[0].astype(bf16),
            jnp.pad(gain_rows, ((0, 13), (0, wcols - 2 * width))),
            output_weight[0].T.astype(bf16),
        ],
        axis=0,
    )
    half = expert_in.shape[1] // 2
    groups = [[2 * i + c for i in range(nz)] for c in range(2)]

    def cut(quarters):
        return quarters[0] * half // 4, quarters[1] * half // 4

    def shard(a, b, *ready):
        masters = lax.optimization_barrier((expert_in, expert_down, own, *ready))[:2]

        def low(side):
            return jnp.concatenate(
                [lax.dynamic_slice_in_dim(w[0], side * half + a, b - a, 0).astype(bf16) for w in masters], axis=1
            )

        return jnp.stack([low(core), swap_core(low(1 - core))])

    spans = [cut(quarters) for quarters in GATHERS]
    spans = [(a, b) for a, b in spans if a < b]
    shards = [shard(*spans[0])]
    for a, b in spans[1:]:
        shards.append(shard(a, b))
    column = lax.all_gather(own, "dp", axis=0, tiled=False, axis_index_groups=groups)
    held = {}
    for (a, b), part in zip(spans, shards):
        whole = lax.all_gather(part, "dp", axis=0, tiled=False, axis_index_groups=groups)
        held.update({i: (whole, i - a) for i in range(a, b)})
    dm_near = near(cotangent)
    pieces = spread_t(after(column[:, : 2 * wrows + 16], *dm_near))
    pieces_out = spread_t(after(column[:, 2 * wrows + 16 :], *pieces[1:]))
    dm_far = far(cotangent, list(lax.optimization_barrier((*dm_near, *pieces[1:])))[: len(dm_near)])
    pieces = pieces + [swap_core(piece) for piece in pieces]

    ids = t * 2 * half + jnp.arange(2 * half, dtype=jnp.int32)
    chosen = routes[0].T[None, :, :] == ids[:, None, None]
    c_all = jnp.sum(jnp.where(chosen, gate_weights[0].T[None, :, :], 0.0), axis=1)
    c_mine = lax.dynamic_slice_in_dim(c_all, core * half, half, 0)
    c_got = swap_core(lax.dynamic_slice_in_dim(c_all, (1 - core) * half, half, 0))
    c_both = jnp.stack([c_mine, c_got], axis=1).reshape(half, 2, nt, rows)
    c_both = jnp.take(c_both, jnp.arange(nt, dtype=jnp.int32) ^ t, axis=2)
    subs = 2 * nt * rows // SUB
    c_rows = c_both.reshape(half * subs, SUB)
    taken = c_rows != 0.0
    upto = lax.broadcasted_iota(jnp.int32, (SUB, SUB), 0) <= lax.broadcasted_iota(jnp.int32, (SUB, SUB), 1)
    rank = dot(taken.astype(bf16), upto.astype(bf16))
    pos = jnp.where(taken, rank - 1.0, -1.0)
    sizes = (rank[:, SUB - 1].astype(jnp.int32).reshape(half, subs) + 15) // 16 * 16
    offs = jnp.pad(jnp.cumsum(sizes, axis=1), ((0, 0), (1, 0)))
    pos_columns = pos.reshape(half, subs * SUB).T

    sequence = after(tokens, offs, pos, c_rows, pos_columns)
    if sharers > 1:
        seq_groups = [list(range(i, i + sharers)) for i in range(0, nt, sharers)]
        sequence = lax.all_gather(tokens, "tensor", axis=0, tiled=True, axis_index_groups=seq_groups)
    first_row = (t % sharers) * rows
    q, kv, o, lse, qkv_weights, gains = attend_forward((nz, nt), place, sequence, pieces)
    o, *pieces_out = lax.optimization_barrier((o, *pieces_out))
    pieces_out = pieces_out + [swap_core(piece) for piece in pieces_out]
    s1, n2, out_weight = attend_out((nz, nt), place, sequence, gains, o, pieces_out)
    if sharers > 1:
        s1 = lax.dynamic_slice_in_dim(s1, first_row, rows, 0)
        n2 = lax.dynamic_slice_in_dim(n2, first_row, rows, 0)

    n2_near = near(n2)
    n2_far = far(n2, n2_near)
    n2_own = [n2] + n2_near
    dm_own = [cotangent] + dm_near + dm_far
    dm_parts = dm_own + [swap_core(part) for part in dm_own]
    dm_slots, c_slots = gather(dm_parts, offs.reshape(-1), pos, c_rows)
    dm_slots, c_slots, *n2_far = lax.optimization_barrier((dm_slots, c_slots, *n2_far))
    n2_own = n2_own + n2_far
    n2_parts = n2_own + [swap_core(part) for part in n2_own]
    (n2_slots,) = gather(n2_parts, offs.reshape(-1), pos)
    slots = (n2_slots, dm_slots, c_slots)
    m_parts, d_parts, expert_grads = [], [], []
    for calls in CALLS:
        start, stop = cut((calls[0][0], calls[-1][1]))
        gw = None
        for quarters in calls:
            a, b = cut(quarters)
            if a == b:
                continue
            arrays, sources = [], []
            for i in range(a, b):
                array, index = held[i]
                if not arrays or arrays[-1] is not array:
                    arrays.append(array)
                sources.append((len(arrays) - 1, index))
            m_part, d_part, gw = experts_step(
                place, slots, offs, a, arrays, tuple(sources), gw, a - start, stop - start
            )
            m_parts.append((m_part, a))
            d_parts.append((d_part, a))
        grad = lax.psum_scatter(gw, "dp", scatter_dimension=0, tiled=False, axis_index_groups=groups)
        expert_grads.append((start, grad))

    def both_cores(own, other):
        both = [
            own[k * rows : (k + 1) * rows].astype(f32) + other[k * rows : (k + 1) * rows].astype(f32)
            for k in range(nt)
        ]
        return both[0], [part.astype(bf16) for part in both[1:]]

    def to_tokens(parts, last=()):
        if nt != 4:
            return [swap_t(parts[k], k) for k in range(1, nt)], parts[1:]
        mid = parts[3].shape[0] // 2
        by_x, by_y = swap_t(parts[3][:mid], 1), swap_t(parts[3][mid:], 2)
        x_first, y_last = swap_t(parts[1][:mid], 1), swap_t(parts[2][mid:], 2)
        by_x, by_y, *_ = lax.optimization_barrier((by_x, by_y, *last))
        x_part = (parts[1][mid:].astype(f32) + by_y.astype(f32)).astype(bf16)
        y_part = (parts[2][:mid].astype(f32) + by_x.astype(f32)).astype(bf16)
        return [x_first, swap_t(x_part, 1), swap_t(y_part, 2), y_last], (x_part, y_part)

    (d_other,) = scatter(offs, pos_columns, d_parts, (1,))
    (d_own,) = scatter(offs, pos_columns, d_parts, (0,))
    d_own, d_sent = both_cores(d_own, swap_core(d_other))
    def to_owners(parts, meanwhile):
        if nt != 4:
            return sum_received([swap_t(parts[k], k) for k in range(1, nt)], nt), meanwhile
        mid = parts[3].shape[0] // 2
        by_x = swap_t(jnp.concatenate([parts[3][:mid], parts[1][:mid]]), 1)
        by_y = swap_t(jnp.concatenate([parts[3][mid:], parts[2][mid:]]), 2)
        by_x, by_y, meanwhile = lax.optimization_barrier((by_x, by_y, meanwhile))
        x_last = swap_t((parts[1][mid:].astype(f32) + by_y[:mid].astype(f32)).astype(bf16), 1)
        y_first = swap_t((parts[2][:mid].astype(f32) + by_x[:mid].astype(f32)).astype(bf16), 2)
        return sum_received([by_x[mid:], x_last, y_first, by_y[mid:]], nt), meanwhile

    d_received, d_last = to_tokens([None] + d_sent)
    m_pos = after(pos_columns, *d_last)
    m_other, m_own = scatter(offs, m_pos, m_parts, (1, 0))
    m_other = jnp.concatenate([swap_core(m_other[k * rows : (k + 1) * rows]) for k in range(nt)])
    m_own, m_sent = both_cores(m_own, m_other)

    whole = sharers == 1
    gs1, gain_two = norm_backward(d_own + sum_received(d_received, nt), s1, gains[1:2], cotangent.astype(f32))
    da, *m_sent = lax.optimization_barrier((gs1.astype(bf16), *m_sent))
    if nt == 4:
        mid = rows // 2
        m_step = [swap_t(m_sent[2][:mid], 1), swap_t(m_sent[2][mid:], 2)]
        m_step += [swap_t(m_sent[0][:mid], 1), swap_t(m_sent[1][mid:], 2)]
    else:
        m_step = [swap_t(part, k + 1) for k, part in enumerate(m_sent)]
    if not whole:
        da = lax.all_gather(da, "tensor", axis=0, tiled=True, axis_index_groups=seq_groups)
    input_grad, grads_own, grads_other = attend_backward(
        (nz, nt), whole, place, sequence, gains, q, kv, o, lse, qkv_weights, out_weight,
        da, gain_two * sharers, *([gs1] if whole else []),
    )
    if not whole:
        dn1 = lax.dynamic_slice_in_dim(input_grad, first_row, rows, 0)
        input_grad, _ = norm_backward(dn1, tokens.astype(f32), gains[0], gs1)

    grads_other, m_step = lax.optimization_barrier((grads_other, m_step))
    swapped = [swap_core(part) for part in grads_other]
    both = [(grads_own[k].astype(f32) + swapped[k].astype(f32)).astype(bf16) for k in range(nt)]
    if nt == 4:
        by_x, by_y, x_first, y_last = m_step
        by_x, by_y, *_ = lax.optimization_barrier((by_x, by_y, grads_own))
        x_last = swap_t((m_sent[0][mid:].astype(f32) + by_y.astype(f32)).astype(bf16), 1)
        y_first = swap_t((m_sent[1][:mid].astype(f32) + by_x.astype(f32)).astype(bf16), 2)
        m_step = [x_first, x_last, y_first, y_last]
    block_out = s1 + m_own + sum_received(m_step, nt)
    states = [expert_in, expert_in_first, expert_in_second, expert_down, expert_down_first, expert_down_second]
    experts_new = None
    for start, got in expert_grads[:-1]:
        got = after(got, grads_own)
        experts_new = adam_experts(place, start, got, swap_core(got[1]), states, experts_new)
    received, (experts_new, block_out) = to_owners(both, (experts_new, block_out))
    total = both[0].astype(f32) + received
    owned = total[0]
    sent = [total[j].astype(bf16) for j in range(1, nz)]
    received = [swap_z(part, j + 1) for j, part in enumerate(sent)]
    for start, got in expert_grads[-1:]:
        got = after(got, *sent, *experts_new)
        experts_new = adam_experts(place, start, got, swap_core(got[1]), states, experts_new)
    received, experts_new = lax.optimization_barrier((received, experts_new))
    states = [query_weight, query_first, query_second, keyval_weight, keyval_first, keyval_second]
    states += [output_weight, output_first, output_second, norm_gains, norm_gains_first, norm_gains_second]
    rest_new = adam_rest(place, 1.0 / sharers, owned, received, states[:9] + states[10:] + states[9:10])
    return (block_out, input_grad, *rest_new[9:], *rest_new[:9], *experts_new)


def solution(mesh):
    rows = P(("dp", "tensor"), None)
    by_rows = P(None, "dp", None)
    gains = P(None, None, ("dp", "tensor"))
    proj = P(None, "dp", "tensor")
    out_proj = P(None, "tensor", "dp")
    expert = P(None, "tensor", "dp", None)
    params = (gains,) * 3 + (proj,) * 6 + (out_proj,) * 3 + (expert,) * 6
    return jax.shard_map(
        functools.partial(on_device, mesh.shape["dp"], mesh.shape["tensor"]),
        mesh=mesh,
        in_specs=(rows, rows, by_rows, by_rows) + params,
        out_specs=(rows, rows) + params,
        check_vma=False,
    )
```

```python
import functools
import math

import jax
import jax.numpy as jnp
import numpy as np
from jax import lax
from jax.experimental import pallas as pl
from jax.experimental.pallas import tpu as pltpu
from jax.sharding import PartitionSpec as P

D = 1024
HD = 64
FFE = 512
SEQ_LEN = 512
STEP = 10
CALLS = (((0, 2),), ((2, 3), (3, 4)))
GATHERS = ((0, 3), (3, 4))
QBLK = 256
SUB = 256
CHUNK = 256
SLOTS = 2560
DEEP = 8
PAIR = 2
HELD = 3072

NORM_EPS = 1e-05
ROPE_BASE = 10000.0
BETA_ONE = 0.9
BETA_TWO = 0.95
ADAM_EPS = 1e-08
LEARN_RATE = 0.1
WEIGHT_DECAY = 0.1
MASK_FILL = -1e30
SCALE = 1.0 / math.sqrt(HD)

bf16 = jnp.bfloat16
f32 = jnp.float32
ANY = pl.BlockSpec(memory_space=pl.ANY)
COST = pl.CostEstimate(flops=1, bytes_accessed=1, transcendentals=0)
HBM = pl.BlockSpec(memory_space=pltpu.HBM)
SMEM = pl.BlockSpec(memory_space=pltpu.SMEM)
VMEM = pl.BlockSpec(memory_space=pltpu.VMEM)


def dot(a, b):
    return jnp.dot(a, b, preferred_element_type=f32)


def dot_t(a, b):
    return lax.dot_general(a, b, (((1,), (1,)), ((), ())), preferred_element_type=f32)


def t_dot(a, b):
    return lax.dot_general(a, b, (((0,), (0,)), ((), ())), preferred_element_type=f32)


def rope_tables():
    half = HD // 2
    position = np.arange(SEQ_LEN, dtype=np.float32)
    exponent = np.arange(half, dtype=np.float32) * np.float32(-2.0 / HD)
    frequency = np.exp(exponent * np.float32(math.log(ROPE_BASE))).astype(np.float32)
    angle = (position[:, None] * frequency[None, :]).astype(np.float32)
    cosine = np.cos(angle).astype(np.float32)
    sine = np.sin(angle).astype(np.float32)
    return np.tile(cosine, (1, 4)), np.concatenate([-sine, sine, -sine, sine], axis=1)


def adam_update(master, first_moment, second_moment, gradient, decay_rate):
    first_new = BETA_ONE * first_moment + (1.0 - BETA_ONE) * gradient
    second_new = BETA_TWO * second_moment + (1.0 - BETA_TWO) * gradient * gradient
    first_fixed = first_new / (1.0 - BETA_ONE**STEP)
    second_fixed = second_new / (1.0 - BETA_TWO**STEP)
    master_new = master - LEARN_RATE * (
        first_fixed / (jnp.sqrt(second_fixed) + ADAM_EPS) + decay_rate * master
    )
    return (master_new, first_new, second_new)


def adam_change(first_moment, second_moment, gradient):
    first_new = BETA_ONE * first_moment + (1.0 - BETA_ONE) * gradient
    second_new = BETA_TWO * second_moment + (1.0 - BETA_TWO) * gradient * gradient
    first_fixed = first_new / (1.0 - BETA_ONE**STEP)
    second_fixed = second_new / (1.0 - BETA_TWO**STEP)
    change = -LEARN_RATE * (first_fixed / (jnp.sqrt(second_fixed) + ADAM_EPS))
    return (change, first_new, second_new)


def sum_received(received, nt):
    received = [part.astype(f32) for part in received]
    if nt != 4:
        return functools.reduce(jnp.add, received)
    x_first, x_last, y_first, y_last = received
    return jnp.concatenate([x_first + y_first, x_last + y_last], axis=0)


def rms_scale(values):
    return lax.rsqrt(jnp.mean(values * values, axis=-1, keepdims=True) + NORM_EPS)


def weight_spots(place_ref, nz, nt, relative):
    rows, cols = D // (2 * nz), D // nt
    z, core, t = place_ref[0], place_ref[1], place_ref[2]
    for c in range(2):
        for k in range(nt):
            for j in range(nz):
                row = pl.multiple_of(((z ^ j if relative else j) * 2 + (core ^ c)) * rows, rows)
                col = pl.multiple_of((t ^ k) * cols, cols)
                yield c, k, j, (pl.ds(row, rows), pl.ds(col, cols))


def gather_copies(place_ref, pieces, first, w_ref, sem, nz, nt):
    rows = D // (2 * nz)
    return [
        pltpu.make_async_copy(
            pieces[c * nt + k].at[j, (first + member) * rows : (first + member + 1) * rows, :],
            w_ref.at[(member,) + spot],
            sem.at[((c * nt + k) * nz + j) * w_ref.shape[0] + member],
        )
        for c, k, j, spot in weight_spots(place_ref, nz, nt, False)
        for member in range(w_ref.shape[0])
    ]


def rotate(x, cosine, sine, first_half):
    width = x.shape[-1]
    swapped = jnp.where(
        first_half, pltpu.roll(x, width - HD // 2, 1), pltpu.roll(x, HD // 2, 1)
    )
    return x * cosine + swapped * sine


def join_gains(parts, width):
    owners = parts.shape[0]
    both = jnp.sum(parts[:, :, :128].astype(f32), axis=1)
    lane = lax.broadcasted_iota(jnp.int32, (owners, 128), 1)
    owner = lax.broadcasted_iota(jnp.int32, (owners, D), 0)
    mine = lax.broadcasted_iota(jnp.int32, (owners, D), 1) // width == owner
    out = []
    for values in (both, pltpu.roll(both, 128 - width, 1)):
        values = jnp.where(lane < width, values, 0.0)
        shift = width
        while shift < 128:
            values = values + pltpu.roll(values, shift, 1)
            shift *= 2
        wide = jnp.concatenate([values] * (D // 128), axis=1)
        out.append(jnp.sum(jnp.where(mine, wide, 0.0), axis=0, keepdims=True))
    return jnp.concatenate(out, axis=0)


def attend_forward_kernel(nz, nt, place_ref, tokens_ref, cos_ref, sin_ref, *rest):
    pieces = rest[: 2 * nt]
    q_ref, kv_ref, o_ref, lse_ref, w_ref, gains_ref = rest[2 * nt : 2 * nt + 6]
    qlin_ref, kvlin_ref, parts_ref, sems, gain_sems = rest[2 * nt + 6 :]
    length = tokens_ref.shape[0]
    rows = D // (2 * nz)
    core, t = place_ref[1], place_ref[2]
    gain_copies = [
        pltpu.make_async_copy(
            pieces[c * nt + k].at[j, 2 * rows :, :],
            parts_ref.at[(j * 2 + (core ^ c)) * nt + (t ^ k)],
            gain_sems.at[(c * nt + k) * nz + j],
        )
        for c in range(2)
        for k in range(nt)
        for j in range(nz)
    ]
    for copy in gain_copies:
        copy.start()
    copies = gather_copies(place_ref, pieces, 0, w_ref, sems, nz, nt)
    for copy in copies:
        copy.start()
    lse_ref[...] = jnp.zeros_like(lse_ref)
    for copy in gain_copies:
        copy.wait()
    gains_ref[...] = join_gains(parts_ref[...], D // (2 * nz * nt))
    stream = tokens_ref[...].astype(f32)
    n1 = (stream * rms_scale(stream) * gains_ref[0:1, :]).astype(bf16)
    for copy in copies:
        copy.wait()
    qlin_ref[...] = dot(n1, w_ref[0])
    kvlin_ref[...] = dot(n1, w_ref[1])

    def group(g, carry):
        part = pl.ds(pl.multiple_of(g * 128, 128), 128)
        lane = lax.broadcasted_iota(jnp.int32, (length, 128), 1)
        low = lane < HD
        first_half = (lane & (HD // 2)) == 0
        cosine, sine = cos_ref[...], sin_ref[...]
        q = rotate(qlin_ref[:, part], cosine, sine, first_half)
        kv = kvlin_ref[:, part]
        kv = jnp.where(low, rotate(kv, cosine, sine, first_half), kv)
        q_ref[:, part] = q.astype(bf16)
        kv_ref[:, part] = kv.astype(bf16)
        vk = pltpu.roll(kv, HD, 1).astype(bf16)
        kv = kv.astype(bf16)
        heads = (
            (jnp.where(low, q * SCALE, 0.0).astype(bf16), kv, vk),
            (jnp.where(low, 0.0, q * SCALE).astype(bf16), vk, kv),
        )
        row = lax.broadcasted_iota(jnp.int32, (QBLK, QBLK), 0)
        column = lax.broadcasted_iota(jnp.int32, (QBLK, QBLK), 1)
        seen = column <= row
        for b in range(length // QBLK):
            rows = slice(b * QBLK, (b + 1) * QBLK)
            keys = (b + 1) * QBLK
            outs = []
            lses = lse_ref[rows, :]
            lane_b = lax.broadcasted_iota(jnp.int32, (QBLK, 128), 1)
            for h, (qh, key_side, value_side) in enumerate(heads):
                scores = jnp.where(seen, dot_t(qh[rows], key_side[rows]), MASK_FILL)
                if b > 0:
                    scores = jnp.concatenate([dot_t(qh[rows], key_side[: b * QBLK]), scores], axis=1)
                top = jnp.max(scores, axis=-1, keepdims=True)
                e = jnp.exp(scores - top)
                total = jnp.sum(e, axis=-1, keepdims=True)
                outs.append(dot(e.astype(bf16), value_side[:keys]) * (1.0 / total))
                lses = jnp.where(lane_b == 2 * g + h, top + jnp.log(total), lses)
            lse_ref[rows, :] = lses
            o_ref[rows, part] = jnp.where(lane_b < HD, outs[0], outs[1]).astype(bf16)
        return carry

    lax.fori_loop(0, D // 128, group, 0)


def attend_forward(mesh_sizes, place, tokens, pieces):
    nz, nt = mesh_sizes
    length = tokens.shape[0]
    cosine, sine = rope_tables()
    return pl.pallas_call(
        functools.partial(attend_forward_kernel, nz, nt),
        out_shape=(
            jax.ShapeDtypeStruct((length, D), bf16),
            jax.ShapeDtypeStruct((length, D), bf16),
            jax.ShapeDtypeStruct((length, D), bf16),
            jax.ShapeDtypeStruct((length, 128), f32),
            jax.ShapeDtypeStruct((2, D, D), bf16),
            jax.ShapeDtypeStruct((2, D), f32),
        ),
        in_specs=[SMEM] + [VMEM] * 3 + [ANY] * len(pieces),
        out_specs=[VMEM] * 6,
        scratch_shapes=[
            pltpu.VMEM((length, D), f32),
            pltpu.VMEM((length, D), f32),
            pltpu.VMEM((2 * nz * nt, 16, D // nt), bf16),
            pltpu.SemaphoreType.DMA((2 * nt * nz * 2,)),
            pltpu.SemaphoreType.DMA((2 * nt * nz,)),
        ],
        compiler_params=pltpu.CompilerParams(vmem_limit_bytes=40 * 2**20),
        cost_estimate=pl.CostEstimate(flops=25 * 10**9, bytes_accessed=12 * 2**20, transcendentals=4 * 2**20),
        name="attend_forward",
    )(place, tokens, jnp.asarray(cosine), jnp.asarray(sine), *pieces)


def attend_out_kernel(nz, nt, place_ref, tokens_ref, gains_ref, o_ref, *rest):
    pieces = rest[: 2 * nt]
    s1_ref, n2_ref, w_ref, sems = rest[2 * nt :]
    copies = gather_copies(place_ref, pieces, 0, w_ref, sems, nz, nt)
    for copy in copies:
        copy.start()
    for copy in copies:
        copy.wait()
    s1 = tokens_ref[...].astype(f32) + dot_t(o_ref[...], w_ref[0])
    s1_ref[...] = s1
    n2_ref[...] = (s1 * rms_scale(s1) * gains_ref[1:2, :]).astype(bf16)


def attend_out(mesh_sizes, place, tokens, gains, o, pieces):
    nz, nt = mesh_sizes
    length = tokens.shape[0]
    return pl.pallas_call(
        functools.partial(attend_out_kernel, nz, nt),
        out_shape=(
            jax.ShapeDtypeStruct((length, D), f32),
            jax.ShapeDtypeStruct((length, D), bf16),
            jax.ShapeDtypeStruct((1, D, D), bf16),
        ),
        in_specs=[SMEM] + [VMEM] * 3 + [ANY] * len(pieces),
        out_specs=[VMEM] * 3,
        scratch_shapes=[pltpu.SemaphoreType.DMA((2 * nt * nz,))],
        compiler_params=pltpu.CompilerParams(vmem_limit_bytes=32 * 2**20),
        cost_estimate=COST,
        name="attend_out",
    )(place, tokens, gains, o, *pieces)


def norm_backward(grad, stream, gain, given):
    inverse = rms_scale(stream)
    unit = stream * inverse
    scaled = grad * gain
    through = inverse * (scaled - unit * jnp.mean(scaled * unit, axis=-1, keepdims=True))
    return given + through, jnp.sum(grad * unit, axis=0, keepdims=True)


def attend_backward_kernel(nz, nt, whole, place_ref, tokens_ref, gains_ref, cos_ref, sin_ref, q_ref, kv_ref, o_ref, *rest):
    lse_ref, w_ref, wo_ref, rest = rest[0], rest[1], rest[2], rest[3:]
    da_ref, gain_two_ref, rest = rest[0], rest[1], rest[2:]
    if whole:
        gs1_ref, rest = rest[0], rest[1:]
    out_ref, own_ref, others, rest = rest[0], rest[1], rest[2 : 2 + nt], rest[2 + nt :]
    gw_ref, gg_ref, do_ref, dq_ref, dkv_ref, lse_t_ref, sems = rest
    length = tokens_ref.shape[0]
    rows, cols = D // (2 * nz), D // nt
    sides = ([own_ref.at[k] for k in range(nt)], others)
    da, gain_two = da_ref[...], gain_two_ref[...]

    def member_copies(members):
        return [
            pltpu.make_async_copy(
                gw_ref.at[(member,) + spot],
                sides[c][k].at[j, member * rows : (member + 1) * rows, :],
                sems.at[member, (c * nt + k) * nz + j],
            )
            for member in members
            for c, k, j, spot in weight_spots(place_ref, nz, nt, True)
        ]

    gw_ref[2] = t_dot(da, o_ref[...]).astype(bf16)
    first = member_copies((2,))
    for copy in first:
        copy.start()
    do_ref[...] = dot(da, wo_ref[0]).astype(bf16)
    lse_t_ref[...] = lse_ref[...].T

    def group(g, carry):
        part = pl.ds(pl.multiple_of(g * 128, 128), 128)
        lane = lax.broadcasted_iota(jnp.int32, (length, 128), 1)
        low = lane < HD
        first_half = (lane & (HD // 2)) == 0
        cosine, sine = cos_ref[...], sin_ref[...]
        q = q_ref[:, part].astype(f32)
        kv = kv_ref[:, part].astype(f32)
        do = do_ref[:, part].astype(f32)
        vk = pltpu.roll(kv, HD, 1).astype(bf16)
        kv = kv.astype(bf16)
        q_low = jnp.where(low, q, 0.0).astype(bf16)
        scaled_low = jnp.where(low, q * SCALE, 0.0).astype(bf16)
        scaled_high = jnp.where(low, 0.0, q * SCALE).astype(bf16)
        q_moved = jnp.where(low, pltpu.roll(q, HD, 1), 0.0).astype(bf16)
        do_low = jnp.where(low, do, 0.0).astype(bf16)
        do_high = jnp.where(low, 0.0, do).astype(bf16)
        do_moved = jnp.where(low, 0.0, pltpu.roll(do, HD, 1)).astype(bf16)
        heads = (
            (scaled_low, kv, vk, do_low, q_low, do_moved),
            (scaled_high, vk, kv, do_high, q_moved, do_high),
        )
        row = lax.broadcasted_iota(jnp.int32, (QBLK, QBLK), 0)
        column = lax.broadcasted_iota(jnp.int32, (QBLK, QBLK), 1)
        seen = row <= column
        blocks = length // QBLK
        dkv = [jnp.zeros((QBLK, 128), f32) for _ in range(blocks)]
        dqs = []
        for b in range(blocks):
            rows = slice(b * QBLK, (b + 1) * QBLK)
            keys = (b + 1) * QBLK
            both = []
            for h, (qh, key_side, value_side, doh, q_for_k, do_for_v) in enumerate(heads):
                scores = jnp.where(seen, dot_t(key_side[rows], qh[rows]), MASK_FILL)
                if b > 0:
                    scores = jnp.concatenate([dot_t(key_side[: b * QBLK], qh[rows]), scores], axis=0)
                e = jnp.exp(scores - lse_t_ref[pl.ds(2 * g + h, 1), rows])
                dp = dot_t(value_side[:keys], doh[rows])
                mean = jnp.sum(e * dp, axis=0, keepdims=True)
                dz = (e * (dp - mean)).astype(bf16)
                both.append(t_dot(key_side[:keys], dz))
                add = dot(dz, q_for_k[rows]) + dot(e.astype(bf16), do_for_v[rows])
                for i in range(b + 1):
                    dkv[i] = dkv[i] + add[i * QBLK : (i + 1) * QBLK]
            dqs.append(jnp.concatenate([both[0][:HD], both[1][HD:]], axis=0))
        dq = jnp.concatenate(dqs, axis=1).T * SCALE
        dkv_all = jnp.concatenate(dkv, axis=0)
        dq_ref[:, part] = rotate(dq, cosine, -sine, first_half).astype(bf16)
        dk = rotate(dkv_all * SCALE, cosine, -sine, first_half)
        dkv_ref[:, part] = jnp.where(low, dk, dkv_all).astype(bf16)
        return carry

    lax.fori_loop(0, D // 128, group, 0)
    stream = tokens_ref[...].astype(f32)
    n1 = (stream * rms_scale(stream) * gains_ref[0:1, :]).astype(bf16)
    gw_ref[0] = t_dot(n1, dq_ref[...]).astype(bf16)
    gw_ref[1] = t_dot(n1, dkv_ref[...]).astype(bf16)
    second = member_copies((0, 1))
    for copy in second:
        copy.start()
    dn1 = dot_t(dq_ref[...], w_ref[0]) + dot_t(dkv_ref[...], w_ref[1])
    input_grad, gain_one = norm_backward(dn1, stream, gains_ref[0:1, :], gs1_ref[...] if whole else 0.0)
    out_ref[...] = input_grad if whole else dn1
    gg_ref[...] = jnp.zeros_like(gg_ref)
    for i in range(nt):
        gg_ref[i : i + 1, :] = gain_one[:, i * cols : (i + 1) * cols].astype(bf16)
        gg_ref[nt + i : nt + i + 1, :] = gain_two[:, i * cols : (i + 1) * cols].astype(bf16)
    third = [
        pltpu.make_async_copy(gg_ref, sides[c][k].at[j, 3 * rows :, :], sems.at[3, (c * nt + k) * nz + j])
        for c in range(2)
        for k in range(nt)
        for j in range(nz)
    ]
    for copy in third:
        copy.start()
    for copy in first + second + third:
        copy.wait()


def attend_backward(mesh_sizes, whole, place, tokens, gains, q, kv, o, lse, weights, out_weight, *given):
    nz, nt = mesh_sizes
    length = tokens.shape[0]
    cosine, sine = rope_tables()
    part = (nz, 3 * D // (2 * nz) + 16, D // nt)
    out = pl.pallas_call(
        functools.partial(attend_backward_kernel, nz, nt, whole),
        out_shape=[jax.ShapeDtypeStruct((length, D), f32), jax.ShapeDtypeStruct((nt,) + part, bf16)]
        + [jax.ShapeDtypeStruct(part, bf16)] * nt,
        in_specs=[SMEM] + [VMEM] * (10 + len(given)),
        out_specs=[VMEM] + [ANY] * (1 + nt),
        scratch_shapes=[
            pltpu.VMEM((3, D, D), bf16),
            pltpu.VMEM((16, D // nt), bf16),
            pltpu.VMEM((length, D), bf16),
            pltpu.VMEM((length, D), bf16),
            pltpu.VMEM((length, D), bf16),
            pltpu.VMEM((128, length), f32),
            pltpu.SemaphoreType.DMA((4, 2 * nt * nz)),
        ],
        compiler_params=pltpu.CompilerParams(vmem_limit_bytes=60 * 2**20),
        cost_estimate=COST,
        name="attend_backward",
    )(
        place, tokens, gains, jnp.asarray(cosine), jnp.asarray(sine), q, kv, o, lse, weights, out_weight, *given
    )
    return out[0], out[1], out[2:]


def gather_kernel(starts, experts, with_c, offs_ref, pos_ref, *rest):
    tiles = len(starts) - 1
    if with_c:
        c_ref, rest = rest[0], rest[1:]
    parts, rest = rest[:tiles], rest[tiles:]
    outs, rest = rest[: 1 + with_c], rest[1 + with_c :]
    held, (buf, in_sems, out_sems) = rest[: 1 + with_c], rest[1 + with_c :]
    subs = starts[-1] // SUB

    def block_copy(s):
        j = max(i for i in range(tiles) if starts[i] <= s * SUB)
        return pltpu.make_async_copy(
            parts[j].at[pl.ds(s * SUB - starts[j], SUB)], buf.at[s % DEEP], in_sems.at[s % DEEP]
        )

    def flush(e, chunk):
        spot = pl.ds(pl.multiple_of(chunk * CHUNK, CHUNK), CHUNK)
        return [
            pltpu.make_async_copy(slots.at[e, spot, :], out.at[e, spot, :], out_sems.at[i, e, chunk])
            for i, (slots, out) in enumerate(zip(held, outs))
        ]

    for s in range(DEEP - 1):
        block_copy(s).start()

    def block(s, carry):
        for ahead in range(DEEP - 1, subs):

            @pl.when(s + DEEP - 1 == ahead)
            def _():
                block_copy(ahead).start()

        slot = lax.rem(s, DEEP)
        begin = [offs_ref[e * (subs + 1) + s] for e in range(experts)]
        end = [offs_ref[e * (subs + 1) + s + 1] for e in range(experts)]
        most = functools.reduce(jnp.maximum, [end[e] - begin[e] for e in range(experts)])
        pltpu.make_async_copy(parts[0].at[pl.ds(0, SUB)], buf.at[slot], in_sems.at[slot]).wait()

        def fill(count):
            slots = lax.broadcasted_iota(jnp.int32, (count, SUB), 0).astype(f32)
            spots = [pl.ds(pl.multiple_of(begin[e], 16), count) for e in range(experts)]
            picks = []
            for e in range(experts):
                hit = slots == pos_ref[pl.ds(e * subs + s, 1), :]
                picks.append(jnp.where(hit, 1.0, 0.0).astype(bf16))
                if with_c:
                    c = jnp.sum(jnp.where(hit, c_ref[pl.ds(e * subs + s, 1), :], 0.0), axis=1, keepdims=True)
                    held[1][e, spots[e], :] = jnp.broadcast_to(c, (count, 128))
            rows = dot(jnp.concatenate(picks, axis=0), buf[slot]).astype(bf16)
            for e in range(experts):
                held[0][e, spots[e], :] = rows[e * count : (e + 1) * count]

        @pl.when(most <= SUB // 2)
        def _():
            fill(SUB // 2)

        @pl.when(most > SUB // 2)
        def _():
            fill(SUB)

        for e in range(experts):

            @pl.when(end[e] // CHUNK > begin[e] // CHUNK)
            def _():
                for copy in flush(e, begin[e] // CHUNK):
                    copy.start()

        return carry

    lax.fori_loop(0, subs, block, 0)
    for e in range(experts):
        total = offs_ref[e * (subs + 1) + subs]
        tail = pl.ds(pl.multiple_of(total, 16), CHUNK)
        for slots in held:
            slots[e, tail, :] = jnp.zeros((CHUNK, slots.shape[2]), slots.dtype)
        for copy in flush(e, total // CHUNK):
            copy.start()
    for e in range(experts):

        def drain(chunk, carry):
            for copy in flush(e, chunk):
                copy.wait()
            return carry

        lax.fori_loop(0, offs_ref[e * (subs + 1) + subs] // CHUNK + 1, drain, 0)


def gather(parts, offs, pos, c=None):
    starts = [0]
    for part in parts:
        starts.append(starts[-1] + part.shape[0])
    experts = pos.shape[0] * SUB // starts[-1]
    with_c = c is not None
    held = [((experts, SLOTS, D), bf16)] + [((experts, SLOTS, 128), f32)] * with_c
    return pl.pallas_call(
        functools.partial(gather_kernel, tuple(starts), experts, with_c),
        out_shape=[jax.ShapeDtypeStruct(*kind) for kind in held],
        in_specs=[SMEM, VMEM] + [VMEM] * with_c + [HBM] * len(parts),
        out_specs=[HBM] * len(held),
        scratch_shapes=[pltpu.VMEM(*kind) for kind in held]
        + [
            pltpu.VMEM((DEEP, SUB, D), bf16),
            pltpu.SemaphoreType.DMA((DEEP,)),
            pltpu.SemaphoreType.DMA((1 + with_c, experts, SLOTS // CHUNK)),
        ],
        compiler_params=pltpu.CompilerParams(vmem_limit_bytes=62 * 2**20),
        cost_estimate=COST,
        name="gather_rows",
    )(offs, pos, *([c] if with_c else []), *parts)


def experts_kernel(first, subs, sources, kept, place_ref, offs_ref, n2_ref, dm_ref, c_ref, *rest):
    arrays = 1 + sources[-1][0]
    weights, rest = rest[:arrays], rest[arrays + kept :]
    m_ref, d_ref, gw_ref = rest[:3]
    win_buf, wdown_buf, n2_in, dm_in, c_in, m_out, d_out, zeros, gin, gdown, w_sems, in_sems, out_sems = rest[3:]
    e = pl.program_id(0)
    nz, cores, _, wrows, _ = gw_ref.shape
    rin, rdown = D // (nz * cores), FFE // (nz * cores)
    core = place_ref[1]
    total = offs_ref[(first + e) * (subs + 1) + subs]
    chunks = jnp.maximum((total + CHUNK - 1) // CHUNK, 1)

    def weight_copies(index):
        i, place = sources[index]
        slot = index % 2
        expert = core * (weights[i].shape[1] // 2) + place
        return [
            pltpu.make_async_copy(weights[i].at[:, expert, spot, :], buf.at[slot], w_sems.at[j, slot])
            for j, (spot, buf) in enumerate(((slice(0, rin), win_buf), (slice(rin, wrows), wdown_buf)))
        ]

    def in_copies(e, k, slot):
        spot = pl.ds(pl.multiple_of(k * CHUNK, CHUNK), CHUNK)
        return [
            pltpu.make_async_copy(source.at[first + e, spot, :], target.at[slot], in_sems.at[i, slot])
            for i, (source, target) in enumerate(((n2_ref, n2_in), (dm_ref, dm_in), (c_ref, c_in)))
        ]

    def out_copies(k, slot):
        spot = pl.ds(pl.multiple_of(k * CHUNK, CHUNK), CHUNK)
        return (
            pltpu.make_async_copy(m_out.at[slot], m_ref.at[e, spot, :], out_sems.at[0, slot]),
            pltpu.make_async_copy(d_out.at[slot], d_ref.at[e, spot, :], out_sems.at[1, slot]),
        )

    @pl.when(e == 0)
    def _():
        for copy in in_copies(e, 0, 0) + weight_copies(0):
            copy.start()
        zeros[...] = jnp.zeros_like(zeros)

    for index in range(len(sources)):

        @pl.when(e == index)
        def _():
            for copy in weight_copies(index):
                copy.wait()
            if index + 1 < len(sources):
                for copy in weight_copies(index + 1):
                    copy.start()

    at = lax.rem(e, 2)

    def one_chunk(k, carry):
        slot = lax.rem(k, 2)
        for copy in in_copies(e, k, slot):
            copy.wait()

        @pl.when(k + 1 < chunks)
        def _():
            for copy in in_copies(e, k + 1, 1 - slot):
                copy.start()

        @pl.when(k >= 2)
        def _():
            for copy in out_copies(k - 2, slot):
                copy.wait()

        win = win_buf[at].reshape(D, D)
        wdown = wdown_buf[at].reshape(FFE, D)
        n2, dm, c = n2_in[slot], dm_in[slot], c_in[slot][:, 0:1]
        hidden = dot(n2, win)
        gate, up = hidden[:, :FFE], hidden[:, FFE:]
        sigma = jax.nn.sigmoid(gate)
        silu = gate * sigma
        active = (c * silu * up).astype(bf16)
        m_out[slot] = dot(active, wdown).astype(bf16)
        gdown[...] = jnp.where(k == 0, 0.0, gdown[...]) + dot(active.T, dm)
        da = c * dot_t(dm, wdown)
        dgate = da * up * (sigma + silu * (1.0 - sigma))
        dup = da * silu
        dh = jnp.concatenate([dgate.astype(bf16), dup.astype(bf16)], axis=1)
        gin[...] = jnp.where(k == 0, 0.0, gin[...]) + dot(n2.T, dh)
        d_out[slot] = dot_t(dh, win).astype(bf16)
        for copy in out_copies(k, slot):
            copy.start()
        return carry

    lax.fori_loop(0, chunks, one_chunk, 0)

    @pl.when(e + 1 < len(sources))
    def _():
        for copy in in_copies(e + 1, 0, 0):
            copy.start()

    spot = pl.ds(pl.multiple_of(chunks * CHUNK, CHUNK), CHUNK)
    ends = (
        pltpu.make_async_copy(zeros, m_ref.at[e, spot, :], out_sems.at[0, 2]),
        pltpu.make_async_copy(zeros, d_ref.at[e, spot, :], out_sems.at[1, 2]),
    )
    for copy in ends:
        copy.start()
    for j in range(nz):
        for side in range(2):
            owner = 2 * j + (core ^ side)
            at_in, at_down = pl.multiple_of(owner * rin, rin), pl.multiple_of(owner * rdown, rdown)
            gw_ref[j, side, 0, :rin, :] = gin[pl.ds(at_in, rin), :].astype(bf16)
            gw_ref[j, side, 0, rin:, :] = gdown[pl.ds(at_down, rdown), :].astype(bf16)
    for copy in ends:
        copy.wait()
    for back in (1, 2):

        @pl.when(chunks >= back)
        def _():
            for copy in out_copies(chunks - back, lax.rem(chunks - back, 2)):
                copy.wait()


def experts_step(place, slots, offs, first, weights, sources, before, spot, count):
    owners, _, wrows, _ = weights[0].shape
    nz, cores = owners // 2, 2
    experts = len(sources)
    rin, rdown = D // (nz * cores), FFE // (nz * cores)
    part = jax.ShapeDtypeStruct((experts, HELD, D), bf16)
    kept = [] if before is None else [before]
    subs = offs.shape[1] - 1
    return pl.pallas_call(
        functools.partial(experts_kernel, first, subs, sources, len(kept)),
        grid=(experts,),
        out_shape=(part, part, jax.ShapeDtypeStruct((nz, cores, count, wrows, D), bf16)),
        in_specs=[SMEM, SMEM] + [HBM] * (3 + len(weights) + len(kept)),
        out_specs=(HBM, HBM, pl.BlockSpec((nz, cores, 1, wrows, D), lambda e: (0, 0, spot + e, 0, 0))),
        scratch_shapes=[
            pltpu.VMEM((2, owners, rin, D), bf16),
            pltpu.VMEM((2, owners, rdown, D), bf16),
            pltpu.VMEM((2, CHUNK, D), bf16),
            pltpu.VMEM((2, CHUNK, D), bf16),
            pltpu.VMEM((2, CHUNK, 128), f32),
            pltpu.VMEM((2, CHUNK, D), bf16),
            pltpu.VMEM((2, CHUNK, D), bf16),
            pltpu.VMEM((CHUNK, D), bf16),
            pltpu.VMEM((D, D), f32),
            pltpu.VMEM((FFE, D), f32),
            pltpu.SemaphoreType.DMA((2, 2)),
            pltpu.SemaphoreType.DMA((3, 2)),
            pltpu.SemaphoreType.DMA((2, 3)),
        ],
        input_output_aliases={5 + len(weights): 2} if kept else {},
        compiler_params=pltpu.CompilerParams(
            vmem_limit_bytes=60 * 2**20, dimension_semantics=("arbitrary",)
        ),
        cost_estimate=COST,
        name="experts",
    )(place, offs.reshape(-1), *slots, *weights, *kept)


def scatter_kernel(halves, sources, experts, subs, offs_ref, pos_ref, *rest):
    arrays = 1 + sources[-1][1]
    parts, rest = rest[:arrays], rest[arrays:]
    outs, (slots, sems) = rest[: len(halves)], rest[len(halves) :]
    i, steps = pl.program_id(0), subs // (2 * PAIR)
    first = lax.rem(i * PAIR + halves[0] * (subs // 2), subs)

    half = subs // 2

    def each(low, high, act):
        for spot, (e, array, index) in enumerate(sources):

            def one(chunk, carry):
                rows = pl.ds(pl.multiple_of(chunk * CHUNK, CHUNK), CHUNK)
                act(pltpu.make_async_copy(parts[array].at[index, rows, :], slots.at[spot, rows, :], sems.at[spot, chunk]))
                return carry

            lax.fori_loop(*spans(e, low, high), one, 0)

    def spans(e, low, high):
        middle = offs_ref[e * (subs + 1) + half] // CHUNK
        last_low = (offs_ref[e * (subs + 1) + low] + CHUNK - 1) // CHUNK + 1
        begin = jnp.where(lax.rem(low, half) == 0, offs_ref[e * (subs + 1) + low] // CHUNK, last_low)
        end = (offs_ref[e * (subs + 1) + high] + CHUNK - 1) // CHUNK + 1
        if len(halves) == 2:
            early = jnp.asarray(low) < half
            begin = jnp.where(early, jnp.minimum(begin, middle), begin)
            end = jnp.where(early, jnp.minimum(end, middle), end)
        return begin, end

    @pl.when(i == 0)
    def _():
        for h in halves:
            each(h * half, (h + 1) * half, lambda copy: copy.start())

    each(first, first + PAIR, lambda copy: copy.wait())
    lane = lax.broadcasted_iota(jnp.int32, (SUB, SUB), 1).astype(f32)
    totals = []
    for p in range(PAIR):
        picks = [
            jnp.where(lane == pos_ref[p * SUB : (p + 1) * SUB, e : e + 1], 1.0, 0.0).astype(bf16) for e, _, _ in sources
        ]
        windows = [
            slots[spot, pl.ds(pl.multiple_of(offs_ref[e * (subs + 1) + first + p], 16), SUB), :]
            for spot, (e, _, _) in enumerate(sources)
        ]
        totals.append(dot(jnp.concatenate(picks, axis=1), jnp.concatenate(windows, axis=0)).astype(bf16))
    for j, out_ref in enumerate(outs):

        @pl.when(i // steps == j)
        def _():
            for p in range(PAIR):
                out_ref[p * SUB : (p + 1) * SUB, :] = totals[p]


def scatter(offs, pos_columns, parts, halves):
    tokens, experts = pos_columns.shape
    sources = [
        (first + index, i, index) for i, (part, first) in enumerate(parts) for index in range(part.shape[0])
    ]
    subs = tokens // SUB
    steps = subs // (2 * PAIR)
    shift = halves[0] * steps
    blocks = [
        pl.BlockSpec((PAIR * SUB, D), lambda i, j=j: (jnp.clip(i - j * steps, 0, steps - 1), 0))
        for j in range(len(halves))
    ]
    return pl.pallas_call(
        functools.partial(scatter_kernel, halves, sources, experts, subs),
        grid=(len(halves) * steps,),
        out_shape=[jax.ShapeDtypeStruct((tokens // 2, D), bf16)] * len(halves),
        in_specs=[SMEM, pl.BlockSpec((PAIR * SUB, experts), lambda i: (lax.rem(i + shift, 2 * steps), 0))]
        + [HBM] * len(parts),
        out_specs=blocks,
        scratch_shapes=[
            pltpu.VMEM((len(sources), HELD, D), bf16),
            pltpu.SemaphoreType.DMA((len(sources), HELD // CHUNK)),
        ],
        compiler_params=pltpu.CompilerParams(
            vmem_limit_bytes=60 * 2**20, dimension_semantics=("arbitrary",)
        ),
        cost_estimate=COST,
        name="scatter_rows",
    )(offs.reshape(-1), pos_columns, *[part for part, _ in parts])


def adam_kernel(per, place_ref, mine_ref, recv_ref, *rest):
    states, news = rest[:6], rest[-6:]
    here = pl.program_id(0) // per == place_ref[1]
    grad = jnp.where(here, mine_ref[0, 0], recv_ref[0]).astype(f32)
    rin = states[0].shape[2]
    for i, part in ((0, grad[:rin]), (3, grad[rin:])):
        masters = [ref[0, 0] for ref in states[i : i + 3]]
        for ref, new in zip(news[i : i + 3], adam_update(*masters, part, WEIGHT_DECAY)):
            ref[0, 0] = new


def adam_experts(place, a, mine, recv, states, before):
    experts, rin = states[0].shape[1:3]
    rdown = states[3].shape[2]
    per = recv.shape[0]
    half = experts // 2
    spec = [
        pl.BlockSpec((1, 1, r, D), lambda i, place: (0, i // per * half + a + i % per, 0, 0))
        for r in (rin, rdown)
    ]
    specs = [spec[0]] * 3 + [spec[1]] * 3
    kept = [] if before is None else list(before)
    return pl.pallas_call(
        functools.partial(adam_kernel, per),
        grid_spec=pltpu.PrefetchScalarGridSpec(
            num_scalar_prefetch=1,
            grid=(2 * per,),
            in_specs=[
                pl.BlockSpec((1, 1, rin + rdown, D), lambda i, place: (0, i % per, 0, 0)),
                pl.BlockSpec((1, rin + rdown, D), lambda i, place: (i % per, 0, 0)),
            ]
            + specs
            + [HBM] * len(kept),
            out_specs=specs,
        ),
        out_shape=[jax.ShapeDtypeStruct(state.shape, f32) for state in states],
        input_output_aliases={9 + i: i for i in range(len(kept))},
        compiler_params=pltpu.CompilerParams(
            vmem_limit_bytes=60 * 2**20, dimension_semantics=("arbitrary",)
        ),
        cost_estimate=COST,
        name="adam_experts",
    )(place, mine, recv, *states, *kept)


def adam_rest_kernel(scale, place_ref, mine_ref, *rest):
    count = len(rest) - 25
    received, states, news, (grad_ref,) = rest[:count], rest[count : count + 12], rest[count + 12 : count + 24], rest[-1:]
    total = mine_ref[...]
    for part in received:
        total = total + part[...].astype(f32)
    grad_ref[...] = total * scale
    rows, cols = states[0].shape[1:]
    width = states[9].shape[2]
    for i, turned in ((0, False), (1, False), (2, True)):
        part = grad_ref[i * rows : (i + 1) * rows, :]
        refs = slice(3 * i, 3 * i + 3)
        masters = [ref[0] for ref in states[refs]]
        for ref, new in zip(news[refs], adam_update(*masters, part.T if turned else part, WEIGHT_DECAY)):
            ref[0] = new
    start = place_ref[3] * width
    for i in range(2):
        row = grad_ref[pl.ds(3 * rows + i * (D // cols) + start // cols, 1), :]
        part = pltpu.roll(row, lax.rem(cols - lax.rem(start, cols), cols), 1)[:, :width]
        moments = [ref[0, i : i + 1, :] for ref in states[9:11]]
        for ref, new in zip(news[9:], adam_change(*moments, part)):
            ref[0, i : i + 1, :] = new


def adam_rest(place, scale, mine, received, states):
    return pl.pallas_call(
        functools.partial(adam_rest_kernel, scale),
        out_shape=[jax.ShapeDtypeStruct(state.shape, f32) for state in states],
        in_specs=[SMEM] + [VMEM] * (1 + len(received) + len(states)),
        out_specs=[VMEM] * len(states),
        scratch_shapes=[pltpu.VMEM(mine.shape, f32)],
        compiler_params=pltpu.CompilerParams(vmem_limit_bytes=32 * 2**20),
        cost_estimate=COST,
        name="adam_rest",
    )(place, mine, *received, *states)


def on_device(
    ndp,
    nt,
    tokens,
    cotangent,
    routes,
    gate_weights,
    norm_gains,
    norm_gains_first,
    norm_gains_second,
    query_weight,
    query_first,
    query_second,
    keyval_weight,
    keyval_first,
    keyval_second,
    output_weight,
    output_first,
    output_second,
    expert_in,
    expert_in_first,
    expert_in_second,
    expert_down,
    expert_down_first,
    expert_down_second,
):
    nz = ndp // 2
    place_dp = lax.axis_index("dp")
    t = lax.axis_index("tensor")
    z, core = place_dp // 2, place_dp % 2
    place = jnp.stack([z, core, t, place_dp * nt + t]).astype(jnp.int32)
    rows = tokens.shape[0]
    sharers = max(1, SEQ_LEN // rows)

    def swap_core(x):
        return lax.ppermute(x, "dp", [(i, i ^ 1) for i in range(ndp)])

    def swap_z(x, j):
        return lax.ppermute(x, "dp", [(i, i ^ (2 * j)) for i in range(ndp)])

    def swap_t(x, k):
        return lax.ppermute(x, "tensor", [(i, i ^ k) for i in range(nt)])

    def spread_t(x):
        return [x] + [swap_t(x, k) for k in range(1, nt)]

    def spread_z(x):
        return [x] + [swap_z(x, j) for j in range(1, nz)]

    def after(x, *others):
        return lax.optimization_barrier((x,) + others)[0]

    def near(x):
        return [swap_t(x, k) for k in range(1, nt)] if nt != 4 else [swap_t(x, 1), swap_t(x, 2)]

    def far(x, others):
        mid = x.shape[0] // 2
        return [] if nt != 4 else [swap_t(others[0][:mid], 2), swap_t(others[1][mid:], 1)]

    width = norm_gains.shape[2]
    wrows, wcols = query_weight.shape[1:]
    high = lax.reduce_precision(norm_gains[0], 8, 7)
    middle = lax.reduce_precision(norm_gains[0] - high, 8, 7)
    gain_rows = jnp.stack([high, middle, norm_gains[0] - high - middle]).astype(bf16).reshape(3, 2 * width)
    own = jnp.concatenate(
        [
            query_weight[0].astype(bf16),
            keyval_weight[0].astype(bf16),
            jnp.pad(gain_rows, ((0, 13), (0, wcols - 2 * width))),
            output_weight[0].T.astype(bf16),
        ],
        axis=0,
    )
    half = expert_in.shape[1] // 2
    groups = [[2 * i + c for i in range(nz)] for c in range(2)]

    def cut(quarters):
        return quarters[0] * half // 4, quarters[1] * half // 4

    def shard(a, b):
        low = [
            jnp.concatenate([w[0, a:b], w[0, half + a : half + b]]).astype(bf16) for w in (expert_in, expert_down)
        ]
        return jnp.concatenate(low, axis=1)

    spans = [cut(quarters) for quarters in GATHERS]
    spans = [(a, b) for a, b in spans if a < b]
    shards = [shard(*spans[0])]
    for a, b in spans[1:]:
        shards.append(shard(a, b))
    column = lax.all_gather(own, "dp", axis=0, tiled=False, axis_index_groups=groups)
    held = {}
    for (a, b), part in zip(spans, shards):
        whole = lax.all_gather(part, "dp", axis=0, tiled=False)
        held.update({i: (whole, i - a) for i in range(a, b)})
    dm_near = near(cotangent)
    pieces = spread_t(after(column[:, : 2 * wrows + 16], *dm_near))
    pieces_out = spread_t(after(column[:, 2 * wrows + 16 :], *pieces[1:]))
    dm_far = far(cotangent, list(lax.optimization_barrier((*dm_near, *pieces[1:])))[: len(dm_near)])
    pieces = pieces + [swap_core(piece) for piece in pieces]

    ids = t * 2 * half + jnp.arange(2 * half, dtype=jnp.int32)
    chosen = routes[0].T[None, :, :] == ids[:, None, None]
    c_all = jnp.sum(jnp.where(chosen, gate_weights[0].T[None, :, :], 0.0), axis=1)
    c_mine = lax.dynamic_slice_in_dim(c_all, core * half, half, 0)
    c_got = swap_core(lax.dynamic_slice_in_dim(c_all, (1 - core) * half, half, 0))
    c_both = jnp.stack([c_mine, c_got], axis=1).reshape(half, 2, nt, rows)
    c_both = jnp.take(c_both, jnp.arange(nt, dtype=jnp.int32) ^ t, axis=2)
    subs = 2 * nt * rows // SUB
    c_rows = c_both.reshape(half * subs, SUB)
    taken = c_rows != 0.0
    upto = lax.broadcasted_iota(jnp.int32, (SUB, SUB), 0) <= lax.broadcasted_iota(jnp.int32, (SUB, SUB), 1)
    rank = dot(taken.astype(bf16), upto.astype(bf16))
    pos = jnp.where(taken, rank - 1.0, -1.0)
    sizes = (rank[:, SUB - 1].astype(jnp.int32).reshape(half, subs) + 15) // 16 * 16
    offs = jnp.pad(jnp.cumsum(sizes, axis=1), ((0, 0), (1, 0)))
    pos_columns = pos.reshape(half, subs * SUB).T

    sequence = after(tokens, offs, pos, c_rows, pos_columns)
    if sharers > 1:
        seq_groups = [list(range(i, i + sharers)) for i in range(0, nt, sharers)]
        sequence = lax.all_gather(tokens, "tensor", axis=0, tiled=True, axis_index_groups=seq_groups)
    first_row = (t % sharers) * rows
    q, kv, o, lse, qkv_weights, gains = attend_forward((nz, nt), place, sequence, pieces)
    o, *pieces_out = lax.optimization_barrier((o, *pieces_out))
    pieces_out = pieces_out + [swap_core(piece) for piece in pieces_out]
    s1, n2, out_weight = attend_out((nz, nt), place, sequence, gains, o, pieces_out)
    if sharers > 1:
        s1 = lax.dynamic_slice_in_dim(s1, first_row, rows, 0)
        n2 = lax.dynamic_slice_in_dim(n2, first_row, rows, 0)

    n2_near = near(n2)
    n2_far = far(n2, n2_near)
    n2_own = [n2] + n2_near
    dm_own = [cotangent] + dm_near + dm_far
    dm_parts = dm_own + [swap_core(part) for part in dm_own]
    dm_slots, c_slots = gather(dm_parts, offs.reshape(-1), pos, c_rows)
    dm_slots, c_slots, *n2_far = lax.optimization_barrier((dm_slots, c_slots, *n2_far))
    n2_own = n2_own + n2_far
    n2_parts = n2_own + [swap_core(part) for part in n2_own]
    (n2_slots,) = gather(n2_parts, offs.reshape(-1), pos)
    slots = (n2_slots, dm_slots, c_slots)
    m_parts, d_parts, expert_grads = [], [], []
    for calls in CALLS:
        start, stop = cut((calls[0][0], calls[-1][1]))
        gw = None
        for quarters in calls:
            a, b = cut(quarters)
            if a == b:
                continue
            arrays, sources = [], []
            for i in range(a, b):
                array, index = held[i]
                if not arrays or arrays[-1] is not array:
                    arrays.append(array)
                sources.append((len(arrays) - 1, index))
            m_part, d_part, gw = experts_step(
                place, slots, offs, a, arrays, tuple(sources), gw, a - start, stop - start
            )
            m_parts.append((m_part, a))
            d_parts.append((d_part, a))
        grad = lax.psum_scatter(gw, "dp", scatter_dimension=0, tiled=False, axis_index_groups=groups)
        expert_grads.append((start, grad))

    def both_cores(own, other):
        both = [
            own[k * rows : (k + 1) * rows].astype(f32) + other[k * rows : (k + 1) * rows].astype(f32)
            for k in range(nt)
        ]
        return both[0], [part.astype(bf16) for part in both[1:]]

    def to_tokens(parts, last=()):
        if nt != 4:
            return [swap_t(parts[k], k) for k in range(1, nt)], parts[1:]
        mid = parts[3].shape[0] // 2
        by_x, by_y = swap_t(parts[3][:mid], 1), swap_t(parts[3][mid:], 2)
        x_first, y_last = swap_t(parts[1][:mid], 1), swap_t(parts[2][mid:], 2)
        by_x, by_y, *_ = lax.optimization_barrier((by_x, by_y, *last))
        x_part = (parts[1][mid:].astype(f32) + by_y.astype(f32)).astype(bf16)
        y_part = (parts[2][:mid].astype(f32) + by_x.astype(f32)).astype(bf16)
        return [x_first, swap_t(x_part, 1), swap_t(y_part, 2), y_last], (x_part, y_part)

    (d_other,) = scatter(offs, pos_columns, d_parts, (1,))
    (d_own,) = scatter(offs, pos_columns, d_parts, (0,))
    d_own, d_sent = both_cores(d_own, swap_core(d_other))
    def to_owners(parts, meanwhile):
        if nt != 4:
            return sum_received([swap_t(parts[k], k) for k in range(1, nt)], nt), meanwhile
        mid = parts[3].shape[0] // 2
        by_x = swap_t(jnp.concatenate([parts[3][:mid], parts[1][:mid]]), 1)
        by_y = swap_t(jnp.concatenate([parts[3][mid:], parts[2][mid:]]), 2)
        by_x, by_y, meanwhile = lax.optimization_barrier((by_x, by_y, meanwhile))
        x_last = swap_t((parts[1][mid:].astype(f32) + by_y[:mid].astype(f32)).astype(bf16), 1)
        y_first = swap_t((parts[2][:mid].astype(f32) + by_x[:mid].astype(f32)).astype(bf16), 2)
        return sum_received([by_x[mid:], x_last, y_first, by_y[mid:]], nt), meanwhile

    d_received, d_last = to_tokens([None] + d_sent)
    m_pos = after(pos_columns, *d_last)
    m_other, m_own = scatter(offs, m_pos, m_parts, (1, 0))
    m_other = jnp.concatenate([swap_core(m_other[k * rows : (k + 1) * rows]) for k in range(nt)])
    m_own, m_sent = both_cores(m_own, m_other)

    whole = sharers == 1
    gs1, gain_two = norm_backward(d_own + sum_received(d_received, nt), s1, gains[1:2], cotangent.astype(f32))
    da, *m_sent = lax.optimization_barrier((gs1.astype(bf16), *m_sent))
    if nt == 4:
        mid = rows // 2
        m_step = [swap_t(m_sent[2][:mid], 1), swap_t(m_sent[2][mid:], 2)]
        m_step += [swap_t(m_sent[0][:mid], 1), swap_t(m_sent[1][mid:], 2)]
    else:
        m_step = [swap_t(part, k + 1) for k, part in enumerate(m_sent)]
    if not whole:
        da = lax.all_gather(da, "tensor", axis=0, tiled=True, axis_index_groups=seq_groups)
    input_grad, grads_own, grads_other = attend_backward(
        (nz, nt), whole, place, sequence, gains, q, kv, o, lse, qkv_weights, out_weight,
        da, gain_two * sharers, *([gs1] if whole else []),
    )
    if not whole:
        dn1 = lax.dynamic_slice_in_dim(input_grad, first_row, rows, 0)
        input_grad, _ = norm_backward(dn1, tokens.astype(f32), gains[0], gs1)

    grads_other, m_step = lax.optimization_barrier((grads_other, m_step))
    swapped = [swap_core(part) for part in grads_other]
    both = [(grads_own[k].astype(f32) + swapped[k].astype(f32)).astype(bf16) for k in range(nt)]
    if nt == 4:
        by_x, by_y, x_first, y_last = m_step
        by_x, by_y, *_ = lax.optimization_barrier((by_x, by_y, grads_own))
        x_last = swap_t((m_sent[0][mid:].astype(f32) + by_y.astype(f32)).astype(bf16), 1)
        y_first = swap_t((m_sent[1][:mid].astype(f32) + by_x.astype(f32)).astype(bf16), 2)
        m_step = [x_first, x_last, y_first, y_last]
    block_out = s1 + m_own + sum_received(m_step, nt)
    states = [expert_in, expert_in_first, expert_in_second, expert_down, expert_down_first, expert_down_second]
    experts_new = None
    for start, got in expert_grads[:-1]:
        got = after(got, grads_own)
        experts_new = adam_experts(place, start, got, swap_core(got[1]), states, experts_new)
    received, (experts_new, block_out) = to_owners(both, (experts_new, block_out))
    total = both[0].astype(f32) + received
    owned = total[0]
    sent = [total[j].astype(bf16) for j in range(1, nz)]
    received = [swap_z(part, j + 1) for j, part in enumerate(sent)]
    for start, got in expert_grads[-1:]:
        got = after(got, *sent, *experts_new)
        experts_new = adam_experts(place, start, got, swap_core(got[1]), states, experts_new)
    received, experts_new = lax.optimization_barrier((received, experts_new))
    states = [query_weight, query_first, query_second, keyval_weight, keyval_first, keyval_second]
    states += [output_weight, output_first, output_second, norm_gains, norm_gains_first, norm_gains_second]
    rest_new = adam_rest(place, 1.0 / sharers, owned, received, states[:9] + states[10:] + states[9:10])
    return (block_out, input_grad, *rest_new[9:], *rest_new[:9], *experts_new)


def solution(mesh):
    rows = P(("dp", "tensor"), None)
    by_rows = P(None, "dp", None)
    gains = P(None, None, ("dp", "tensor"))
    proj = P(None, "dp", "tensor")
    out_proj = P(None, "tensor", "dp")
    expert = P(None, "tensor", "dp", None)
    params = (gains,) * 3 + (proj,) * 6 + (out_proj,) * 3 + (expert,) * 6
    return jax.shard_map(
        functools.partial(on_device, mesh.shape["dp"], mesh.shape["tensor"]),
        mesh=mesh,
        in_specs=(rows, rows, by_rows, by_rows) + params,
        out_specs=(rows, rows) + params,
        check_vma=False,
    )
```

```python
import functools
import math

import jax
import jax.numpy as jnp
import numpy as np
from jax import lax
from jax.experimental import pallas as pl
from jax.experimental.pallas import tpu as pltpu
from jax.sharding import PartitionSpec as P

D = 1024
HD = 64
FFE = 512
SEQ_LEN = 512
STEP = 10
CALLS = (((0, 2),), ((2, 3), (3, 4)))
GATHERS = ((0, 3), (3, 4))
QBLK = 256
SUB = 256
CHUNK = 256
SLOTS = 2560
DEEP = 8
PAIR = 2
HELD = 3072

NORM_EPS = 1e-05
ROPE_BASE = 10000.0
BETA_ONE = 0.9
BETA_TWO = 0.95
ADAM_EPS = 1e-08
LEARN_RATE = 0.1
WEIGHT_DECAY = 0.1
MASK_FILL = -1e30
SCALE = 1.0 / math.sqrt(HD)

bf16 = jnp.bfloat16
f32 = jnp.float32
ANY = pl.BlockSpec(memory_space=pl.ANY)
COST = pl.CostEstimate(flops=1, bytes_accessed=1, transcendentals=0)
HBM = pl.BlockSpec(memory_space=pltpu.HBM)
SMEM = pl.BlockSpec(memory_space=pltpu.SMEM)
VMEM = pl.BlockSpec(memory_space=pltpu.VMEM)


def dot(a, b):
    return jnp.dot(a, b, preferred_element_type=f32)


def dot_t(a, b):
    return lax.dot_general(a, b, (((1,), (1,)), ((), ())), preferred_element_type=f32)


def t_dot(a, b):
    return lax.dot_general(a, b, (((0,), (0,)), ((), ())), preferred_element_type=f32)


def rope_tables():
    half = HD // 2
    position = np.arange(SEQ_LEN, dtype=np.float32)
    exponent = np.arange(half, dtype=np.float32) * np.float32(-2.0 / HD)
    frequency = np.exp(exponent * np.float32(math.log(ROPE_BASE))).astype(np.float32)
    angle = (position[:, None] * frequency[None, :]).astype(np.float32)
    cosine = np.cos(angle).astype(np.float32)
    sine = np.sin(angle).astype(np.float32)
    return np.tile(cosine, (1, 4)), np.concatenate([-sine, sine, -sine, sine], axis=1)


def adam_update(master, first_moment, second_moment, gradient, decay_rate):
    first_new = BETA_ONE * first_moment + (1.0 - BETA_ONE) * gradient
    second_new = BETA_TWO * second_moment + (1.0 - BETA_TWO) * gradient * gradient
    first_fixed = first_new / (1.0 - BETA_ONE**STEP)
    second_fixed = second_new / (1.0 - BETA_TWO**STEP)
    master_new = master - LEARN_RATE * (
        first_fixed / (jnp.sqrt(second_fixed) + ADAM_EPS) + decay_rate * master
    )
    return (master_new, first_new, second_new)


def adam_change(first_moment, second_moment, gradient):
    first_new = BETA_ONE * first_moment + (1.0 - BETA_ONE) * gradient
    second_new = BETA_TWO * second_moment + (1.0 - BETA_TWO) * gradient * gradient
    first_fixed = first_new / (1.0 - BETA_ONE**STEP)
    second_fixed = second_new / (1.0 - BETA_TWO**STEP)
    change = -LEARN_RATE * (first_fixed / (jnp.sqrt(second_fixed) + ADAM_EPS))
    return (change, first_new, second_new)


def sum_received(received, nt):
    received = [part.astype(f32) for part in received]
    if nt != 4:
        return functools.reduce(jnp.add, received)
    x_first, x_last, y_first, y_last = received
    return jnp.concatenate([x_first + y_first, x_last + y_last], axis=0)


def rms_scale(values):
    return lax.rsqrt(jnp.mean(values * values, axis=-1, keepdims=True) + NORM_EPS)


def weight_spots(place_ref, nz, nt, relative):
    rows, cols = D // (2 * nz), D // nt
    z, core, t = place_ref[0], place_ref[1], place_ref[2]
    for c in range(2):
        for k in range(nt):
            for j in range(nz):
                row = pl.multiple_of(((z ^ j if relative else j) * 2 + (core ^ c)) * rows, rows)
                col = pl.multiple_of((t ^ k) * cols, cols)
                yield c, k, j, (pl.ds(row, rows), pl.ds(col, cols))


def gather_copies(place_ref, pieces, first, w_ref, sem, nz, nt):
    rows = D // (2 * nz)
    return [
        pltpu.make_async_copy(
            pieces[c * nt + k].at[j, (first + member) * rows : (first + member + 1) * rows, :],
            w_ref.at[(member,) + spot],
            sem.at[((c * nt + k) * nz + j) * w_ref.shape[0] + member],
        )
        for c, k, j, spot in weight_spots(place_ref, nz, nt, False)
        for member in range(w_ref.shape[0])
    ]


def rotate(x, cosine, sine, first_half):
    width = x.shape[-1]
    swapped = jnp.where(
        first_half, pltpu.roll(x, width - HD // 2, 1), pltpu.roll(x, HD // 2, 1)
    )
    return x * cosine + swapped * sine


def join_gains(parts, width):
    owners = parts.shape[0]
    both = jnp.sum(parts[:, :, :128].astype(f32), axis=1)
    lane = lax.broadcasted_iota(jnp.int32, (owners, 128), 1)
    owner = lax.broadcasted_iota(jnp.int32, (owners, D), 0)
    mine = lax.broadcasted_iota(jnp.int32, (owners, D), 1) // width == owner
    out = []
    for values in (both, pltpu.roll(both, 128 - width, 1)):
        values = jnp.where(lane < width, values, 0.0)
        shift = width
        while shift < 128:
            values = values + pltpu.roll(values, shift, 1)
            shift *= 2
        wide = jnp.concatenate([values] * (D // 128), axis=1)
        out.append(jnp.sum(jnp.where(mine, wide, 0.0), axis=0, keepdims=True))
    return jnp.concatenate(out, axis=0)


def attend_forward_kernel(nz, nt, place_ref, tokens_ref, cos_ref, sin_ref, *rest):
    pieces = rest[: 2 * nt]
    q_ref, kv_ref, o_ref, lse_ref, w_ref, gains_ref = rest[2 * nt : 2 * nt + 6]
    qlin_ref, kvlin_ref, parts_ref, sems, gain_sems = rest[2 * nt + 6 :]
    length = tokens_ref.shape[0]
    rows = D // (2 * nz)
    core, t = place_ref[1], place_ref[2]
    gain_copies = [
        pltpu.make_async_copy(
            pieces[c * nt + k].at[j, 2 * rows :, :],
            parts_ref.at[(j * 2 + (core ^ c)) * nt + (t ^ k)],
            gain_sems.at[(c * nt + k) * nz + j],
        )
        for c in range(2)
        for k in range(nt)
        for j in range(nz)
    ]
    for copy in gain_copies:
        copy.start()
    copies = gather_copies(place_ref, pieces, 0, w_ref, sems, nz, nt)
    for copy in copies:
        copy.start()
    lse_ref[...] = jnp.zeros_like(lse_ref)
    for copy in gain_copies:
        copy.wait()
    gains_ref[...] = join_gains(parts_ref[...], D // (2 * nz * nt))
    stream = tokens_ref[...].astype(f32)
    n1 = (stream * rms_scale(stream) * gains_ref[0:1, :]).astype(bf16)
    for copy in copies:
        copy.wait()
    qlin_ref[...] = dot(n1, w_ref[0])
    kvlin_ref[...] = dot(n1, w_ref[1])

    def group(g, carry):
        part = pl.ds(pl.multiple_of(g * 128, 128), 128)
        lane = lax.broadcasted_iota(jnp.int32, (length, 128), 1)
        low = lane < HD
        first_half = (lane & (HD // 2)) == 0
        cosine, sine = cos_ref[...], sin_ref[...]
        q = rotate(qlin_ref[:, part], cosine, sine, first_half)
        kv = kvlin_ref[:, part]
        kv = jnp.where(low, rotate(kv, cosine, sine, first_half), kv)
        q_ref[:, part] = q.astype(bf16)
        kv_ref[:, part] = kv.astype(bf16)
        vk = pltpu.roll(kv, HD, 1).astype(bf16)
        kv = kv.astype(bf16)
        heads = (
            (jnp.where(low, q * SCALE, 0.0).astype(bf16), kv, vk),
            (jnp.where(low, 0.0, q * SCALE).astype(bf16), vk, kv),
        )
        row = lax.broadcasted_iota(jnp.int32, (QBLK, QBLK), 0)
        column = lax.broadcasted_iota(jnp.int32, (QBLK, QBLK), 1)
        seen = column <= row
        for b in range(length // QBLK):
            rows = slice(b * QBLK, (b + 1) * QBLK)
            keys = (b + 1) * QBLK
            outs = []
            lses = lse_ref[rows, :]
            lane_b = lax.broadcasted_iota(jnp.int32, (QBLK, 128), 1)
            for h, (qh, key_side, value_side) in enumerate(heads):
                scores = jnp.where(seen, dot_t(qh[rows], key_side[rows]), MASK_FILL)
                if b > 0:
                    scores = jnp.concatenate([dot_t(qh[rows], key_side[: b * QBLK]), scores], axis=1)
                top = jnp.max(scores, axis=-1, keepdims=True)
                e = jnp.exp(scores - top)
                total = jnp.sum(e, axis=-1, keepdims=True)
                outs.append(dot(e.astype(bf16), value_side[:keys]) * (1.0 / total))
                lses = jnp.where(lane_b == 2 * g + h, top + jnp.log(total), lses)
            lse_ref[rows, :] = lses
            o_ref[rows, part] = jnp.where(lane_b < HD, outs[0], outs[1]).astype(bf16)
        return carry

    lax.fori_loop(0, D // 128, group, 0)


def attend_forward(mesh_sizes, place, tokens, pieces):
    nz, nt = mesh_sizes
    length = tokens.shape[0]
    cosine, sine = rope_tables()
    return pl.pallas_call(
        functools.partial(attend_forward_kernel, nz, nt),
        out_shape=(
            jax.ShapeDtypeStruct((length, D), bf16),
            jax.ShapeDtypeStruct((length, D), bf16),
            jax.ShapeDtypeStruct((length, D), bf16),
            jax.ShapeDtypeStruct((length, 128), f32),
            jax.ShapeDtypeStruct((2, D, D), bf16),
            jax.ShapeDtypeStruct((2, D), f32),
        ),
        in_specs=[SMEM] + [VMEM] * 3 + [ANY] * len(pieces),
        out_specs=[VMEM] * 6,
        scratch_shapes=[
            pltpu.VMEM((length, D), f32),
            pltpu.VMEM((length, D), f32),
            pltpu.VMEM((2 * nz * nt, 16, D // nt), bf16),
            pltpu.SemaphoreType.DMA((2 * nt * nz * 2,)),
            pltpu.SemaphoreType.DMA((2 * nt * nz,)),
        ],
        compiler_params=pltpu.CompilerParams(vmem_limit_bytes=40 * 2**20),
        cost_estimate=pl.CostEstimate(flops=25 * 10**9, bytes_accessed=12 * 2**20, transcendentals=4 * 2**20),
        name="attend_forward",
    )(place, tokens, jnp.asarray(cosine), jnp.asarray(sine), *pieces)


def attend_out_kernel(nz, nt, place_ref, tokens_ref, gains_ref, o_ref, *rest):
    pieces = rest[: 2 * nt]
    s1_ref, n2_ref, w_ref, sems = rest[2 * nt :]
    copies = gather_copies(place_ref, pieces, 0, w_ref, sems, nz, nt)
    for copy in copies:
        copy.start()
    for copy in copies:
        copy.wait()
    s1 = tokens_ref[...].astype(f32) + dot_t(o_ref[...], w_ref[0])
    s1_ref[...] = s1
    n2_ref[...] = (s1 * rms_scale(s1) * gains_ref[1:2, :]).astype(bf16)


def attend_out(mesh_sizes, place, tokens, gains, o, pieces):
    nz, nt = mesh_sizes
    length = tokens.shape[0]
    return pl.pallas_call(
        functools.partial(attend_out_kernel, nz, nt),
        out_shape=(
            jax.ShapeDtypeStruct((length, D), f32),
            jax.ShapeDtypeStruct((length, D), bf16),
            jax.ShapeDtypeStruct((1, D, D), bf16),
        ),
        in_specs=[SMEM] + [VMEM] * 3 + [ANY] * len(pieces),
        out_specs=[VMEM] * 3,
        scratch_shapes=[pltpu.SemaphoreType.DMA((2 * nt * nz,))],
        compiler_params=pltpu.CompilerParams(vmem_limit_bytes=32 * 2**20),
        cost_estimate=COST,
        name="attend_out",
    )(place, tokens, gains, o, *pieces)


def norm_backward(grad, stream, gain, given):
    inverse = rms_scale(stream)
    unit = stream * inverse
    scaled = grad * gain
    through = inverse * (scaled - unit * jnp.mean(scaled * unit, axis=-1, keepdims=True))
    return given + through, jnp.sum(grad * unit, axis=0, keepdims=True)


def attend_backward_kernel(nz, nt, whole, place_ref, tokens_ref, gains_ref, cos_ref, sin_ref, q_ref, kv_ref, o_ref, *rest):
    lse_ref, w_ref, wo_ref, rest = rest[0], rest[1], rest[2], rest[3:]
    da_ref, gain_two_ref, rest = rest[0], rest[1], rest[2:]
    if whole:
        gs1_ref, rest = rest[0], rest[1:]
    out_ref, own_ref, others, rest = rest[0], rest[1], rest[2 : 2 + nt], rest[2 + nt :]
    gw_ref, gg_ref, do_ref, dq_ref, dkv_ref, lse_t_ref, sems = rest
    length = tokens_ref.shape[0]
    rows, cols = D // (2 * nz), D // nt
    sides = ([own_ref.at[k] for k in range(nt)], others)
    da, gain_two = da_ref[...], gain_two_ref[...]

    def member_copies(members):
        return [
            pltpu.make_async_copy(
                gw_ref.at[(member,) + spot],
                sides[c][k].at[j, member * rows : (member + 1) * rows, :],
                sems.at[member, (c * nt + k) * nz + j],
            )
            for member in members
            for c, k, j, spot in weight_spots(place_ref, nz, nt, True)
        ]

    gw_ref[2] = t_dot(da, o_ref[...]).astype(bf16)
    first = member_copies((2,))
    for copy in first:
        copy.start()
    do_ref[...] = dot(da, wo_ref[0]).astype(bf16)
    lse_t_ref[...] = lse_ref[...].T

    def group(g, carry):
        part = pl.ds(pl.multiple_of(g * 128, 128), 128)
        lane = lax.broadcasted_iota(jnp.int32, (length, 128), 1)
        low = lane < HD
        first_half = (lane & (HD // 2)) == 0
        cosine, sine = cos_ref[...], sin_ref[...]
        q = q_ref[:, part].astype(f32)
        kv = kv_ref[:, part].astype(f32)
        do = do_ref[:, part].astype(f32)
        vk = pltpu.roll(kv, HD, 1).astype(bf16)
        kv = kv.astype(bf16)
        q_low = jnp.where(low, q, 0.0).astype(bf16)
        scaled_low = jnp.where(low, q * SCALE, 0.0).astype(bf16)
        scaled_high = jnp.where(low, 0.0, q * SCALE).astype(bf16)
        q_moved = jnp.where(low, pltpu.roll(q, HD, 1), 0.0).astype(bf16)
        do_low = jnp.where(low, do, 0.0).astype(bf16)
        do_high = jnp.where(low, 0.0, do).astype(bf16)
        do_moved = jnp.where(low, 0.0, pltpu.roll(do, HD, 1)).astype(bf16)
        heads = (
            (scaled_low, kv, vk, do_low, q_low, do_moved),
            (scaled_high, vk, kv, do_high, q_moved, do_high),
        )
        row = lax.broadcasted_iota(jnp.int32, (QBLK, QBLK), 0)
        column = lax.broadcasted_iota(jnp.int32, (QBLK, QBLK), 1)
        seen = row <= column
        blocks = length // QBLK
        dkv = [jnp.zeros((QBLK, 128), f32) for _ in range(blocks)]
        dqs = []
        for b in range(blocks):
            rows = slice(b * QBLK, (b + 1) * QBLK)
            keys = (b + 1) * QBLK
            both = []
            for h, (qh, key_side, value_side, doh, q_for_k, do_for_v) in enumerate(heads):
                scores = jnp.where(seen, dot_t(key_side[rows], qh[rows]), MASK_FILL)
                if b > 0:
                    scores = jnp.concatenate([dot_t(key_side[: b * QBLK], qh[rows]), scores], axis=0)
                e = jnp.exp(scores - lse_t_ref[pl.ds(2 * g + h, 1), rows])
                dp = dot_t(value_side[:keys], doh[rows])
                mean = jnp.sum(e * dp, axis=0, keepdims=True)
                dz = (e * (dp - mean)).astype(bf16)
                both.append(t_dot(key_side[:keys], dz))
                add = dot(dz, q_for_k[rows]) + dot(e.astype(bf16), do_for_v[rows])
                for i in range(b + 1):
                    dkv[i] = dkv[i] + add[i * QBLK : (i + 1) * QBLK]
            dqs.append(jnp.concatenate([both[0][:HD], both[1][HD:]], axis=0))
        dq = jnp.concatenate(dqs, axis=1).T * SCALE
        dkv_all = jnp.concatenate(dkv, axis=0)
        dq_ref[:, part] = rotate(dq, cosine, -sine, first_half).astype(bf16)
        dk = rotate(dkv_all * SCALE, cosine, -sine, first_half)
        dkv_ref[:, part] = jnp.where(low, dk, dkv_all).astype(bf16)
        return carry

    lax.fori_loop(0, D // 128, group, 0)
    stream = tokens_ref[...].astype(f32)
    n1 = (stream * rms_scale(stream) * gains_ref[0:1, :]).astype(bf16)
    gw_ref[0] = t_dot(n1, dq_ref[...]).astype(bf16)
    gw_ref[1] = t_dot(n1, dkv_ref[...]).astype(bf16)
    second = member_copies((0, 1))
    for copy in second:
        copy.start()
    dn1 = dot_t(dq_ref[...], w_ref[0]) + dot_t(dkv_ref[...], w_ref[1])
    input_grad, gain_one = norm_backward(dn1, stream, gains_ref[0:1, :], gs1_ref[...] if whole else 0.0)
    out_ref[...] = input_grad if whole else dn1
    gg_ref[...] = jnp.zeros_like(gg_ref)
    for i in range(nt):
        gg_ref[i : i + 1, :] = gain_one[:, i * cols : (i + 1) * cols].astype(bf16)
        gg_ref[nt + i : nt + i + 1, :] = gain_two[:, i * cols : (i + 1) * cols].astype(bf16)
    third = [
        pltpu.make_async_copy(gg_ref, sides[c][k].at[j, 3 * rows :, :], sems.at[3, (c * nt + k) * nz + j])
        for c in range(2)
        for k in range(nt)
        for j in range(nz)
    ]
    for copy in third:
        copy.start()
    for copy in first + second + third:
        copy.wait()


def attend_backward(mesh_sizes, whole, place, tokens, gains, q, kv, o, lse, weights, out_weight, *given):
    nz, nt = mesh_sizes
    length = tokens.shape[0]
    cosine, sine = rope_tables()
    part = (nz, 3 * D // (2 * nz) + 16, D // nt)
    out = pl.pallas_call(
        functools.partial(attend_backward_kernel, nz, nt, whole),
        out_shape=[jax.ShapeDtypeStruct((length, D), f32), jax.ShapeDtypeStruct((nt,) + part, bf16)]
        + [jax.ShapeDtypeStruct(part, bf16)] * nt,
        in_specs=[SMEM] + [VMEM] * (10 + len(given)),
        out_specs=[VMEM] + [ANY] * (1 + nt),
        scratch_shapes=[
            pltpu.VMEM((3, D, D), bf16),
            pltpu.VMEM((16, D // nt), bf16),
            pltpu.VMEM((length, D), bf16),
            pltpu.VMEM((length, D), bf16),
            pltpu.VMEM((length, D), bf16),
            pltpu.VMEM((128, length), f32),
            pltpu.SemaphoreType.DMA((4, 2 * nt * nz)),
        ],
        compiler_params=pltpu.CompilerParams(vmem_limit_bytes=60 * 2**20),
        cost_estimate=COST,
        name="attend_backward",
    )(
        place, tokens, gains, jnp.asarray(cosine), jnp.asarray(sine), q, kv, o, lse, weights, out_weight, *given
    )
    return out[0], out[1], out[2:]


def gather_kernel(starts, experts, with_c, offs_ref, pos_ref, *rest):
    tiles = len(starts) - 1
    if with_c:
        c_ref, rest = rest[0], rest[1:]
    parts, rest = rest[:tiles], rest[tiles:]
    outs, rest = rest[: 1 + with_c], rest[1 + with_c :]
    held, (buf, in_sems, out_sems) = rest[: 1 + with_c], rest[1 + with_c :]
    subs = starts[-1] // SUB

    def block_copy(s):
        j = max(i for i in range(tiles) if starts[i] <= s * SUB)
        return pltpu.make_async_copy(
            parts[j].at[pl.ds(s * SUB - starts[j], SUB)], buf.at[s % DEEP], in_sems.at[s % DEEP]
        )

    def flush(e, chunk):
        spot = pl.ds(pl.multiple_of(chunk * CHUNK, CHUNK), CHUNK)
        return [
            pltpu.make_async_copy(slots.at[e, spot, :], out.at[e, spot, :], out_sems.at[i, e, chunk])
            for i, (slots, out) in enumerate(zip(held, outs))
        ]

    for s in range(DEEP - 1):
        block_copy(s).start()

    def block(s, carry):
        for ahead in range(DEEP - 1, subs):

            @pl.when(s + DEEP - 1 == ahead)
            def _():
                block_copy(ahead).start()

        slot = lax.rem(s, DEEP)
        begin = [offs_ref[e * (subs + 1) + s] for e in range(experts)]
        end = [offs_ref[e * (subs + 1) + s + 1] for e in range(experts)]
        most = functools.reduce(jnp.maximum, [end[e] - begin[e] for e in range(experts)])
        pltpu.make_async_copy(parts[0].at[pl.ds(0, SUB)], buf.at[slot], in_sems.at[slot]).wait()

        def fill(count):
            slots = lax.broadcasted_iota(jnp.int32, (count, SUB), 0).astype(f32)
            spots = [pl.ds(pl.multiple_of(begin[e], 16), count) for e in range(experts)]
            picks = []
            for e in range(experts):
                hit = slots == pos_ref[pl.ds(e * subs + s, 1), :]
                picks.append(jnp.where(hit, 1.0, 0.0).astype(bf16))
                if with_c:
                    c = jnp.sum(jnp.where(hit, c_ref[pl.ds(e * subs + s, 1), :], 0.0), axis=1, keepdims=True)
                    held[1][e, spots[e], :] = jnp.broadcast_to(c, (count, 128))
            rows = dot(jnp.concatenate(picks, axis=0), buf[slot]).astype(bf16)
            for e in range(experts):
                held[0][e, spots[e], :] = rows[e * count : (e + 1) * count]

        @pl.when(most <= SUB // 2)
        def _():
            fill(SUB // 2)

        @pl.when(most > SUB // 2)
        def _():
            fill(SUB)

        for e in range(experts):

            @pl.when(end[e] // CHUNK > begin[e] // CHUNK)
            def _():
                for copy in flush(e, begin[e] // CHUNK):
                    copy.start()

        return carry

    lax.fori_loop(0, subs, block, 0)
    for e in range(experts):
        total = offs_ref[e * (subs + 1) + subs]
        tail = pl.ds(pl.multiple_of(total, 16), CHUNK)
        for slots in held:
            slots[e, tail, :] = jnp.zeros((CHUNK, slots.shape[2]), slots.dtype)
        for copy in flush(e, total // CHUNK):
            copy.start()
    for e in range(experts):

        def drain(chunk, carry):
            for copy in flush(e, chunk):
                copy.wait()
            return carry

        lax.fori_loop(0, offs_ref[e * (subs + 1) + subs] // CHUNK + 1, drain, 0)


def gather(parts, offs, pos, c=None):
    starts = [0]
    for part in parts:
        starts.append(starts[-1] + part.shape[0])
    experts = pos.shape[0] * SUB // starts[-1]
    with_c = c is not None
    held = [((experts, SLOTS, D), bf16)] + [((experts, SLOTS, 128), f32)] * with_c
    return pl.pallas_call(
        functools.partial(gather_kernel, tuple(starts), experts, with_c),
        out_shape=[jax.ShapeDtypeStruct(*kind) for kind in held],
        in_specs=[SMEM, VMEM] + [VMEM] * with_c + [HBM] * len(parts),
        out_specs=[HBM] * len(held),
        scratch_shapes=[pltpu.VMEM(*kind) for kind in held]
        + [
            pltpu.VMEM((DEEP, SUB, D), bf16),
            pltpu.SemaphoreType.DMA((DEEP,)),
            pltpu.SemaphoreType.DMA((1 + with_c, experts, SLOTS // CHUNK)),
        ],
        compiler_params=pltpu.CompilerParams(vmem_limit_bytes=62 * 2**20),
        cost_estimate=COST,
        name="gather_rows",
    )(offs, pos, *([c] if with_c else []), *parts)


def experts_kernel(first, subs, sources, kept, place_ref, offs_ref, n2_ref, dm_ref, c_ref, *rest):
    arrays = 1 + sources[-1][0]
    weights, rest = rest[:arrays], rest[arrays + kept :]
    m_ref, d_ref, gw_ref = rest[:3]
    win_buf, wdown_buf, n2_in, dm_in, c_in, m_out, d_out, zeros, gin, gdown, w_sems, in_sems, out_sems = rest[3:]
    e = pl.program_id(0)
    nz, cores, _, wrows, _ = gw_ref.shape
    rin, rdown = D // (nz * cores), FFE // (nz * cores)
    core = place_ref[1]
    total = offs_ref[(first + e) * (subs + 1) + subs]
    chunks = jnp.maximum((total + CHUNK - 1) // CHUNK, 1)

    def weight_copies(index):
        i, place = sources[index]
        slot = index % 2
        expert = core * (weights[i].shape[1] // 2) + place
        return [
            pltpu.make_async_copy(weights[i].at[:, expert, spot, :], buf.at[slot], w_sems.at[j, slot])
            for j, (spot, buf) in enumerate(((slice(0, rin), win_buf), (slice(rin, wrows), wdown_buf)))
        ]

    def in_copies(e, k, slot):
        spot = pl.ds(pl.multiple_of(k * CHUNK, CHUNK), CHUNK)
        return [
            pltpu.make_async_copy(source.at[first + e, spot, :], target.at[slot], in_sems.at[i, slot])
            for i, (source, target) in enumerate(((n2_ref, n2_in), (dm_ref, dm_in), (c_ref, c_in)))
        ]

    def out_copies(k, slot):
        spot = pl.ds(pl.multiple_of(k * CHUNK, CHUNK), CHUNK)
        return (
            pltpu.make_async_copy(m_out.at[slot], m_ref.at[e, spot, :], out_sems.at[0, slot]),
            pltpu.make_async_copy(d_out.at[slot], d_ref.at[e, spot, :], out_sems.at[1, slot]),
        )

    @pl.when(e == 0)
    def _():
        for copy in in_copies(e, 0, 0) + weight_copies(0):
            copy.start()
        zeros[...] = jnp.zeros_like(zeros)

    for index in range(len(sources)):

        @pl.when(e == index)
        def _():
            for copy in weight_copies(index):
                copy.wait()
            if index + 1 < len(sources):
                for copy in weight_copies(index + 1):
                    copy.start()

    at = lax.rem(e, 2)

    def one_chunk(k, carry):
        slot = lax.rem(k, 2)
        for copy in in_copies(e, k, slot):
            copy.wait()

        @pl.when(k + 1 < chunks)
        def _():
            for copy in in_copies(e, k + 1, 1 - slot):
                copy.start()

        @pl.when(k >= 2)
        def _():
            for copy in out_copies(k - 2, slot):
                copy.wait()

        win = win_buf[at].reshape(D, D)
        wdown = wdown_buf[at].reshape(FFE, D)
        n2, dm, c = n2_in[slot], dm_in[slot], c_in[slot][:, 0:1]
        hidden = dot(n2, win)
        gate, up = hidden[:, :FFE], hidden[:, FFE:]
        sigma = jax.nn.sigmoid(gate)
        silu = gate * sigma
        active = (c * silu * up).astype(bf16)
        m_out[slot] = dot(active, wdown).astype(bf16)
        gdown[...] = jnp.where(k == 0, 0.0, gdown[...]) + dot(active.T, dm)
        da = c * dot_t(dm, wdown)
        dgate = da * up * (sigma + silu * (1.0 - sigma))
        dup = da * silu
        dh = jnp.concatenate([dgate.astype(bf16), dup.astype(bf16)], axis=1)
        gin[...] = jnp.where(k == 0, 0.0, gin[...]) + dot(n2.T, dh)
        d_out[slot] = dot_t(dh, win).astype(bf16)
        for copy in out_copies(k, slot):
            copy.start()
        return carry

    lax.fori_loop(0, chunks, one_chunk, 0)

    @pl.when(e + 1 < len(sources))
    def _():
        for copy in in_copies(e + 1, 0, 0):
            copy.start()

    spot = pl.ds(pl.multiple_of(chunks * CHUNK, CHUNK), CHUNK)
    ends = (
        pltpu.make_async_copy(zeros, m_ref.at[e, spot, :], out_sems.at[0, 2]),
        pltpu.make_async_copy(zeros, d_ref.at[e, spot, :], out_sems.at[1, 2]),
    )
    for copy in ends:
        copy.start()
    for j in range(nz):
        for side in range(2):
            owner = 2 * j + (core ^ side)
            at_in, at_down = pl.multiple_of(owner * rin, rin), pl.multiple_of(owner * rdown, rdown)
            gw_ref[j, side, 0, :rin, :] = gin[pl.ds(at_in, rin), :].astype(bf16)
            gw_ref[j, side, 0, rin:, :] = gdown[pl.ds(at_down, rdown), :].astype(bf16)
    for copy in ends:
        copy.wait()
    for back in (1, 2):

        @pl.when(chunks >= back)
        def _():
            for copy in out_copies(chunks - back, lax.rem(chunks - back, 2)):
                copy.wait()


def experts_step(place, slots, offs, first, weights, sources, before, spot, count):
    owners, _, wrows, _ = weights[0].shape
    nz, cores = owners // 2, 2
    experts = len(sources)
    rin, rdown = D // (nz * cores), FFE // (nz * cores)
    part = jax.ShapeDtypeStruct((experts, HELD, D), bf16)
    kept = [] if before is None else [before]
    subs = offs.shape[1] - 1
    return pl.pallas_call(
        functools.partial(experts_kernel, first, subs, sources, len(kept)),
        grid=(experts,),
        out_shape=(part, part, jax.ShapeDtypeStruct((nz, cores, count, wrows, D), bf16)),
        in_specs=[SMEM, SMEM] + [HBM] * (3 + len(weights) + len(kept)),
        out_specs=(HBM, HBM, pl.BlockSpec((nz, cores, 1, wrows, D), lambda e: (0, 0, spot + e, 0, 0))),
        scratch_shapes=[
            pltpu.VMEM((2, owners, rin, D), bf16),
            pltpu.VMEM((2, owners, rdown, D), bf16),
            pltpu.VMEM((2, CHUNK, D), bf16),
            pltpu.VMEM((2, CHUNK, D), bf16),
            pltpu.VMEM((2, CHUNK, 128), f32),
            pltpu.VMEM((2, CHUNK, D), bf16),
            pltpu.VMEM((2, CHUNK, D), bf16),
            pltpu.VMEM((CHUNK, D), bf16),
            pltpu.VMEM((D, D), f32),
            pltpu.VMEM((FFE, D), f32),
            pltpu.SemaphoreType.DMA((2, 2)),
            pltpu.SemaphoreType.DMA((3, 2)),
            pltpu.SemaphoreType.DMA((2, 3)),
        ],
        input_output_aliases={5 + len(weights): 2} if kept else {},
        compiler_params=pltpu.CompilerParams(
            vmem_limit_bytes=60 * 2**20, dimension_semantics=("arbitrary",)
        ),
        cost_estimate=COST,
        name="experts",
    )(place, offs.reshape(-1), *slots, *weights, *kept)


def scatter_kernel(halves, sources, experts, subs, offs_ref, pos_ref, *rest):
    arrays = 1 + sources[-1][1]
    parts, rest = rest[:arrays], rest[arrays:]
    outs, (slots, sems) = rest[: len(halves)], rest[len(halves) :]
    i, steps = pl.program_id(0), subs // (2 * PAIR)
    first = lax.rem(i * PAIR + halves[0] * (subs // 2), subs)

    half = subs // 2

    def each(low, high, act):
        for spot, (e, array, index) in enumerate(sources):

            def one(chunk, carry):
                rows = pl.ds(pl.multiple_of(chunk * CHUNK, CHUNK), CHUNK)
                act(pltpu.make_async_copy(parts[array].at[index, rows, :], slots.at[spot, rows, :], sems.at[spot, chunk]))
                return carry

            lax.fori_loop(*spans(e, low, high), one, 0)

    def spans(e, low, high):
        middle = offs_ref[e * (subs + 1) + half] // CHUNK
        last_low = (offs_ref[e * (subs + 1) + low] + CHUNK - 1) // CHUNK + 1
        begin = jnp.where(lax.rem(low, half) == 0, offs_ref[e * (subs + 1) + low] // CHUNK, last_low)
        end = (offs_ref[e * (subs + 1) + high] + CHUNK - 1) // CHUNK + 1
        if len(halves) == 2:
            early = jnp.asarray(low) < half
            begin = jnp.where(early, jnp.minimum(begin, middle), begin)
            end = jnp.where(early, jnp.minimum(end, middle), end)
        return begin, end

    @pl.when(i == 0)
    def _():
        for h in halves:
            each(h * half, (h + 1) * half, lambda copy: copy.start())

    each(first, first + PAIR, lambda copy: copy.wait())
    lane = lax.broadcasted_iota(jnp.int32, (SUB, SUB), 1).astype(f32)
    totals = []
    for p in range(PAIR):
        picks = [
            jnp.where(lane == pos_ref[p * SUB : (p + 1) * SUB, e : e + 1], 1.0, 0.0).astype(bf16) for e, _, _ in sources
        ]
        windows = [
            slots[spot, pl.ds(pl.multiple_of(offs_ref[e * (subs + 1) + first + p], 16), SUB), :]
            for spot, (e, _, _) in enumerate(sources)
        ]
        totals.append(dot(jnp.concatenate(picks, axis=1), jnp.concatenate(windows, axis=0)).astype(bf16))
    for j, out_ref in enumerate(outs):

        @pl.when(i // steps == j)
        def _():
            for p in range(PAIR):
                out_ref[p * SUB : (p + 1) * SUB, :] = totals[p]


def scatter(offs, pos_columns, parts, halves):
    tokens, experts = pos_columns.shape
    sources = [
        (first + index, i, index) for i, (part, first) in enumerate(parts) for index in range(part.shape[0])
    ]
    subs = tokens // SUB
    steps = subs // (2 * PAIR)
    shift = halves[0] * steps
    blocks = [
        pl.BlockSpec((PAIR * SUB, D), lambda i, j=j: (jnp.clip(i - j * steps, 0, steps - 1), 0))
        for j in range(len(halves))
    ]
    return pl.pallas_call(
        functools.partial(scatter_kernel, halves, sources, experts, subs),
        grid=(len(halves) * steps,),
        out_shape=[jax.ShapeDtypeStruct((tokens // 2, D), bf16)] * len(halves),
        in_specs=[SMEM, pl.BlockSpec((PAIR * SUB, experts), lambda i: (lax.rem(i + shift, 2 * steps), 0))]
        + [HBM] * len(parts),
        out_specs=blocks,
        scratch_shapes=[
            pltpu.VMEM((len(sources), HELD, D), bf16),
            pltpu.SemaphoreType.DMA((len(sources), HELD // CHUNK)),
        ],
        compiler_params=pltpu.CompilerParams(
            vmem_limit_bytes=60 * 2**20, dimension_semantics=("arbitrary",)
        ),
        cost_estimate=COST,
        name="scatter_rows",
    )(offs.reshape(-1), pos_columns, *[part for part, _ in parts])


def adam_kernel(per, place_ref, mine_ref, recv_ref, *rest):
    states, news = rest[:6], rest[-6:]
    here = pl.program_id(0) // per == place_ref[1]
    grad = jnp.where(here, mine_ref[0, 0], recv_ref[0]).astype(f32)
    rin = states[0].shape[2]
    for i, part in ((0, grad[:rin]), (3, grad[rin:])):
        masters = [ref[0, 0] for ref in states[i : i + 3]]
        for ref, new in zip(news[i : i + 3], adam_update(*masters, part, WEIGHT_DECAY)):
            ref[0, 0] = new


def adam_experts(place, a, mine, recv, states, before):
    experts, rin = states[0].shape[1:3]
    rdown = states[3].shape[2]
    per = recv.shape[0]
    half = experts // 2
    spec = [
        pl.BlockSpec((1, 1, r, D), lambda i, place: (0, i // per * half + a + i % per, 0, 0))
        for r in (rin, rdown)
    ]
    specs = [spec[0]] * 3 + [spec[1]] * 3
    kept = [] if before is None else list(before)
    return pl.pallas_call(
        functools.partial(adam_kernel, per),
        grid_spec=pltpu.PrefetchScalarGridSpec(
            num_scalar_prefetch=1,
            grid=(2 * per,),
            in_specs=[
                pl.BlockSpec((1, 1, rin + rdown, D), lambda i, place: (0, i % per, 0, 0)),
                pl.BlockSpec((1, rin + rdown, D), lambda i, place: (i % per, 0, 0)),
            ]
            + specs
            + [HBM] * len(kept),
            out_specs=specs,
        ),
        out_shape=[jax.ShapeDtypeStruct(state.shape, f32) for state in states],
        input_output_aliases={9 + i: i for i in range(len(kept))},
        compiler_params=pltpu.CompilerParams(
            vmem_limit_bytes=60 * 2**20, dimension_semantics=("arbitrary",)
        ),
        cost_estimate=COST,
        name="adam_experts",
    )(place, mine, recv, *states, *kept)


def adam_rest_kernel(scale, place_ref, mine_ref, *rest):
    count = len(rest) - 25
    received, states, news, (grad_ref,) = rest[:count], rest[count : count + 12], rest[count + 12 : count + 24], rest[-1:]
    total = mine_ref[...]
    for part in received:
        total = total + part[...].astype(f32)
    grad_ref[...] = total * scale
    rows, cols = states[0].shape[1:]
    width = states[9].shape[2]
    for i, turned in ((0, False), (1, False), (2, True)):
        part = grad_ref[i * rows : (i + 1) * rows, :]
        refs = slice(3 * i, 3 * i + 3)
        masters = [ref[0] for ref in states[refs]]
        for ref, new in zip(news[refs], adam_update(*masters, part.T if turned else part, WEIGHT_DECAY)):
            ref[0] = new
    start = place_ref[3] * width
    for i in range(2):
        row = grad_ref[pl.ds(3 * rows + i * (D // cols) + start // cols, 1), :]
        part = pltpu.roll(row, lax.rem(cols - lax.rem(start, cols), cols), 1)[:, :width]
        moments = [ref[0, i : i + 1, :] for ref in states[9:11]]
        for ref, new in zip(news[9:], adam_change(*moments, part)):
            ref[0, i : i + 1, :] = new


def adam_rest(place, scale, mine, received, states):
    return pl.pallas_call(
        functools.partial(adam_rest_kernel, scale),
        out_shape=[jax.ShapeDtypeStruct(state.shape, f32) for state in states],
        in_specs=[SMEM] + [VMEM] * (1 + len(received) + len(states)),
        out_specs=[VMEM] * len(states),
        scratch_shapes=[pltpu.VMEM(mine.shape, f32)],
        compiler_params=pltpu.CompilerParams(vmem_limit_bytes=32 * 2**20),
        cost_estimate=COST,
        name="adam_rest",
    )(place, mine, *received, *states)


def on_device(
    ndp,
    nt,
    tokens,
    cotangent,
    routes,
    gate_weights,
    norm_gains,
    norm_gains_first,
    norm_gains_second,
    query_weight,
    query_first,
    query_second,
    keyval_weight,
    keyval_first,
    keyval_second,
    output_weight,
    output_first,
    output_second,
    expert_in,
    expert_in_first,
    expert_in_second,
    expert_down,
    expert_down_first,
    expert_down_second,
):
    nz = ndp // 2
    place_dp = lax.axis_index("dp")
    t = lax.axis_index("tensor")
    z, core = place_dp // 2, place_dp % 2
    place = jnp.stack([z, core, t, place_dp * nt + t]).astype(jnp.int32)
    rows = tokens.shape[0]
    sharers = max(1, SEQ_LEN // rows)

    def swap_core(x):
        return lax.ppermute(x, "dp", [(i, i ^ 1) for i in range(ndp)])

    def swap_z(x, j):
        return lax.ppermute(x, "dp", [(i, i ^ (2 * j)) for i in range(ndp)])

    def swap_t(x, k):
        return lax.ppermute(x, "tensor", [(i, i ^ k) for i in range(nt)])

    def spread_t(x):
        return [x] + [swap_t(x, k) for k in range(1, nt)]

    def spread_z(x):
        return [x] + [swap_z(x, j) for j in range(1, nz)]

    def after(x, *others):
        return lax.optimization_barrier((x,) + others)[0]

    def near(x):
        return [swap_t(x, k) for k in range(1, nt)] if nt != 4 else [swap_t(x, 1), swap_t(x, 2)]

    def far(x, others):
        mid = x.shape[0] // 2
        return [] if nt != 4 else [swap_t(others[0][:mid], 2), swap_t(others[1][mid:], 1)]

    width = norm_gains.shape[2]
    wrows, wcols = query_weight.shape[1:]
    high = lax.reduce_precision(norm_gains[0], 8, 7)
    middle = lax.reduce_precision(norm_gains[0] - high, 8, 7)
    gain_rows = jnp.stack([high, middle, norm_gains[0] - high - middle]).astype(bf16).reshape(3, 2 * width)
    own = jnp.concatenate(
        [
            query_weight[0].astype(bf16),
            keyval_weight[0].astype(bf16),
            jnp.pad(gain_rows, ((0, 13), (0, wcols - 2 * width))),
            output_weight[0].T.astype(bf16),
        ],
        axis=0,
    )
    half = expert_in.shape[1] // 2
    groups = [[2 * i + c for i in range(nz)] for c in range(2)]

    def cut(quarters):
        return quarters[0] * half // 4, quarters[1] * half // 4

    def shard(a, b):
        low = [
            jnp.concatenate([w[0, a:b], w[0, half + a : half + b]]).astype(bf16) for w in (expert_in, expert_down)
        ]
        return jnp.concatenate(low, axis=1)

    spans = [cut(quarters) for quarters in GATHERS]
    spans = [(a, b) for a, b in spans if a < b]
    shards = [shard(*spans[0])]
    for a, b in spans[1:]:
        shards.append(shard(a, b))
    column = lax.all_gather(own, "dp", axis=0, tiled=False, axis_index_groups=groups)
    held = {}
    for (a, b), part in zip(spans, shards):
        whole = lax.all_gather(part, "dp", axis=0, tiled=False)
        held.update({i: (whole, i - a) for i in range(a, b)})
    dm_near = near(cotangent)
    pieces = spread_t(after(column[:, : 2 * wrows + 16], *dm_near))
    pieces_out = spread_t(after(column[:, 2 * wrows + 16 :], *pieces[1:]))
    dm_far = far(cotangent, list(lax.optimization_barrier((*dm_near, *pieces[1:])))[: len(dm_near)])
    pieces = pieces + [swap_core(piece) for piece in pieces]

    ids = t * 2 * half + jnp.arange(2 * half, dtype=jnp.int32)
    chosen = routes[0].T[None, :, :] == ids[:, None, None]
    c_all = jnp.sum(jnp.where(chosen, gate_weights[0].T[None, :, :], 0.0), axis=1)
    c_mine = lax.dynamic_slice_in_dim(c_all, core * half, half, 0)
    c_got = swap_core(lax.dynamic_slice_in_dim(c_all, (1 - core) * half, half, 0))
    c_both = jnp.stack([c_mine, c_got], axis=1).reshape(half, 2, nt, rows)
    c_both = jnp.take(c_both, jnp.arange(nt, dtype=jnp.int32) ^ t, axis=2)
    subs = 2 * nt * rows // SUB
    c_rows = c_both.reshape(half * subs, SUB)
    taken = c_rows != 0.0
    upto = lax.broadcasted_iota(jnp.int32, (SUB, SUB), 0) <= lax.broadcasted_iota(jnp.int32, (SUB, SUB), 1)
    rank = dot(taken.astype(bf16), upto.astype(bf16))
    pos = jnp.where(taken, rank - 1.0, -1.0)
    sizes = (rank[:, SUB - 1].astype(jnp.int32).reshape(half, subs) + 15) // 16 * 16
    offs = jnp.pad(jnp.cumsum(sizes, axis=1), ((0, 0), (1, 0)))
    pos_columns = pos.reshape(half, subs * SUB).T

    sequence = after(tokens, offs, pos, c_rows, pos_columns)
    if sharers > 1:
        seq_groups = [list(range(i, i + sharers)) for i in range(0, nt, sharers)]
        sequence = lax.all_gather(tokens, "tensor", axis=0, tiled=True, axis_index_groups=seq_groups)
    first_row = (t % sharers) * rows
    q, kv, o, lse, qkv_weights, gains = attend_forward((nz, nt), place, sequence, pieces)
    o, *pieces_out = lax.optimization_barrier((o, *pieces_out))
    pieces_out = pieces_out + [swap_core(piece) for piece in pieces_out]
    s1, n2, out_weight = attend_out((nz, nt), place, sequence, gains, o, pieces_out)
    if sharers > 1:
        s1 = lax.dynamic_slice_in_dim(s1, first_row, rows, 0)
        n2 = lax.dynamic_slice_in_dim(n2, first_row, rows, 0)

    n2_near = near(n2)
    n2_far = far(n2, n2_near)
    n2_own = [n2] + n2_near
    dm_own = [cotangent] + dm_near + dm_far
    dm_parts = dm_own + [swap_core(part) for part in dm_own]
    dm_slots, c_slots = gather(dm_parts, offs.reshape(-1), pos, c_rows)
    dm_slots, c_slots, *n2_far = lax.optimization_barrier((dm_slots, c_slots, *n2_far))
    n2_own = n2_own + n2_far
    n2_parts = n2_own + [swap_core(part) for part in n2_own]
    (n2_slots,) = gather(n2_parts, offs.reshape(-1), pos)
    slots = (n2_slots, dm_slots, c_slots)
    m_parts, d_parts, expert_grads = [], [], []
    for calls in CALLS:
        start, stop = cut((calls[0][0], calls[-1][1]))
        gw = None
        for quarters in calls:
            a, b = cut(quarters)
            if a == b:
                continue
            arrays, sources = [], []
            for i in range(a, b):
                array, index = held[i]
                if not arrays or arrays[-1] is not array:
                    arrays.append(array)
                sources.append((len(arrays) - 1, index))
            m_part, d_part, gw = experts_step(
                place, slots, offs, a, arrays, tuple(sources), gw, a - start, stop - start
            )
            m_parts.append((m_part, a))
            d_parts.append((d_part, a))
        grad = lax.psum_scatter(gw, "dp", scatter_dimension=0, tiled=False, axis_index_groups=groups)
        expert_grads.append((start, grad))

    def both_cores(own, other):
        both = [
            own[k * rows : (k + 1) * rows].astype(f32) + other[k * rows : (k + 1) * rows].astype(f32)
            for k in range(nt)
        ]
        return both[0], [part.astype(bf16) for part in both[1:]]

    def to_tokens(parts, last=()):
        if nt != 4:
            return [swap_t(parts[k], k) for k in range(1, nt)], parts[1:]
        mid = parts[3].shape[0] // 2
        by_x, by_y = swap_t(parts[3][:mid], 1), swap_t(parts[3][mid:], 2)
        x_first, y_last = swap_t(parts[1][:mid], 1), swap_t(parts[2][mid:], 2)
        by_x, by_y, *_ = lax.optimization_barrier((by_x, by_y, *last))
        x_part = (parts[1][mid:].astype(f32) + by_y.astype(f32)).astype(bf16)
        y_part = (parts[2][:mid].astype(f32) + by_x.astype(f32)).astype(bf16)
        return [x_first, swap_t(x_part, 1), swap_t(y_part, 2), y_last], (x_part, y_part)

    (d_other,) = scatter(offs, pos_columns, d_parts, (1,))
    (d_own,) = scatter(offs, pos_columns, d_parts, (0,))
    d_own, d_sent = both_cores(d_own, swap_core(d_other))
    def to_owners(parts, meanwhile):
        if nt != 4:
            return sum_received([swap_t(parts[k], k) for k in range(1, nt)], nt), meanwhile
        mid = parts[3].shape[0] // 2
        by_x = swap_t(jnp.concatenate([parts[3][:mid], parts[1][:mid]]), 1)
        by_y = swap_t(jnp.concatenate([parts[3][mid:], parts[2][mid:]]), 2)
        by_x, by_y, meanwhile = lax.optimization_barrier((by_x, by_y, meanwhile))
        x_last = swap_t((parts[1][mid:].astype(f32) + by_y[:mid].astype(f32)).astype(bf16), 1)
        y_first = swap_t((parts[2][:mid].astype(f32) + by_x[:mid].astype(f32)).astype(bf16), 2)
        return sum_received([by_x[mid:], x_last, y_first, by_y[mid:]], nt), meanwhile

    d_received, d_last = to_tokens([None] + d_sent)
    m_pos = after(pos_columns, *d_last)
    m_other, m_own = scatter(offs, m_pos, m_parts, (1, 0))
    m_other = jnp.concatenate([swap_core(m_other[k * rows : (k + 1) * rows]) for k in range(nt)])
    m_own, m_sent = both_cores(m_own, m_other)

    whole = sharers == 1
    gs1, gain_two = norm_backward(d_own + sum_received(d_received, nt), s1, gains[1:2], cotangent.astype(f32))
    da, *m_sent = lax.optimization_barrier((gs1.astype(bf16), *m_sent))
    if nt == 4:
        mid = rows // 2
        m_step = [swap_t(m_sent[2][:mid], 1), swap_t(m_sent[2][mid:], 2)]
        m_step += [swap_t(m_sent[0][:mid], 1), swap_t(m_sent[1][mid:], 2)]
    else:
        m_step = [swap_t(part, k + 1) for k, part in enumerate(m_sent)]
    if not whole:
        da = lax.all_gather(da, "tensor", axis=0, tiled=True, axis_index_groups=seq_groups)
    input_grad, grads_own, grads_other = attend_backward(
        (nz, nt), whole, place, sequence, gains, q, kv, o, lse, qkv_weights, out_weight,
        da, gain_two * sharers, *([gs1] if whole else []),
    )
    if not whole:
        dn1 = lax.dynamic_slice_in_dim(input_grad, first_row, rows, 0)
        input_grad, _ = norm_backward(dn1, tokens.astype(f32), gains[0], gs1)

    grads_other, m_step = lax.optimization_barrier((grads_other, m_step))
    swapped = [swap_core(part) for part in grads_other]
    both = [(grads_own[k].astype(f32) + swapped[k].astype(f32)).astype(bf16) for k in range(nt)]
    if nt == 4:
        by_x, by_y, x_first, y_last = m_step
        by_x, by_y, *_ = lax.optimization_barrier((by_x, by_y, grads_own))
        x_last = swap_t((m_sent[0][mid:].astype(f32) + by_y.astype(f32)).astype(bf16), 1)
        y_first = swap_t((m_sent[1][:mid].astype(f32) + by_x.astype(f32)).astype(bf16), 2)
        m_step = [x_first, x_last, y_first, y_last]
    block_out = s1 + m_own + sum_received(m_step, nt)
    states = [expert_in, expert_in_first, expert_in_second, expert_down, expert_down_first, expert_down_second]
    experts_new = None
    for start, got in expert_grads[:-1]:
        got = after(got, grads_own)
        experts_new = adam_experts(place, start, got, swap_core(got[1]), states, experts_new)
    received, (experts_new, block_out) = to_owners(both, (experts_new, block_out))
    total = both[0].astype(f32) + received
    owned = total[0]
    sent = [total[j].astype(bf16) for j in range(1, nz)]
    received = [swap_z(sent[j - 1], j) for j in range(nz - 1, 0, -1)]
    for start, got in expert_grads[-1:]:
        got = after(got, *sent, *experts_new)
        experts_new = adam_experts(place, start, got, swap_core(got[1]), states, experts_new)
    received, experts_new = lax.optimization_barrier((received, experts_new))
    states = [query_weight, query_first, query_second, keyval_weight, keyval_first, keyval_second]
    states += [output_weight, output_first, output_second, norm_gains, norm_gains_first, norm_gains_second]
    rest_new = adam_rest(place, 1.0 / sharers, owned, received, states[:9] + states[10:] + states[9:10])
    return (block_out, input_grad, *rest_new[9:], *rest_new[:9], *experts_new)


def solution(mesh):
    rows = P(("dp", "tensor"), None)
    by_rows = P(None, "dp", None)
    gains = P(None, None, ("dp", "tensor"))
    proj = P(None, "dp", "tensor")
    out_proj = P(None, "tensor", "dp")
    expert = P(None, "tensor", "dp", None)
    params = (gains,) * 3 + (proj,) * 6 + (out_proj,) * 3 + (expert,) * 6
    return jax.shard_map(
        functools.partial(on_device, mesh.shape["dp"], mesh.shape["tensor"]),
        mesh=mesh,
        in_specs=(rows, rows, by_rows, by_rows) + params,
        out_specs=(rows, rows) + params,
        check_vma=False,
    )
```
